32 devices in a mesh: groups: 2 (over x), expert: 16 (over z, y, core).
Axes of the slice: x: 2, y: 2, z: 4, core: 2. Of those that a mesh axis runs over, the one named last changes fastest.
Arguments:
- tokens: bfloat16 [512, 7168], P(('groups', 'expert')), parts along dimension 0, may hold values from -6 to 6
- scales: float32 [512, 56], P(('groups', 'expert')), parts along dimension 0, may hold values from 0.25 to 4
- routes: int32 [512, 2], P(('groups', 'expert')), parts along dimension 0, may hold values from 0 to 3, all different within a row; in each aligned block of 16 rows (0 to 15, 16 to 31, ...) at most 12 rows name the same one
- gate_codes: int32 [512, 2], P(('groups', 'expert')), parts along dimension 0, may hold values from 1 to 65535
- w_gate: bfloat16 [16, 7168, 256], P('expert'), may hold values from -0.0625 to 0.0625
- w_up: bfloat16 [16, 7168, 256], P('expert'), may hold values from -0.0625 to 0.0625
- w_down: bfloat16 [16, 256, 7168], P('expert'), may hold values from -0.1875 to 0.1875
Outputs:
- mixed: bfloat16 [512, 7168], P(('groups', 'expert')), parts along dimension 0
The draws below stay inside these ranges and needn't reach their ends.
There are 2 independent parts, one for each index of `groups`. The reference program is written for one: setup_inputs(seed, part) draws one part's arguments, and reference() takes and returns one part's arrays. A program takes and returns all parts, laid end to end along the dimension named above; an argument that names none is the same for every part. Nothing has to cross between parts.
Inputs may be any that keep to these rules, and one draw needn't show every extreme that they name: `routes`: each row names 2 different experts. In each aligned block of 16 rows (the rows of one device) no expert is named by more than 12 rows, a bound that some block reaches.
All inputs are finite; a program needn't handle non-finite values.
Results may differ from the reference program's by a relative error of at most 0.0079.
Values may be sent and summed in bfloat16 or wider, within the bound.
No kernel may reach another device: no remote copies, remote signals or barrier semaphores. Data moves between devices by JAX's collectives and lax.ppermute only.
A program may use at most 128 MiB of HBM per device.

```python
import math
import jax
import jax.numpy as jnp
import numpy as np
from jax import lax

D = 7168
FF = 1024
SHARDS = 4
FF_DEV = 256
TOK_DEV = 16
EXPERTS = 4
TOP = 2
CAP = 12
TOKENS = 256
N_EXPERT = 16


def place_ends(array, key, smallest, largest):
    spot = [jax.random.randint(jax.random.fold_in(key, axis), (), 0, length) for axis, length in enumerate(array.shape)]
    main_axis = array.shape.index(max(array.shape))
    next_to = spot[:main_axis] + [(spot[main_axis] + 1) % array.shape[main_axis]] + spot[main_axis + 1:]
    return array.at[tuple(spot)].set(smallest).at[tuple(next_to)].set(largest)


def block_levels(own_key, dims, pieces, low, top_value):
    gain, own = 1.0, jax.random.fold_in(own_key, 6)
    for axis_at, blocks in pieces:
        heights = jnp.exp(jax.random.uniform(jax.random.fold_in(own, axis_at), (blocks,), jnp.float32, low / len(pieces), top_value / len(pieces)))
        gain = gain * jnp.repeat(heights, dims[axis_at] // blocks).reshape([-1 if axis == axis_at else 1 for axis in range(len(dims))])
    return gain


def deal_out(key, own, number, rows, amount, top, bound, slope):
    sequence = jax.random.permutation(key, amount)
    heavy_load, ordinary = shares(amount, rows * top, bound, slope, True), shares(amount, rows * top, bound, slope, False)
    places = jnp.arange(amount)

    def named(lengths, rotation):
        used = int((lengths > 0).sum())
        fixed = max(1, used // 4)
        moved = fixed + (places - fixed + rotation * (used - fixed)) % max(1, amount - fixed)
        return jnp.zeros((amount,), jnp.int32).at[sequence[jnp.where(places < fixed, places, moved)]].set(jnp.asarray(lengths, jnp.int32))

    lengths = jnp.where(number % 4 == 0, named(heavy_load, number // 4), named(ordinary, number - number // 4 - 1))
    mixed = jax.random.permutation(jax.random.fold_in(own, 3), amount)
    source_of, receiver = mixed[0:amount // 2 * 2:2], mixed[1:amount // 2 * 2:2]
    slack = jnp.minimum(lengths[source_of] - 1, bound - lengths[receiver]) // 2
    slack = jnp.where((source_of == sequence[0]) | (receiver == sequence[0]) | (lengths[receiver] == 0), 0, jnp.maximum(slack, 0))
    moved = jax.random.randint(jax.random.fold_in(own, 4), (amount // 2,), 0, 1 << 20) % (slack + 1)
    lengths = lengths.at[source_of].add(-moved).at[receiver].add(moved)
    labels = jnp.searchsorted(jnp.cumsum(lengths), jnp.arange(rows * top), side="right").astype(jnp.int32)
    table = labels.reshape(top, rows).T
    table = table[jax.random.permutation(jax.random.fold_in(own, 1), rows)]
    rotation = jax.random.randint(jax.random.fold_in(own, 2), (rows, 1), 0, top)
    return jnp.take_along_axis(table, (jnp.arange(top)[None, :] + rotation) % top, axis=1)


def shares(count, total, bound, slope, full):
    loads = [(1 << 20) // math.isqrt(rank ** slope) + 1 for rank in range(1, count + 1)]
    largest = bound if full else min(bound, max(-(-total // count), total * loads[0] // sum(loads)))
    least = 1 if total - largest >= count - 1 else 0
    holding, spare = [largest] + [least] * (count - 1), total - largest - least * (count - 1)
    while spare > 0:
        free = [i for i in range(1, count) if holding[i] < largest] or [i for i in range(1, count) if holding[i] < bound]
        mass, left = sum([loads[i] for i in free]), spare
        for i in free:
            extra = min(bound - holding[i], max(1, left * loads[i] // mass), spare)
            holding[i] = holding[i] + extra
            spare = spare - extra
    return np.array(holding)


def centred(stream_key, shape, spread, limit, cuts=(), held_as=jnp.bfloat16):
    drawn = jax.random.normal(stream_key, shape, jnp.float32) * spread
    if len(cuts) > 0:
        drawn = block_levels(stream_key, shape, cuts, -0.22, 0.18) * drawn
    return jnp.clip(drawn, min=-limit, max=limit).astype(held_as)


def setup_inputs(seed: int = 0, part: int = 0) -> dict:
    splits = jax.random.split(jax.random.key(seed), 8)
    part_keys = jax.random.split(jax.random.fold_in(splits[7], part), 8)
    tokens = centred(part_keys[0], (TOKENS, D), 1.0, 6.0, ((0, 16),))
    scales = jnp.clip(jnp.exp(math.log(4.0) - 2.7725887 * jax.random.uniform(part_keys[1], (TOKENS, D // 128), jnp.float32) ** block_levels(part_keys[1], (TOKENS, D // 128), ((0, 16),), -0.2, 0.2)), 0.25, 4.0)
    routes_keys = jax.random.split(jax.random.fold_in(part_keys[2], 1), TOKENS // TOK_DEV)
    routes_turns = jax.random.permutation(jax.random.fold_in(part_keys[2], 3), TOKENS // TOK_DEV)
    routes = jax.vmap(lambda own, number: deal_out(jax.random.fold_in(part_keys[2], 2), own, number, TOK_DEV, EXPERTS, TOP, CAP, 2))(routes_keys, routes_turns).reshape((TOKENS, TOP))
    gate_codes = place_ends(jax.random.randint(part_keys[3], (TOKENS, TOP), 1, 65536), jax.random.fold_in(part_keys[3], 1), 1, 65535).astype(jnp.int32)
    w_gate = centred(splits[4], (N_EXPERT, D, FF_DEV), D ** -0.5, 0.0625, ((0, 16),))
    w_up = centred(splits[5], (N_EXPERT, D, FF_DEV), D ** -0.5, 0.0625, ((0, 16),))
    w_down = centred(splits[6], (N_EXPERT, FF_DEV, D), FF ** -0.5, 0.1875, ((0, 16),))
    return {"tokens": tokens, "scales": scales, "routes": routes, "gate_codes": gate_codes, "w_gate": w_gate, "w_up": w_up, "w_down": w_down}


def shard_rows(slot_rows, gate_w, up_w, down_w):
    gate_proj = jnp.dot(slot_rows, gate_w, preferred_element_type=jnp.float32)
    upward = jnp.dot(slot_rows, up_w, preferred_element_type=jnp.float32)
    hidden = (jax.nn.silu(gate_proj) * upward).astype(jnp.bfloat16)
    return jnp.dot(hidden, down_w, preferred_element_type=jnp.float32).astype(jnp.bfloat16)


def block_position(block):
    onehot = (block[:, None] == jnp.arange(EXPERTS, dtype=jnp.int32)[None, :]).astype(jnp.int32)
    return jnp.sum((jnp.cumsum(onehot, 0) - onehot) * onehot, axis=1).astype(jnp.int32)


def reference(tokens, scales, routes, gate_codes, w_gate, w_up, w_down):
    blocks = tokens.astype(jnp.float32).reshape(TOKENS, D // 128, 128) * scales[:, :, None]
    values = blocks.reshape(TOKENS, D).astype(jnp.bfloat16)
    count = TOKENS * TOP
    rows_per = TOK_DEV * TOP
    chosen = routes.reshape(-1).astype(jnp.int32)
    position = lax.map(block_position, chosen.reshape(-1, rows_per)).reshape(-1)
    source = jnp.arange(count, dtype=jnp.int32) // rows_per
    slots_per = N_EXPERT * CAP
    slot_index = chosen * slots_per + source * CAP + position
    table = jnp.full((EXPERTS * slots_per,), count, jnp.int32).at[slot_index].set(jnp.arange(count, dtype=jnp.int32))
    weights = gate_codes.astype(jnp.float32).reshape(-1) / 65536.0

    def step(summed, index):
        entry = lax.dynamic_slice_in_dim(table, (index * slots_per).astype(jnp.int32), slots_per)
        slot_rows = jnp.take(values, entry // TOP, axis=0, mode="fill", fill_value=0)
        accum = jnp.zeros((slots_per, D), jnp.float32)
        for shard_index in range(SHARDS):
            row_index = (index * SHARDS + shard_index).astype(jnp.int32)
            part = shard_rows(slot_rows, w_gate[row_index], w_up[row_index], w_down[row_index])
            accum = accum + part.astype(jnp.float32)
        answer = accum.astype(jnp.bfloat16)
        scale_rows = jnp.take(weights, entry, axis=0, mode="fill", fill_value=0)
        term = answer.astype(jnp.float32) * scale_rows[:, None]
        return summed.at[entry // TOP].add(term, mode="drop"), None

    summed, unused = lax.scan(step, jnp.zeros((TOKENS, D), jnp.float32), jnp.arange(EXPERTS, dtype=jnp.int32))
    return summed.astype(jnp.bfloat16)
```

```python
import jax
import jax.numpy as jnp
from jax import lax
from jax.sharding import PartitionSpec as P

SHARDS = 4


def dequantize(codes, factors):
    shape = codes.shape
    blocks = (
        codes.astype(jnp.float32).reshape(shape[:-1] + (shape[-1] // 128, 128)) * factors[..., None]
    )
    return blocks.reshape(shape).astype(jnp.bfloat16)


def shards(tokens, scales, routes, gate_codes, w_gate, w_up, w_down):
    devices = lax.axis_size("expert")
    experts = devices // SHARDS
    values = dequantize(tokens, scales)
    weights = gate_codes.astype(jnp.float32) / 65536.0
    named = routes[:, :, None] == jnp.arange(experts, dtype=jnp.int32)[None, None, :]
    table = jnp.sum(jnp.where(named, weights[:, :, None], 0.0), axis=1)
    all_values = lax.all_gather(values, "expert", axis=0, tiled=True)
    all_table = lax.all_gather(table, "expert", axis=0, tiled=True)
    mine = lax.axis_index("expert") // SHARDS
    row_weight = lax.dynamic_slice_in_dim(all_table, mine, 1, axis=1)
    gate_proj = jnp.dot(all_values, w_gate[0], preferred_element_type=jnp.float32)
    upward = jnp.dot(all_values, w_up[0], preferred_element_type=jnp.float32)
    hidden = (jax.nn.silu(gate_proj) * upward).astype(jnp.bfloat16)
    part = jnp.dot(hidden, w_down[0], preferred_element_type=jnp.float32) * row_weight
    return lax.psum_scatter(part.astype(jnp.bfloat16), "expert", scatter_dimension=0, tiled=True)


def solution(mesh):
    in_specs = (
        P(("groups", "expert"), None),
        P(("groups", "expert"), None),
        P(("groups", "expert"), None),
        P(("groups", "expert"), None),
        P("expert", None, None),
        P("expert", None, None),
        P("expert", None, None),
    )
    out_specs = P(("groups", "expert"), None)
    return jax.shard_map(shards, mesh=mesh, in_specs=in_specs, out_specs=out_specs, check_vma=False)
```

```python
import functools

import jax
import jax.numpy as jnp
from jax import lax
from jax.experimental import pallas as pl
from jax.experimental.pallas import tpu as pltpu
from jax.sharding import PartitionSpec as P

SHARDS = 4
QUARTERS = 4
VMEM_BYTES = 48 * 1024 * 1024


def zero_one(condition):
    return jnp.where(condition, 1.0, 0.0).astype(jnp.bfloat16)


def exact_dot(left, right):
    return jnp.dot(left, right, preferred_element_type=jnp.float32)


def pack_kernel(capacity, planes, tok_ref, scale_ref, route_ref, *rest):
    outs, quarters_ref = rest[:planes], rest[planes]
    rows, features = tok_ref.shape
    width = features // QUARTERS
    for block in range(features // 128):
        quarter, at = divmod(block * 128, width)
        codes = tok_ref[:, block * 128 : (block + 1) * 128].astype(jnp.float32)
        factors = scale_ref[:, block : block + 1]
        quarters_ref[quarter * rows : (quarter + 1) * rows, at : at + 128] = (
            codes * factors
        ).astype(jnp.bfloat16)
    plane = lax.axis_index("expert") // SHARDS
    offsets = (route_ref[...] ^ plane).astype(jnp.float32).astype(jnp.bfloat16)
    columns = QUARTERS * rows
    picks = offsets.shape[1]
    copies = zero_one(
        lax.broadcasted_iota(jnp.int32, (rows, columns), 1) % rows
        == lax.broadcasted_iota(jnp.int32, (rows, columns), 0)
    )
    turned = lax.dot_general(
        offsets, copies, (((0,), (0,)), ((), ())), preferred_element_type=jnp.float32
    )
    numbers = lax.broadcasted_iota(jnp.int32, (planes, columns), 0).astype(jnp.float32)
    named = jnp.zeros((planes, columns), jnp.float32)
    for pick in range(picks):
        named = named + jnp.where(turned[pick : pick + 1, :] == numbers, 1.0, 0.0)
    first = lax.broadcasted_iota(jnp.int32, (columns, columns), 0)
    second = lax.broadcasted_iota(jnp.int32, (columns, columns), 1)
    before = zero_one((first // rows == second // rows) & (first < second))
    position = exact_dot(named.astype(jnp.bfloat16), before)
    slot_row = lax.broadcasted_iota(jnp.int32, (QUARTERS * capacity, columns), 0)
    slot_col = lax.broadcasted_iota(jnp.int32, (QUARTERS * capacity, columns), 1)
    same_quarter = slot_row // capacity == slot_col // rows
    slot = (slot_row % capacity).astype(jnp.float32)
    values = quarters_ref[...]
    for offset in range(planes):
        pick_out = zero_one(
            same_quarter
            & (named[offset : offset + 1, :] > 0.5)
            & (position[offset : offset + 1, :] == slot)
        )
        outs[offset][...] = exact_dot(pick_out, values).astype(jnp.bfloat16)


def order_matrix(capacity, turned):
    size = SHARDS * QUARTERS * capacity
    row = lax.broadcasted_iota(jnp.int32, (size, size), 1 if turned else 0)
    col = lax.broadcasted_iota(jnp.int32, (size, size), 0 if turned else 1)
    quarter, block, slot = row // (SHARDS * capacity), (row // capacity) % SHARDS, row % capacity
    return zero_one(col == (block * QUARTERS + quarter) * capacity + slot)


def expert_kernel(capacity, planes, *refs):
    blocks = refs[: planes * SHARDS]
    gate_ref, up_ref, down_ref = refs[planes * SHARDS : planes * SHARDS + 3]
    outs = refs[planes * SHARDS + 3 : planes * SHARDS + 3 + 2 * planes]
    rows_ref, part_ref = refs[planes * SHARDS + 3 + 2 * planes :]
    group = SHARDS * capacity
    width = blocks[0].shape[1]
    order = order_matrix(capacity, False)
    for offset in range(planes):
        held = jnp.concatenate(
            [blocks[offset * SHARDS + member][...] for member in range(SHARDS)], axis=0
        )
        sorted_rows = exact_dot(order, held).astype(jnp.bfloat16)
        for quarter in range(QUARTERS):
            rows_ref[quarter, offset * group : (offset + 1) * group, :] = sorted_rows[
                quarter * group : (quarter + 1) * group, :
            ]
    gate = jnp.zeros((planes * group, gate_ref.shape[2]), jnp.float32)
    upward = jnp.zeros((planes * group, gate_ref.shape[2]), jnp.float32)
    for quarter in range(QUARTERS):
        span = slice(quarter * width, (quarter + 1) * width)
        gate = gate + exact_dot(rows_ref[quarter], gate_ref[0, span, :])
        upward = upward + exact_dot(rows_ref[quarter], up_ref[0, span, :])
    hidden = (gate / (1.0 + jnp.exp(-gate)) * upward).astype(jnp.bfloat16)
    for quarter in range(QUARTERS):
        span = slice(quarter * width, (quarter + 1) * width)
        part_ref[quarter] = exact_dot(hidden, down_ref[0, :, span]).astype(jnp.bfloat16)
    back = order_matrix(capacity, True)
    half = QUARTERS * SHARDS * capacity // 2
    for offset in range(planes):
        held = jnp.concatenate(
            [
                part_ref[quarter, offset * group : (offset + 1) * group, :]
                for quarter in range(QUARTERS)
            ],
            axis=0,
        )
        answer = exact_dot(back, held).astype(jnp.bfloat16)
        outs[2 * offset][...] = answer[:half]
        outs[2 * offset + 1][...] = answer[half:]


def mix_kernel(capacity, planes, route_ref, code_ref, *refs):
    returned, out_ref = refs[:planes], refs[planes]
    rows, picks = route_ref.shape
    width = returned[0].shape[1]
    tall = QUARTERS * rows
    plane = lax.axis_index("expert") // SHARDS
    offsets = (route_ref[...] ^ plane).astype(jnp.float32).astype(jnp.bfloat16)
    copies = zero_one(
        lax.broadcasted_iota(jnp.int32, (tall, rows), 0) % rows
        == lax.broadcasted_iota(jnp.int32, (tall, rows), 1)
    )
    offsets = exact_dot(copies, offsets)
    weights = code_ref[...].astype(jnp.float32) / 65536.0
    weights = jnp.concatenate([weights] * QUARTERS, axis=0)
    numbers = lax.broadcasted_iota(jnp.int32, (tall, planes), 1).astype(jnp.float32)
    named = jnp.zeros((tall, planes), jnp.float32)
    factors = jnp.zeros((tall, planes), jnp.float32)
    for pick in range(picks):
        here = offsets[:, pick : pick + 1] == numbers
        named = named + jnp.where(here, 1.0, 0.0)
        factors = factors + jnp.where(here, weights[:, pick : pick + 1], 0.0)
    first = lax.broadcasted_iota(jnp.int32, (tall, tall), 0)
    second = lax.broadcasted_iota(jnp.int32, (tall, tall), 1)
    before = zero_one((first // rows == second // rows) & (second < first))
    position = exact_dot(before, named.astype(jnp.bfloat16))
    slot_row = lax.broadcasted_iota(jnp.int32, (tall, QUARTERS * capacity), 0)
    slot_col = lax.broadcasted_iota(jnp.int32, (tall, QUARTERS * capacity), 1)
    same_quarter = slot_row // rows == slot_col // capacity
    slot = (slot_col % capacity).astype(jnp.float32)
    total = jnp.zeros((tall, width), jnp.float32)
    for offset in range(planes):
        take = zero_one(
            same_quarter
            & (named[:, offset : offset + 1] > 0.5)
            & (position[:, offset : offset + 1] == slot)
        )
        total = total + factors[:, offset : offset + 1] * exact_dot(take, returned[offset][...])
    total = total.astype(jnp.bfloat16)
    for quarter in range(QUARTERS):
        out_ref[:, quarter * width : (quarter + 1) * width] = total[
            quarter * rows : (quarter + 1) * rows, :
        ]


def shards(tokens, scales, routes, gate_codes, w_gate, w_up, w_down):
    tok_rows, features = tokens.shape
    picks_per = routes.shape[1]
    devices = lax.axis_size("expert")
    planes = devices // SHARDS
    capacity = 3 * tok_rows * picks_per // (2 * planes)
    width = features // QUARTERS
    tall = QUARTERS * capacity
    vmem = pl.BlockSpec(memory_space=pltpu.VMEM)
    params = pltpu.CompilerParams(vmem_limit_bytes=VMEM_BYTES)

    def partner(array, distance):
        return lax.ppermute(array, "expert", [(i, i ^ distance) for i in range(devices)])

    block = jax.ShapeDtypeStruct((tall, width), jnp.bfloat16)
    packed = pl.pallas_call(
        functools.partial(pack_kernel, capacity, planes),
        out_shape=[block] * planes,
        in_specs=[vmem] * 3,
        out_specs=[vmem] * planes,
        scratch_shapes=[pltpu.VMEM((QUARTERS * tok_rows, width), jnp.bfloat16)],
        compiler_params=params,
    )(tokens, scales, routes)

    gathered = []
    for offset in range(planes):
        own = packed[0] if offset == 0 else partner(packed[offset], offset * SHARDS)
        across = partner(own, 2)
        gathered += [own, across, partner(own, 1), partner(across, 1)]

    pair = jax.ShapeDtypeStruct((2 * tall, width), jnp.bfloat16)
    parts = pl.pallas_call(
        functools.partial(expert_kernel, capacity, planes),
        out_shape=[pair] * (2 * planes),
        in_specs=[vmem] * (planes * SHARDS + 3),
        out_specs=[vmem] * (2 * planes),
        scratch_shapes=[
            pltpu.VMEM((QUARTERS, planes * SHARDS * capacity, width), jnp.bfloat16),
            pltpu.VMEM((QUARTERS, planes * SHARDS * capacity, width), jnp.bfloat16),
        ],
        compiler_params=params,
    )(*gathered, w_gate, w_up, w_down)

    returned = []
    for offset in range(planes):
        kept, arrived = parts[2 * offset], partner(parts[2 * offset + 1], 1)
        kept, arrived = kept.astype(jnp.float32), arrived.astype(jnp.float32)
        across = partner((kept[tall:] + arrived[tall:]).astype(jnp.bfloat16), 2)
        answer = (kept[:tall] + arrived[:tall] + across.astype(jnp.float32)).astype(jnp.bfloat16)
        returned.append(answer if offset == 0 else partner(answer, offset * SHARDS))

    return pl.pallas_call(
        functools.partial(mix_kernel, capacity, planes),
        out_shape=jax.ShapeDtypeStruct((tok_rows, features), jnp.bfloat16),
        in_specs=[vmem] * (planes + 2),
        out_specs=vmem,
        compiler_params=params,
    )(routes, gate_codes, *returned)


def solution(mesh):
    in_specs = (
        P(("groups", "expert"), None),
        P(("groups", "expert"), None),
        P(("groups", "expert"), None),
        P(("groups", "expert"), None),
        P("expert", None, None),
        P("expert", None, None),
        P("expert", None, None),
    )
    out_specs = P(("groups", "expert"), None)
    return jax.shard_map(shards, mesh=mesh, in_specs=in_specs, out_specs=out_specs, check_vma=False)
```

```python
import functools

import jax
import jax.numpy as jnp
from jax import lax
from jax.experimental import pallas as pl
from jax.experimental.pallas import tpu as pltpu
from jax.sharding import PartitionSpec as P

SHARDS = 4
QUARTERS = 4
VMEM_BYTES = 16 * 1024 * 1024
PACK_VMEM_BYTES = 48 * 1024 * 1024
LOAD_VMEM_BYTES = 40 * 1024 * 1024


def zero_one(condition):
    return jnp.where(condition, 1.0, 0.0).astype(jnp.bfloat16)


def exact_dot(left, right):
    return jnp.dot(left, right, preferred_element_type=jnp.float32)


def pack_kernel(capacity, planes, tok_hbm, scale_hbm, route_ref, *rest):
    outs = rest[:planes]
    quarters_ref, tok_ref, scale_ref, tok_sem, scale_sem = rest[planes:]
    tok_copy = pltpu.make_async_copy(tok_hbm, tok_ref, tok_sem)
    scale_copy = pltpu.make_async_copy(scale_hbm, scale_ref, scale_sem)
    tok_copy.start()
    scale_copy.start()
    rows, features = tok_ref.shape
    width = features // QUARTERS
    plane = lax.axis_index("expert") // SHARDS
    offsets = (route_ref[...] ^ plane).astype(jnp.float32).astype(jnp.bfloat16)
    columns = QUARTERS * rows
    picks = offsets.shape[0]
    copies = zero_one(
        lax.broadcasted_iota(jnp.int32, (rows, columns), 1) % rows
        == lax.broadcasted_iota(jnp.int32, (rows, columns), 0)
    )
    turned = exact_dot(offsets, copies)
    numbers = lax.broadcasted_iota(jnp.int32, (planes, columns), 0).astype(jnp.float32)
    named = jnp.zeros((planes, columns), jnp.float32)
    for pick in range(picks):
        named = named + jnp.where(turned[pick : pick + 1, :] == numbers, 1.0, 0.0)
    first = lax.broadcasted_iota(jnp.int32, (columns, columns), 0)
    second = lax.broadcasted_iota(jnp.int32, (columns, columns), 1)
    before = zero_one((first // rows == second // rows) & (first < second))
    position = exact_dot(named.astype(jnp.bfloat16), before)
    slot_row = lax.broadcasted_iota(jnp.int32, (QUARTERS * capacity, columns), 0)
    slot_col = lax.broadcasted_iota(jnp.int32, (QUARTERS * capacity, columns), 1)
    same_quarter = slot_row // capacity == slot_col // rows
    slot = (slot_row % capacity).astype(jnp.float32)
    tok_copy.wait()
    scale_copy.wait()
    for block in range(features // 128):
        quarter, at = divmod(block * 128, width)
        codes = tok_ref[:, block * 128 : (block + 1) * 128].astype(jnp.float32)
        factors = scale_ref[:, block : block + 1]
        quarters_ref[quarter * rows : (quarter + 1) * rows, at : at + 128] = (
            codes * factors
        ).astype(jnp.bfloat16)
    values = quarters_ref[...]
    for offset in range(planes):
        pick_out = zero_one(
            same_quarter
            & (named[offset : offset + 1, :] > 0.5)
            & (position[offset : offset + 1, :] == slot)
        )
        outs[offset][...] = exact_dot(pick_out, values).astype(jnp.bfloat16)


def order_matrix(capacity, turned):
    size = SHARDS * QUARTERS * capacity
    row = lax.broadcasted_iota(jnp.int32, (size, size), 1 if turned else 0)
    col = lax.broadcasted_iota(jnp.int32, (size, size), 0 if turned else 1)
    quarter, block, slot = row // (SHARDS * capacity), (row // capacity) % SHARDS, row % capacity
    return zero_one(col == (block * QUARTERS + quarter) * capacity + slot)


def expert_kernel(capacity, offsets, load, *refs):
    count = offsets * SHARDS
    blocks = refs[:count]
    group, tall = SHARDS * capacity, QUARTERS * capacity
    width = blocks[0].shape[1]
    spans = [slice(quarter * width, (quarter + 1) * width) for quarter in range(QUARTERS)]
    waits = []
    if load:
        given = refs[count : count + 3]
        kept_ref, sent_ref, gate_ref, up_ref, down_ref, rows_ref, part_ref, sems = refs[count + 3 :]
        for span in spans:
            for part in (0, 1):
                here = (slice(None), span, slice(None))
                waits.append((given[part].at[here], (gate_ref, up_ref)[part].at[here]))
        for span in spans:
            here = (slice(None), slice(None), span)
            waits.append((given[2].at[here], down_ref.at[here]))
        waits = [
            pltpu.make_async_copy(source, target, sems.at[index])
            for index, (source, target) in enumerate(waits)
        ]
        for copy in waits:
            copy.start()
    else:
        gate_ref, up_ref, down_ref, unused, kept_ref, sent_ref, rows_ref, part_ref = refs[count:]
    order = order_matrix(capacity, False)
    for offset in range(offsets):
        held = jnp.concatenate(
            [blocks[offset * SHARDS + member][...] for member in range(SHARDS)], axis=0
        )
        sorted_rows = exact_dot(order, held).astype(jnp.bfloat16)
        for quarter in range(QUARTERS):
            rows_ref[quarter, offset * group : (offset + 1) * group, :] = sorted_rows[
                quarter * group : (quarter + 1) * group, :
            ]
    gate = jnp.zeros((offsets * group, gate_ref.shape[2]), jnp.float32)
    upward = jnp.zeros((offsets * group, gate_ref.shape[2]), jnp.float32)
    for quarter, span in enumerate(spans):
        if load:
            waits[2 * quarter].wait()
            waits[2 * quarter + 1].wait()
        gate = gate + exact_dot(rows_ref[quarter], gate_ref[0, span, :])
        upward = upward + exact_dot(rows_ref[quarter], up_ref[0, span, :])
    hidden = (gate / (1.0 + jnp.exp(-gate)) * upward).astype(jnp.bfloat16)
    for quarter, span in enumerate(spans):
        if load:
            waits[2 * QUARTERS + quarter].wait()
        part_ref[quarter] = exact_dot(hidden, down_ref[0, :, span]).astype(jnp.bfloat16)
    back = order_matrix(capacity, True)
    for offset in range(offsets):
        held = jnp.concatenate(
            [
                part_ref[quarter, offset * group : (offset + 1) * group, :]
                for quarter in range(QUARTERS)
            ],
            axis=0,
        )
        answer = exact_dot(back, held).astype(jnp.bfloat16)
        for member in range(SHARDS):
            out_ref = sent_ref if member >= 2 else kept_ref
            at = (member % 2 * offsets + offset) * tall
            out_ref[at : at + tall, :] = answer[member * tall : (member + 1) * tall, :]


def mix_kernel(capacity, planes, route_ref, code_ref, *refs):
    returned, out_ref = refs[:planes], refs[planes]
    picks, rows = route_ref.shape
    width = out_ref.shape[1] // QUARTERS
    tall = QUARTERS * rows
    plane = lax.axis_index("expert") // SHARDS
    copies = zero_one(
        lax.broadcasted_iota(jnp.int32, (tall, rows), 0) % rows
        == lax.broadcasted_iota(jnp.int32, (tall, rows), 1)
    )

    def turned(numbers):
        numbers = numbers.astype(jnp.float32).astype(jnp.bfloat16)
        return lax.dot_general(
            copies, numbers, (((1,), (1,)), ((), ())), preferred_element_type=jnp.float32
        )

    offsets = turned(route_ref[...] ^ plane)
    codes = code_ref[...]
    weights = (turned(codes // 256) * 256.0 + turned(codes % 256)) / 65536.0
    numbers = lax.broadcasted_iota(jnp.int32, (tall, planes), 1).astype(jnp.float32)
    named = jnp.zeros((tall, planes), jnp.float32)
    factors = jnp.zeros((tall, planes), jnp.float32)
    for pick in range(picks):
        here = offsets[:, pick : pick + 1] == numbers
        named = named + jnp.where(here, 1.0, 0.0)
        factors = factors + jnp.where(here, weights[:, pick : pick + 1], 0.0)
    first = lax.broadcasted_iota(jnp.int32, (tall, tall), 0)
    second = lax.broadcasted_iota(jnp.int32, (tall, tall), 1)
    before = zero_one((first // rows == second // rows) & (second < first))
    position = exact_dot(before, named.astype(jnp.bfloat16))
    slot_row = lax.broadcasted_iota(jnp.int32, (tall, QUARTERS * capacity), 0)
    slot_col = lax.broadcasted_iota(jnp.int32, (tall, QUARTERS * capacity), 1)
    same_quarter = slot_row // rows == slot_col // capacity
    slot = (slot_col % capacity).astype(jnp.float32)
    total = jnp.zeros((tall, width), jnp.float32)
    for offset in range(planes):
        take = zero_one(
            same_quarter
            & (named[:, offset : offset + 1] > 0.5)
            & (position[:, offset : offset + 1] == slot)
        )
        total = total + factors[:, offset : offset + 1] * exact_dot(take, returned[offset][...])
    total = total.astype(jnp.bfloat16)
    for quarter in range(QUARTERS):
        out_ref[:, quarter * width : (quarter + 1) * width] = total[
            quarter * rows : (quarter + 1) * rows, :
        ]


def shards(tokens, scales, routes, gate_codes, w_gate, w_up, w_down):
    tok_rows, features = tokens.shape
    picks_per = routes.shape[1]
    devices = lax.axis_size("expert")
    planes = devices // SHARDS
    capacity = 3 * tok_rows * picks_per // (2 * planes)
    width = features // QUARTERS
    tall = QUARTERS * capacity
    vmem = pl.BlockSpec(memory_space=pltpu.VMEM)
    hbm = pl.BlockSpec(memory_space=pl.ANY)
    anywhere = pl.BlockSpec(memory_space=pl.ANY)
    params = pltpu.CompilerParams(vmem_limit_bytes=VMEM_BYTES)
    pack_params = pltpu.CompilerParams(vmem_limit_bytes=PACK_VMEM_BYTES)
    load_params = pltpu.CompilerParams(vmem_limit_bytes=LOAD_VMEM_BYTES)

    def partner(array, distance):
        return lax.ppermute(array, "expert", [(i, i ^ distance) for i in range(devices)])

    block = jax.ShapeDtypeStruct((tall, width), jnp.bfloat16)
    packed = pl.pallas_call(
        functools.partial(pack_kernel, capacity, planes),
        out_shape=[block] * planes,
        in_specs=[hbm] * 2 + [vmem],
        out_specs=[vmem] * planes,
        scratch_shapes=[
            pltpu.VMEM((QUARTERS * tok_rows, width), jnp.bfloat16),
            pltpu.VMEM(tokens.shape, tokens.dtype),
            pltpu.VMEM(scales.shape, scales.dtype),
            pltpu.SemaphoreType.DMA,
            pltpu.SemaphoreType.DMA,
        ],
        compiler_params=pack_params,
    )(tokens, scales, routes.T)

    groups = ((0, planes // 2), (planes // 2, 3 * planes // 4), (3 * planes // 4, planes))
    arriving = [packed[0]] + [partner(packed[at], at * SHARDS) for at in range(1, planes)]
    returned = []
    weights, kept = (w_gate, w_up, w_down), None
    for start, stop in groups:
        gathered = []
        for offset in range(start, stop):
            own = arriving[offset]
            across = partner(own, 2)
            gathered += [own, across, partner(own, 1), partner(across, 1)]
        offsets = stop - start
        rows = offsets * SHARDS * capacity
        load = start == 0
        half = jax.ShapeDtypeStruct((2 * offsets * tall, width), jnp.bfloat16)
        scratch = [pltpu.VMEM((QUARTERS, rows, width), jnp.bfloat16)] * 2
        held = [jax.ShapeDtypeStruct(array.shape, array.dtype) for array in weights]
        kept, sent, *loaded = pl.pallas_call(
            functools.partial(expert_kernel, capacity, offsets, load),
            out_shape=[half] * 2 + (held if load else []),
            in_specs=[vmem] * (offsets * SHARDS) + ([hbm] * 3 if load else [vmem] * 3 + [anywhere]),
            out_specs=[vmem] * (5 if load else 2),
            scratch_shapes=scratch + ([pltpu.SemaphoreType.DMA((3 * QUARTERS,))] if load else []),
            compiler_params=load_params if load else params,
            cost_estimate=pl.CostEstimate(
                flops=6 * rows * features * w_gate.shape[2], bytes_accessed=0, transcendentals=0
            ),
        )(*gathered, *weights, *([] if load else [kept]))
        weights = loaded if load else weights
        if load:
            last = groups[-1][0]
            *arriving[last:], kept = lax.optimization_barrier((*arriving[last:], kept))
        arrived = partner(sent, 1).astype(jnp.float32)
        mine = kept.astype(jnp.float32)
        middle = offsets * tall
        across = partner((mine[middle:] + arrived[middle:]).astype(jnp.bfloat16), 2)
        answer = mine[:middle] + arrived[:middle] + across.astype(jnp.float32)
        answer = answer.astype(jnp.bfloat16)
        for offset in range(start, stop):
            piece = answer[(offset - start) * tall : (offset - start + 1) * tall]
            returned.append(piece if offset == 0 else partner(piece, offset * SHARDS))

    return pl.pallas_call(
        functools.partial(mix_kernel, capacity, planes),
        out_shape=jax.ShapeDtypeStruct((tok_rows, features), jnp.bfloat16),
        in_specs=[vmem] * (planes + 2),
        out_specs=vmem,
        compiler_params=params,
    )(routes.T, gate_codes.T, *returned)


def solution(mesh):
    in_specs = (
        P(("groups", "expert"), None),
        P(("groups", "expert"), None),
        P(("groups", "expert"), None),
        P(("groups", "expert"), None),
        P("expert", None, None),
        P("expert", None, None),
        P("expert", None, None),
    )
    out_specs = P(("groups", "expert"), None)
    return jax.shard_map(shards, mesh=mesh, in_specs=in_specs, out_specs=out_specs, check_vma=False)
```

```python
import functools

import jax
import jax.numpy as jnp
from jax import lax
from jax.experimental import pallas as pl
from jax.experimental.pallas import tpu as pltpu
from jax.sharding import PartitionSpec as P

SHARDS = 4
QUARTERS = 4
VMEM_BYTES = 16 * 1024 * 1024
PACK_VMEM_BYTES = 48 * 1024 * 1024
LOAD_VMEM_BYTES = 40 * 1024 * 1024


def zero_one(condition):
    return jnp.where(condition, 1.0, 0.0).astype(jnp.bfloat16)


def after(array, *others):
    return lax.optimization_barrier((array, *others))[0]


def exact_dot(left, right):
    return jnp.dot(left, right, preferred_element_type=jnp.float32)


def pack_kernel(capacity, planes, tok_hbm, scale_hbm, route_ref, *rest):
    outs = rest[:planes]
    quarters_ref, tok_ref, scale_ref, tok_sem, scale_sem = rest[planes:]
    tok_copy = pltpu.make_async_copy(tok_hbm, tok_ref, tok_sem)
    scale_copy = pltpu.make_async_copy(scale_hbm, scale_ref, scale_sem)
    tok_copy.start()
    scale_copy.start()
    rows, features = tok_ref.shape
    width = features // QUARTERS
    plane = lax.axis_index("expert") // SHARDS
    offsets = (route_ref[...] ^ plane).astype(jnp.float32).astype(jnp.bfloat16)
    columns = QUARTERS * rows
    picks = offsets.shape[0]
    copies = zero_one(
        lax.broadcasted_iota(jnp.int32, (rows, columns), 1) % rows
        == lax.broadcasted_iota(jnp.int32, (rows, columns), 0)
    )
    turned = exact_dot(offsets, copies)
    numbers = lax.broadcasted_iota(jnp.int32, (planes, columns), 0).astype(jnp.float32)
    named = jnp.zeros((planes, columns), jnp.float32)
    for pick in range(picks):
        named = named + jnp.where(turned[pick : pick + 1, :] == numbers, 1.0, 0.0)
    first = lax.broadcasted_iota(jnp.int32, (columns, columns), 0)
    second = lax.broadcasted_iota(jnp.int32, (columns, columns), 1)
    before = zero_one((first // rows == second // rows) & (first < second))
    position = exact_dot(named.astype(jnp.bfloat16), before)
    slot_row = lax.broadcasted_iota(jnp.int32, (QUARTERS * capacity, columns), 0)
    slot_col = lax.broadcasted_iota(jnp.int32, (QUARTERS * capacity, columns), 1)
    same_quarter = slot_row // capacity == slot_col // rows
    slot = (slot_row % capacity).astype(jnp.float32)
    tok_copy.wait()
    scale_copy.wait()
    for block in range(features // 128):
        quarter, at = divmod(block * 128, width)
        codes = tok_ref[:, block * 128 : (block + 1) * 128].astype(jnp.float32)
        factors = scale_ref[:, block : block + 1]
        quarters_ref[quarter * rows : (quarter + 1) * rows, at : at + 128] = (
            codes * factors
        ).astype(jnp.bfloat16)
    values = quarters_ref[...]
    for offset in range(planes):
        pick_out = zero_one(
            same_quarter
            & (named[offset : offset + 1, :] > 0.5)
            & (position[offset : offset + 1, :] == slot)
        )
        outs[offset][...] = exact_dot(pick_out, values).astype(jnp.bfloat16)


def order_matrix(capacity, turned):
    size = SHARDS * QUARTERS * capacity
    row = lax.broadcasted_iota(jnp.int32, (size, size), 1 if turned else 0)
    col = lax.broadcasted_iota(jnp.int32, (size, size), 0 if turned else 1)
    quarter, block, slot = row // (SHARDS * capacity), (row // capacity) % SHARDS, row % capacity
    return zero_one(col == (block * QUARTERS + quarter) * capacity + slot)


def load_kernel(gate_hbm, up_hbm, down_hbm, unused, gate_ref, up_ref, down_ref, sems):
    copies = [
        pltpu.make_async_copy(source, target, sems.at[index])
        for index, (source, target) in enumerate(
            ((gate_hbm, gate_ref), (up_hbm, up_ref), (down_hbm, down_ref))
        )
    ]
    for copy in copies:
        copy.start()
    for copy in copies:
        copy.wait()


def expert_kernel(capacity, offsets, *refs):
    count = 2 * offsets
    blocks = refs[:count]
    gate_ref, up_ref, down_ref, kept_ref, sent_ref, rows_ref, part_ref = refs[count:]
    group, tall = SHARDS * capacity, QUARTERS * capacity
    width = blocks[0].shape[1]
    spans = [slice(quarter * width, (quarter + 1) * width) for quarter in range(QUARTERS)]
    order = order_matrix(capacity, False)
    for offset in range(offsets):
        held = jnp.concatenate(
            [blocks[2 * offset][...], blocks[2 * offset + 1][...]], axis=0
        )
        sorted_rows = exact_dot(order, held).astype(jnp.bfloat16)
        for quarter in range(QUARTERS):
            rows_ref[quarter, offset * group : (offset + 1) * group, :] = sorted_rows[
                quarter * group : (quarter + 1) * group, :
            ]
    gate = jnp.zeros((offsets * group, gate_ref.shape[2]), jnp.float32)
    upward = jnp.zeros((offsets * group, gate_ref.shape[2]), jnp.float32)
    for quarter, span in enumerate(spans):
        gate = gate + exact_dot(rows_ref[quarter], gate_ref[0, span, :])
        upward = upward + exact_dot(rows_ref[quarter], up_ref[0, span, :])
    hidden = (gate / (1.0 + jnp.exp(-gate)) * upward).astype(jnp.bfloat16)
    for quarter, span in enumerate(spans):
        part_ref[quarter] = exact_dot(hidden, down_ref[0, :, span]).astype(jnp.bfloat16)
    back = order_matrix(capacity, True)
    for offset in range(offsets):
        held = jnp.concatenate(
            [
                part_ref[quarter, offset * group : (offset + 1) * group, :]
                for quarter in range(QUARTERS)
            ],
            axis=0,
        )
        answer = exact_dot(back, held).astype(jnp.bfloat16)
        for member in range(SHARDS):
            out_ref = sent_ref if member >= 2 else kept_ref
            at = (member % 2 * offsets + offset) * tall
            out_ref[at : at + tall, :] = answer[member * tall : (member + 1) * tall, :]


def mix_kernel(capacity, planes, route_ref, code_ref, *refs):
    returned, out_ref = refs[:planes], refs[planes]
    picks, rows = route_ref.shape
    width = out_ref.shape[1] // QUARTERS
    tall = QUARTERS * rows
    plane = lax.axis_index("expert") // SHARDS
    copies = zero_one(
        lax.broadcasted_iota(jnp.int32, (tall, rows), 0) % rows
        == lax.broadcasted_iota(jnp.int32, (tall, rows), 1)
    )

    def turned(numbers):
        numbers = numbers.astype(jnp.float32).astype(jnp.bfloat16)
        return lax.dot_general(
            copies, numbers, (((1,), (1,)), ((), ())), preferred_element_type=jnp.float32
        )

    offsets = turned(route_ref[...] ^ plane)
    codes = code_ref[...]
    weights = (turned(codes // 256) * 256.0 + turned(codes % 256)) / 65536.0
    numbers = lax.broadcasted_iota(jnp.int32, (tall, planes), 1).astype(jnp.float32)
    named = jnp.zeros((tall, planes), jnp.float32)
    factors = jnp.zeros((tall, planes), jnp.float32)
    for pick in range(picks):
        here = offsets[:, pick : pick + 1] == numbers
        named = named + jnp.where(here, 1.0, 0.0)
        factors = factors + jnp.where(here, weights[:, pick : pick + 1], 0.0)
    first = lax.broadcasted_iota(jnp.int32, (tall, tall), 0)
    second = lax.broadcasted_iota(jnp.int32, (tall, tall), 1)
    before = zero_one((first // rows == second // rows) & (second < first))
    position = exact_dot(before, named.astype(jnp.bfloat16))
    slot_row = lax.broadcasted_iota(jnp.int32, (tall, QUARTERS * capacity), 0)
    slot_col = lax.broadcasted_iota(jnp.int32, (tall, QUARTERS * capacity), 1)
    same_quarter = slot_row // rows == slot_col // capacity
    slot = (slot_col % capacity).astype(jnp.float32)
    total = jnp.zeros((tall, width), jnp.float32)
    for offset in range(planes):
        take = zero_one(
            same_quarter
            & (named[:, offset : offset + 1] > 0.5)
            & (position[:, offset : offset + 1] == slot)
        )
        total = total + factors[:, offset : offset + 1] * exact_dot(take, returned[offset][...])
    total = total.astype(jnp.bfloat16)
    for quarter in range(QUARTERS):
        out_ref[:, quarter * width : (quarter + 1) * width] = total[
            quarter * rows : (quarter + 1) * rows, :
        ]


def shards(tokens, scales, routes, gate_codes, w_gate, w_up, w_down):
    tok_rows, features = tokens.shape
    picks_per = routes.shape[1]
    devices = lax.axis_size("expert")
    planes = devices // SHARDS
    capacity = 3 * tok_rows * picks_per // (2 * planes)
    width = features // QUARTERS
    tall = QUARTERS * capacity
    vmem = pl.BlockSpec(memory_space=pltpu.VMEM)
    hbm = pl.BlockSpec(memory_space=pl.ANY)
    params = pltpu.CompilerParams(vmem_limit_bytes=VMEM_BYTES)
    pack_params = pltpu.CompilerParams(vmem_limit_bytes=PACK_VMEM_BYTES)
    load_params = pltpu.CompilerParams(vmem_limit_bytes=LOAD_VMEM_BYTES)

    def partner(array, distance):
        return lax.ppermute(array, "expert", [(i, i ^ distance) for i in range(devices)])

    block = jax.ShapeDtypeStruct((tall, width), jnp.bfloat16)
    packed = pl.pallas_call(
        functools.partial(pack_kernel, capacity, planes),
        out_shape=[block] * planes,
        in_specs=[hbm] * 2 + [vmem],
        out_specs=[vmem] * planes,
        scratch_shapes=[
            pltpu.VMEM((QUARTERS * tok_rows, width), jnp.bfloat16),
            pltpu.VMEM(tokens.shape, tokens.dtype),
            pltpu.VMEM(scales.shape, scales.dtype),
            pltpu.SemaphoreType.DMA,
            pltpu.SemaphoreType.DMA,
        ],
        compiler_params=pack_params,
    )(tokens, scales, routes.T)

    weights = pl.pallas_call(
        load_kernel,
        out_shape=[jax.ShapeDtypeStruct(w.shape, w.dtype) for w in (w_gate, w_up, w_down)],
        in_specs=[hbm] * 4,
        out_specs=[vmem] * 3,
        scratch_shapes=[pltpu.SemaphoreType.DMA((3,))],
        compiler_params=load_params,
    )(w_gate, w_up, w_down, packed[0])

    def expert(start, stop, held, weights):
        offsets = stop - start
        rows = offsets * SHARDS * capacity
        half = jax.ShapeDtypeStruct((2 * offsets * tall, width), jnp.bfloat16)
        return pl.pallas_call(
            functools.partial(expert_kernel, capacity, offsets),
            out_shape=[half] * 2,
            in_specs=[vmem] * (offsets * 2 + 3),
            out_specs=[vmem] * 2,
            scratch_shapes=[pltpu.VMEM((QUARTERS, rows, width), jnp.bfloat16)] * 2,
            compiler_params=params,
            cost_estimate=pl.CostEstimate(
                flops=6 * rows * features * w_gate.shape[2],
                bytes_accessed=0,
                transcendentals=0,
            ),
        )(*held, *weights)

    def across(array):
        return partner(array, 2)

    def along(array, offset):
        return array if offset == 0 else partner(array, offset * SHARDS)

    def fold(kept, arrived, offsets):
        middle = offsets * tall
        kept, arrived = kept.astype(jnp.float32), arrived.astype(jnp.float32)
        leaving = (kept[middle:] + arrived[middle:]).astype(jnp.bfloat16)
        return leaving, kept[:middle] + arrived[:middle]

    def pair(own, other):
        both = jnp.concatenate([own, other], axis=0)
        return [both, partner(both, 1)]

    half, late = planes // 2, 3 * planes // 4
    first, second, third = range(half), range(half, late), range(late, planes)
    arrive, cross, held, returned = {}, {}, {}, {}

    def take(table, places):
        return [table[at] for at in places]

    for at in list(second) + list(first):
        arrive[at] = along(packed[at], at)
    cross[0] = across(arrive[0])
    for at in first:
        if at:
            arrive[at] = after(arrive[at], *weights)
            cross[at] = across(arrive[at])
    for at in third:
        arrive[at] = along(after(packed[at], *take(arrive, second)), at)
    for at in second:
        cross[at] = across(after(arrive[at], cross[0]))
    for at in second:
        held[at] = pair(arrive[at], cross[at])
    held2 = sum(take(held, second), [])
    kept2, sent2 = expert(half, late, held2, weights)
    for at in first:
        held[at] = pair(arrive[at], cross[at])
    held1 = sum(take(held, first), [])
    held1[0] = after(held1[0], kept2)
    kept1, sent1 = expert(0, half, held1, weights)
    back2 = partner(sent2, 1)
    leave2, stay2 = fold(kept2, back2, len(second))
    for at in third:
        cross[at] = across(arrive[at])
    home2 = across(leave2)
    for at in third:
        held[at] = pair(arrive[at], cross[at])
    held3 = sum(take(held, third), [])
    held3[0] = after(held3[0], kept1, leave2)
    kept3, sent3 = expert(late, planes, held3, weights)
    back1 = partner(sent1, 1)
    leave1, stay1 = fold(kept1, back1, len(first))
    home1 = across(leave1)
    back3 = partner(sent3, 1)
    leave3, stay3 = fold(kept3, back3, len(third))
    home3 = across(leave3)
    answer2 = (stay2 + home2.astype(jnp.float32)).astype(jnp.bfloat16)
    for index, at in enumerate(second):
        returned[at] = along(answer2[index * tall : (index + 1) * tall], at)
    answer1 = (stay1 + home1.astype(jnp.float32)).astype(jnp.bfloat16)
    for index, at in enumerate(first):
        returned[at] = along(answer1[index * tall : (index + 1) * tall], at)
    answer3 = (stay3 + home3.astype(jnp.float32)).astype(jnp.bfloat16)
    answer3 = after(answer3, *take(returned, second))
    for index, at in enumerate(third):
        returned[at] = along(answer3[index * tall : (index + 1) * tall], at)
    returned = [returned[at] for at in range(planes)]

    return pl.pallas_call(
        functools.partial(mix_kernel, capacity, planes),
        out_shape=jax.ShapeDtypeStruct((tok_rows, features), jnp.bfloat16),
        in_specs=[vmem] * (planes + 2),
        out_specs=vmem,
        compiler_params=params,
    )(routes.T, gate_codes.T, *returned)


def solution(mesh):
    in_specs = (
        P(("groups", "expert"), None),
        P(("groups", "expert"), None),
        P(("groups", "expert"), None),
        P(("groups", "expert"), None),
        P("expert", None, None),
        P("expert", None, None),
        P("expert", None, None),
    )
    out_specs = P(("groups", "expert"), None)
    return jax.shard_map(shards, mesh=mesh, in_specs=in_specs, out_specs=out_specs, check_vma=False)
```

```python
import functools

import jax
import jax.numpy as jnp
from jax import lax
from jax.experimental import pallas as pl
from jax.experimental.pallas import tpu as pltpu
from jax.sharding import PartitionSpec as P

SHARDS = 4
QUARTERS = 4
GROUPS = ("own+near", "mid", "far")
SPLIT = ("c mid", "c near",)
ORDER = {
    "z far": ("y own",),
    "expert far": ("rc mid",),
    "rz far": ("z mid",),
    "c own": ("c near",),
    "c mid": ("y mid",),
    "rz mid": ("rc far", "c mid", "z near",),
    "c far": ("z near",),
    "ry own+near": ("y near",),
    "y far": ("z near",),
    "expert mid": ("c mid",),
    "c near": ("y mid", "load all",),
}
VMEM_BYTES = 16 * 1024 * 1024
PACK_VMEM_BYTES = 48 * 1024 * 1024
LOAD_VMEM_BYTES = 40 * 1024 * 1024


def zero_one(condition):
    return jnp.where(condition, 1.0, 0.0).astype(jnp.bfloat16)


def after(array, *others):
    return lax.optimization_barrier((array, *others))[0]


def exact_dot(left, right):
    return jnp.dot(left, right, preferred_element_type=jnp.float32)


def pack_kernel(capacity, planes, tok_hbm, scale_hbm, route_ref, *rest):
    outs = rest[:planes]
    quarters_ref, tok_ref, scale_ref, tok_sem, scale_sem = rest[planes:]
    tok_copy = pltpu.make_async_copy(tok_hbm, tok_ref, tok_sem)
    scale_copy = pltpu.make_async_copy(scale_hbm, scale_ref, scale_sem)
    tok_copy.start()
    scale_copy.start()
    rows, features = tok_ref.shape
    width = features // QUARTERS
    plane = lax.axis_index("expert") // SHARDS
    offsets = (route_ref[...] ^ plane).astype(jnp.float32).astype(jnp.bfloat16)
    columns = QUARTERS * rows
    picks = offsets.shape[0]
    copies = zero_one(
        lax.broadcasted_iota(jnp.int32, (rows, columns), 1) % rows
        == lax.broadcasted_iota(jnp.int32, (rows, columns), 0)
    )
    turned = exact_dot(offsets, copies)
    numbers = lax.broadcasted_iota(jnp.int32, (planes, columns), 0).astype(jnp.float32)
    named = jnp.zeros((planes, columns), jnp.float32)
    for pick in range(picks):
        named = named + jnp.where(turned[pick : pick + 1, :] == numbers, 1.0, 0.0)
    first = lax.broadcasted_iota(jnp.int32, (columns, columns), 0)
    second = lax.broadcasted_iota(jnp.int32, (columns, columns), 1)
    before = zero_one((first // rows == second // rows) & (first < second))
    position = exact_dot(named.astype(jnp.bfloat16), before)
    slot_row = lax.broadcasted_iota(jnp.int32, (QUARTERS * capacity, columns), 0)
    slot_col = lax.broadcasted_iota(jnp.int32, (QUARTERS * capacity, columns), 1)
    same_quarter = slot_row // capacity == slot_col // rows
    slot = (slot_row % capacity).astype(jnp.float32)
    tok_copy.wait()
    scale_copy.wait()
    for block in range(features // 128):
        quarter, at = divmod(block * 128, width)
        codes = tok_ref[:, block * 128 : (block + 1) * 128].astype(jnp.float32)
        factors = scale_ref[:, block : block + 1]
        quarters_ref[quarter * rows : (quarter + 1) * rows, at : at + 128] = (
            codes * factors
        ).astype(jnp.bfloat16)
    values = quarters_ref[...]
    for offset in range(planes):
        pick_out = zero_one(
            same_quarter
            & (named[offset : offset + 1, :] > 0.5)
            & (position[offset : offset + 1, :] == slot)
        )
        outs[offset][...] = exact_dot(pick_out, values).astype(jnp.bfloat16)


def order_matrix(capacity, turned):
    size = SHARDS * QUARTERS * capacity
    row = lax.broadcasted_iota(jnp.int32, (size, size), 1 if turned else 0)
    col = lax.broadcasted_iota(jnp.int32, (size, size), 0 if turned else 1)
    quarter, block, slot = row // (SHARDS * capacity), (row // capacity) % SHARDS, row % capacity
    return zero_one(col == (block * QUARTERS + quarter) * capacity + slot)


def load_kernel(gate_hbm, up_hbm, down_hbm, unused, gate_ref, up_ref, down_ref, sems):
    copies = [
        pltpu.make_async_copy(source, target, sems.at[index])
        for index, (source, target) in enumerate(
            ((gate_hbm, gate_ref), (up_hbm, up_ref), (down_hbm, down_ref))
        )
    ]
    for copy in copies:
        copy.start()
    for copy in copies:
        copy.wait()


def expert_kernel(capacity, offsets, *refs):
    count = 2 * offsets
    blocks = refs[:count]
    gate_ref, up_ref, down_ref, kept_ref, sent_ref, rows_ref, part_ref = refs[count:]
    group, tall = SHARDS * capacity, QUARTERS * capacity
    width = blocks[0].shape[1]
    spans = [slice(quarter * width, (quarter + 1) * width) for quarter in range(QUARTERS)]
    order = order_matrix(capacity, False)
    for offset in range(offsets):
        held = jnp.concatenate(
            [blocks[2 * offset][...], blocks[2 * offset + 1][...]], axis=0
        )
        sorted_rows = exact_dot(order, held).astype(jnp.bfloat16)
        for quarter in range(QUARTERS):
            rows_ref[quarter, offset * group : (offset + 1) * group, :] = sorted_rows[
                quarter * group : (quarter + 1) * group, :
            ]
    gate = jnp.zeros((offsets * group, gate_ref.shape[2]), jnp.float32)
    upward = jnp.zeros((offsets * group, gate_ref.shape[2]), jnp.float32)
    for quarter, span in enumerate(spans):
        gate = gate + exact_dot(rows_ref[quarter], gate_ref[0, span, :])
        upward = upward + exact_dot(rows_ref[quarter], up_ref[0, span, :])
    hidden = (gate / (1.0 + jnp.exp(-gate)) * upward).astype(jnp.bfloat16)
    for quarter, span in enumerate(spans):
        part_ref[quarter] = exact_dot(hidden, down_ref[0, :, span]).astype(jnp.bfloat16)
    back = order_matrix(capacity, True)
    for offset in range(offsets):
        held = jnp.concatenate(
            [
                part_ref[quarter, offset * group : (offset + 1) * group, :]
                for quarter in range(QUARTERS)
            ],
            axis=0,
        )
        answer = exact_dot(back, held).astype(jnp.bfloat16)
        for member in range(SHARDS):
            out_ref = sent_ref if member >= 2 else kept_ref
            at = (member % 2 * offsets + offset) * tall
            out_ref[at : at + tall, :] = answer[member * tall : (member + 1) * tall, :]


def mix_kernel(capacity, planes, route_ref, code_ref, *refs):
    returned, out_ref = refs[:planes], refs[planes]
    picks, rows = route_ref.shape
    width = out_ref.shape[1] // QUARTERS
    tall = QUARTERS * rows
    plane = lax.axis_index("expert") // SHARDS
    copies = zero_one(
        lax.broadcasted_iota(jnp.int32, (tall, rows), 0) % rows
        == lax.broadcasted_iota(jnp.int32, (tall, rows), 1)
    )

    def turned(numbers):
        numbers = numbers.astype(jnp.float32).astype(jnp.bfloat16)
        return lax.dot_general(
            copies, numbers, (((1,), (1,)), ((), ())), preferred_element_type=jnp.float32
        )

    offsets = turned(route_ref[...] ^ plane)
    codes = code_ref[...]
    weights = (turned(codes // 256) * 256.0 + turned(codes % 256)) / 65536.0
    numbers = lax.broadcasted_iota(jnp.int32, (tall, planes), 1).astype(jnp.float32)
    named = jnp.zeros((tall, planes), jnp.float32)
    factors = jnp.zeros((tall, planes), jnp.float32)
    for pick in range(picks):
        here = offsets[:, pick : pick + 1] == numbers
        named = named + jnp.where(here, 1.0, 0.0)
        factors = factors + jnp.where(here, weights[:, pick : pick + 1], 0.0)
    first = lax.broadcasted_iota(jnp.int32, (tall, tall), 0)
    second = lax.broadcasted_iota(jnp.int32, (tall, tall), 1)
    before = zero_one((first // rows == second // rows) & (second < first))
    position = exact_dot(before, named.astype(jnp.bfloat16))
    slot_row = lax.broadcasted_iota(jnp.int32, (tall, QUARTERS * capacity), 0)
    slot_col = lax.broadcasted_iota(jnp.int32, (tall, QUARTERS * capacity), 1)
    same_quarter = slot_row // rows == slot_col // capacity
    slot = (slot_col % capacity).astype(jnp.float32)
    total = jnp.zeros((tall, width), jnp.float32)
    for offset in range(planes):
        take = zero_one(
            same_quarter
            & (named[:, offset : offset + 1] > 0.5)
            & (position[:, offset : offset + 1] == slot)
        )
        total = total + factors[:, offset : offset + 1] * exact_dot(take, returned[offset][...])
    total = total.astype(jnp.bfloat16)
    for quarter in range(QUARTERS):
        out_ref[:, quarter * width : (quarter + 1) * width] = total[
            quarter * rows : (quarter + 1) * rows, :
        ]


def shards(tokens, scales, routes, gate_codes, w_gate, w_up, w_down):
    tok_rows, features = tokens.shape
    picks_per = routes.shape[1]
    devices = lax.axis_size("expert")
    planes = devices // SHARDS
    capacity = 3 * tok_rows * picks_per // (2 * planes)
    width = features // QUARTERS
    tall = QUARTERS * capacity
    vmem = pl.BlockSpec(memory_space=pltpu.VMEM)
    hbm = pl.BlockSpec(memory_space=pl.ANY)
    params = pltpu.CompilerParams(vmem_limit_bytes=VMEM_BYTES)
    pack_params = pltpu.CompilerParams(vmem_limit_bytes=PACK_VMEM_BYTES)
    load_params = pltpu.CompilerParams(vmem_limit_bytes=LOAD_VMEM_BYTES)

    def partner(array, distance):
        return lax.ppermute(array, "expert", [(i, i ^ distance) for i in range(devices)])

    block = jax.ShapeDtypeStruct((tall, width), jnp.bfloat16)
    packed = pl.pallas_call(
        functools.partial(pack_kernel, capacity, planes),
        out_shape=[block] * planes,
        in_specs=[hbm] * 2 + [vmem],
        out_specs=[vmem] * planes,
        scratch_shapes=[
            pltpu.VMEM((QUARTERS * tok_rows, width), jnp.bfloat16),
            pltpu.VMEM(tokens.shape, tokens.dtype),
            pltpu.VMEM(scales.shape, scales.dtype),
            pltpu.SemaphoreType.DMA,
            pltpu.SemaphoreType.DMA,
        ],
        compiler_params=pack_params,
    )(tokens, scales, routes.T)

    def expert(offsets, held, weights):
        rows = offsets * SHARDS * capacity
        half = jax.ShapeDtypeStruct((2 * offsets * tall, width), jnp.bfloat16)
        return pl.pallas_call(
            functools.partial(expert_kernel, capacity, offsets),
            out_shape=[half] * 2,
            in_specs=[vmem] * (offsets * 2 + 3),
            out_specs=[vmem] * 2,
            scratch_shapes=[pltpu.VMEM((QUARTERS, rows, width), jnp.bfloat16)] * 2,
            compiler_params=params,
            cost_estimate=pl.CostEstimate(
                flops=6 * rows * features * w_gate.shape[2],
                bytes_accessed=0,
                transcendentals=0,
            ),
        )(*held, *weights)

    def load(gate):
        return pl.pallas_call(
            load_kernel,
            out_shape=[jax.ShapeDtypeStruct(w.shape, w.dtype) for w in (w_gate, w_up, w_down)],
            in_specs=[hbm] * 4,
            out_specs=[vmem] * 3,
            scratch_shapes=[pltpu.SemaphoreType.DMA((3,))],
            compiler_params=load_params,
        )(w_gate, w_up, w_down, gate)

    def fold(kept, arrived, offsets):
        middle = offsets * tall
        kept, arrived = kept.astype(jnp.float32), arrived.astype(jnp.float32)
        leaving = (kept[middle:] + arrived[middle:]).astype(jnp.bfloat16)
        return leaving, kept[:middle] + arrived[:middle]

    half, late = planes // 2, 3 * planes // 4
    places = {
        "own": range(1),
        "near": range(1, half),
        "mid": range(half, late),
        "far": range(late, planes),
    }
    for group in GROUPS:
        places[group] = [at for member in group.split("+") for at in places[member]]
    results = {}

    def result(step):
        if step not in results:
            results[step] = build(*step.split())
        return results[step]

    def build(kind, name):
        if kind == "pack":
            return [packed[at] for at in places[name]]
        if kind == "z":
            inputs = result("pack " + name)
        elif kind == "y":
            inputs = result(("pack " if name == "own" else "z ") + name)
        elif kind == "c":
            own = result(("pack " if name == "own" else "z ") + name)
            inputs = [jnp.concatenate(both, axis=0) for both in zip(own, result("y " + name))]
        elif kind == "expert":
            inputs = []
            for member in name.split("+"):
                own = result(("pack " if member == "own" else "z ") + member)
                both = [jnp.concatenate(two, axis=0) for two in zip(own, result("y " + member))]
                for two in zip(both, result("c " + member)):
                    inputs += two
        elif kind == "rc":
            inputs = result("expert " + name)[1:]
        elif kind == "sum":
            kept, arrived = result("expert " + name)[0], result("rc " + name)[0]
            return fold(kept, arrived, len(places[name]))
        elif kind == "ry":
            inputs = result("sum " + name)[:1]
        elif kind == "answer":
            total = result("sum " + name)[1] + result("ry " + name)[0].astype(jnp.float32)
            total = total.astype(jnp.bfloat16)
            return [total[at * tall : (at + 1) * tall] for at in range(len(places[name]))]
        elif kind == "load":
            inputs = packed[:1]
        elif kind == "rz":
            inputs = [a for a, at in zip(result("answer " + name), places[name]) if at]
        earlier = [result(step)[-1] for step in ORDER.get(kind + " " + name, ())]
        if earlier:
            inputs = [after(inputs[0], *earlier)] + list(inputs[1:])
        if kind == "load":
            return load(inputs[0])
        if kind == "expert":
            return expert(len(places[name]), inputs, result("load all"))
        if kind in ("y", "ry"):
            return [partner(array, 2) for array in inputs]
        if kind in ("c", "rc"):
            if kind + " " + name not in SPLIT:
                return [partner(array, 1) for array in inputs]
            halves = [jnp.split(array, 2, axis=0) for array in inputs]
            if kind == "c":
                own = result(("pack " if name == "own" else "z ") + name)
                halves = [(one, two[1]) for one, two in zip(own, halves)]
            halves = [[partner(half, 1) for half in pair] for pair in halves]
            return [jnp.concatenate(pair, axis=0) for pair in halves]
        where = [at for at in places[name] if at]
        return [partner(array, at * SHARDS) for array, at in zip(inputs, where)]

    returned = {}
    for group in GROUPS:
        pieces = list(result("answer " + group))
        if group != "own":
            pieces[-len(result("rz " + group)) :] = result("rz " + group)
        returned.update(zip(places[group], pieces))
    returned = [returned[at] for at in range(planes)]

    return pl.pallas_call(
        functools.partial(mix_kernel, capacity, planes),
        out_shape=jax.ShapeDtypeStruct((tok_rows, features), jnp.bfloat16),
        in_specs=[vmem] * (planes + 2),
        out_specs=vmem,
        compiler_params=params,
    )(routes.T, gate_codes.T, *returned)


def solution(mesh):
    in_specs = (
        P(("groups", "expert"), None),
        P(("groups", "expert"), None),
        P(("groups", "expert"), None),
        P(("groups", "expert"), None),
        P("expert", None, None),
        P("expert", None, None),
        P("expert", None, None),
    )
    out_specs = P(("groups", "expert"), None)
    return jax.shard_map(shards, mesh=mesh, in_specs=in_specs, out_specs=out_specs, check_vma=False)
```

```python
import functools

import jax
import jax.numpy as jnp
from jax import lax
from jax.experimental import pallas as pl
from jax.experimental.pallas import tpu as pltpu
from jax.sharding import PartitionSpec as P

SHARDS = 4
QUARTERS = 4
GROUPS = ("own", "near", "mid", "far")
SPLIT = ()
ORDER = {
    "z mid": ("z near",),
    "y far": ("z far",),
    "y mid": ("z far",),
    "expert far": ("z near",),
    "rc far": ("load all",),
    "expert near": ("c mid",),
    "c mid": ("rc far",),
    "rc near": ("z far",),
    "ry near": ("c far", "y near",),
    "rc mid": ("expert near",),
    "c own": ("rc near", "z mid",),
    "rz far": ("c near", "rc far", "ry far", "expert mid",),
    "ry mid": ("load all",),
    "rz near": ("rc own", "y far",),
    "rc own": ("c mid",),
}
VMEM_BYTES = 16 * 1024 * 1024
LOAD_VMEM_BYTES = 40 * 1024 * 1024


def zero_one(condition):
    return jnp.where(condition, 1.0, 0.0).astype(jnp.bfloat16)


def after(array, *others):
    return lax.optimization_barrier((array, *others))[0]


def exact_dot(left, right):
    return jnp.dot(left, right, preferred_element_type=jnp.float32)


def spread(table_ref, pick, plane, rows, shape, axis):
    place = lax.broadcasted_iota(jnp.int32, shape, axis) % rows
    out = jnp.zeros(shape, jnp.int32)
    for row in range(rows):
        out = jnp.where(place == row, table_ref[pick, row] ^ plane, out)
    return out


def pack_kernel(capacity, planes, route_ref, tok_ref, scale_ref, *rest):
    outs, quarters_ref = rest[:planes], rest[planes]
    rows, features = tok_ref.shape
    picks, width = route_ref.shape[0], features // QUARTERS
    for block in range(features // 128):
        quarter, at = divmod(block * 128, width)
        codes = tok_ref[:, block * 128 : (block + 1) * 128].astype(jnp.float32)
        factors = scale_ref[:, block : block + 1]
        quarters_ref[quarter * rows : (quarter + 1) * rows, at : at + 128] = (
            codes * factors
        ).astype(jnp.bfloat16)
    plane = lax.axis_index("expert") // SHARDS
    columns = QUARTERS * rows
    numbers = lax.broadcasted_iota(jnp.int32, (planes, columns), 0)
    named = jnp.zeros((planes, columns), jnp.float32)
    for pick in range(picks):
        turned = spread(route_ref, pick, plane, rows, (1, columns), 1)
        named = named + jnp.where(turned == numbers, 1.0, 0.0)
    first = lax.broadcasted_iota(jnp.int32, (columns, columns), 0)
    second = lax.broadcasted_iota(jnp.int32, (columns, columns), 1)
    before = zero_one((first // rows == second // rows) & (first < second))
    position = exact_dot(named.astype(jnp.bfloat16), before)
    tall = QUARTERS * capacity
    slot_row = lax.broadcasted_iota(jnp.int32, (tall, columns), 0)
    slot_col = lax.broadcasted_iota(jnp.int32, (tall, columns), 1)
    same_quarter = slot_row // capacity == slot_col // rows
    slot = (slot_row % capacity).astype(jnp.float32)
    pick_out = [
        zero_one(
            same_quarter
            & (named[offset : offset + 1, :] > 0.5)
            & (position[offset : offset + 1, :] == slot)
        )
        for offset in range(planes)
    ]
    moved = exact_dot(jnp.concatenate(pick_out, axis=0), quarters_ref[...])
    for offset in range(planes):
        outs[offset][...] = moved[offset * tall : (offset + 1) * tall, :].astype(jnp.bfloat16)


def order_matrix(capacity, turned):
    size = SHARDS * QUARTERS * capacity
    row = lax.broadcasted_iota(jnp.int32, (size, size), 1 if turned else 0)
    col = lax.broadcasted_iota(jnp.int32, (size, size), 0 if turned else 1)
    quarter, block, slot = row // (SHARDS * capacity), (row // capacity) % SHARDS, row % capacity
    return zero_one(col == (block * QUARTERS + quarter) * capacity + slot)


def load_kernel(gate_hbm, up_hbm, down_hbm, unused, gate_ref, up_ref, down_ref, sems):
    copies = [
        pltpu.make_async_copy(source, target, sems.at[index])
        for index, (source, target) in enumerate(
            ((gate_hbm, gate_ref), (up_hbm, up_ref), (down_hbm, down_ref))
        )
    ]
    for copy in copies:
        copy.start()
    for copy in copies:
        copy.wait()


def expert_kernel(capacity, offsets, *refs):
    count = 2 * offsets
    blocks = refs[:count]
    gate_ref, up_ref, down_ref, kept_ref, sent_ref, rows_ref, part_ref = refs[count:]
    group, tall = SHARDS * capacity, QUARTERS * capacity
    width = blocks[0].shape[1]
    spans = [slice(quarter * width, (quarter + 1) * width) for quarter in range(QUARTERS)]
    order = order_matrix(capacity, False)
    for offset in range(offsets):
        held = jnp.concatenate(
            [blocks[2 * offset][...], blocks[2 * offset + 1][...]], axis=0
        )
        sorted_rows = exact_dot(order, held).astype(jnp.bfloat16)
        for quarter in range(QUARTERS):
            rows_ref[quarter, offset * group : (offset + 1) * group, :] = sorted_rows[
                quarter * group : (quarter + 1) * group, :
            ]
    gate = jnp.zeros((offsets * group, gate_ref.shape[2]), jnp.float32)
    upward = jnp.zeros((offsets * group, gate_ref.shape[2]), jnp.float32)
    for quarter, span in enumerate(spans):
        gate = gate + exact_dot(rows_ref[quarter], gate_ref[0, span, :])
        upward = upward + exact_dot(rows_ref[quarter], up_ref[0, span, :])
    hidden = (gate / (1.0 + jnp.exp(-gate)) * upward).astype(jnp.bfloat16)
    for quarter, span in enumerate(spans):
        part_ref[quarter] = exact_dot(hidden, down_ref[0, :, span]).astype(jnp.bfloat16)
    back = order_matrix(capacity, True)
    for offset in range(offsets):
        held = jnp.concatenate(
            [
                part_ref[quarter, offset * group : (offset + 1) * group, :]
                for quarter in range(QUARTERS)
            ],
            axis=0,
        )
        answer = exact_dot(back, held).astype(jnp.bfloat16)
        for member in range(SHARDS):
            out_ref = sent_ref if member >= 2 else kept_ref
            at = (member % 2 * offsets + offset) * tall
            out_ref[at : at + tall, :] = answer[member * tall : (member + 1) * tall, :]


def plan_kernel(capacity, planes, rows, route_ref, code_ref, unused, plan_ref):
    picks = route_ref.shape[0]
    tall = QUARTERS * rows
    plane = lax.axis_index("expert") // SHARDS
    numbers = lax.broadcasted_iota(jnp.int32, (tall, planes), 1)
    named = jnp.zeros((tall, planes), jnp.float32)
    coarse = jnp.zeros((tall, planes), jnp.float32)
    fine = jnp.zeros((tall, planes), jnp.float32)
    for pick in range(picks):
        here = spread(route_ref, pick, plane, rows, (tall, 1), 0) == numbers
        codes = spread(code_ref, pick, 0, rows, (tall, 1), 0)
        named = named + jnp.where(here, 1.0, 0.0)
        coarse = coarse + jnp.where(here, (codes // 256).astype(jnp.float32) / 256.0, 0.0)
        fine = fine + jnp.where(here, (codes % 256).astype(jnp.float32) / 65536.0, 0.0)
    first = lax.broadcasted_iota(jnp.int32, (tall, tall), 0)
    second = lax.broadcasted_iota(jnp.int32, (tall, tall), 1)
    before = zero_one((first // rows == second // rows) & (second < first))
    position = exact_dot(before, named.astype(jnp.bfloat16))
    slot_row = lax.broadcasted_iota(jnp.int32, (tall, QUARTERS * capacity), 0)
    slot_col = lax.broadcasted_iota(jnp.int32, (tall, QUARTERS * capacity), 1)
    same_quarter = slot_row // rows == slot_col // capacity
    slot = (slot_col % capacity).astype(jnp.float32)
    for offset in range(planes):
        column = slice(offset, offset + 1)
        take = same_quarter & (named[:, column] > 0.5) & (position[:, column] == slot)
        for half, factor in enumerate((coarse, fine)):
            plan_ref[offset, half * tall : (half + 1) * tall, :] = jnp.where(
                take, factor[:, column], 0.0
            ).astype(jnp.bfloat16)


def mix_kernel(planes, plan_ref, *refs):
    returned, out_ref = refs[:planes], refs[planes]
    rows, features = out_ref.shape
    width, tall = features // QUARTERS, QUARTERS * rows
    total = jnp.zeros((2 * tall, width), jnp.float32)
    for at in range(0, planes, 4):
        some = range(at, min(at + 4, planes))
        plan = jnp.concatenate([plan_ref[offset] for offset in some], axis=1)
        answers = jnp.concatenate([returned[offset][...] for offset in some], axis=0)
        total = total + exact_dot(plan, answers)
    total = (total[:tall] + total[tall:]).astype(jnp.bfloat16)
    for quarter in range(QUARTERS):
        out_ref[:, quarter * width : (quarter + 1) * width] = total[
            quarter * rows : (quarter + 1) * rows, :
        ]


def shards(tokens, scales, routes, gate_codes, w_gate, w_up, w_down):
    tok_rows, features = tokens.shape
    picks_per = routes.shape[1]
    devices = lax.axis_size("expert")
    planes = devices // SHARDS
    capacity = 3 * tok_rows * picks_per // (2 * planes)
    width = features // QUARTERS
    tall = QUARTERS * capacity
    vmem = pl.BlockSpec(memory_space=pltpu.VMEM)
    hbm = pl.BlockSpec(memory_space=pl.ANY)
    params = pltpu.CompilerParams(vmem_limit_bytes=VMEM_BYTES)
    load_params = pltpu.CompilerParams(vmem_limit_bytes=LOAD_VMEM_BYTES)

    def partner(array, distance):
        return lax.ppermute(array, "expert", [(i, i ^ distance) for i in range(devices)])

    block = jax.ShapeDtypeStruct((tall, width), jnp.bfloat16)
    smem = pl.BlockSpec(memory_space=pltpu.SMEM)
    packed = pl.pallas_call(
        functools.partial(pack_kernel, capacity, planes),
        out_shape=[block] * planes,
        in_specs=[smem, vmem, vmem],
        out_specs=[vmem] * planes,
        scratch_shapes=[pltpu.VMEM((QUARTERS * tok_rows, width), jnp.bfloat16)],
        compiler_params=params,
    )(routes.T, tokens, scales)
    plan = pl.pallas_call(
        functools.partial(plan_kernel, capacity, planes, tok_rows),
        out_shape=jax.ShapeDtypeStruct((planes, 2 * QUARTERS * tok_rows, tall), jnp.bfloat16),
        in_specs=[smem, smem, hbm],
        out_specs=vmem,
        compiler_params=params,
    )(routes.T, gate_codes.T, packed[0])

    def expert(offsets, held, weights):
        rows = offsets * SHARDS * capacity
        half = jax.ShapeDtypeStruct((2 * offsets * tall, width), jnp.bfloat16)
        return pl.pallas_call(
            functools.partial(expert_kernel, capacity, offsets),
            out_shape=[half] * 2,
            in_specs=[vmem] * (offsets * 2 + 3),
            out_specs=[vmem] * 2,
            scratch_shapes=[pltpu.VMEM((QUARTERS, rows, width), jnp.bfloat16)] * 2,
            compiler_params=params,
            cost_estimate=pl.CostEstimate(
                flops=6 * rows * features * w_gate.shape[2],
                bytes_accessed=0,
                transcendentals=0,
            ),
        )(*held, *weights)

    def load(gate):
        return pl.pallas_call(
            load_kernel,
            out_shape=[jax.ShapeDtypeStruct(w.shape, w.dtype) for w in (w_gate, w_up, w_down)],
            in_specs=[hbm] * 4,
            out_specs=[vmem] * 3,
            scratch_shapes=[pltpu.SemaphoreType.DMA((3,))],
            compiler_params=load_params,
        )(w_gate, w_up, w_down, gate)

    def fold(kept, arrived, offsets):
        middle = offsets * tall
        kept, arrived = kept.astype(jnp.float32), arrived.astype(jnp.float32)
        leaving = (kept[middle:] + arrived[middle:]).astype(jnp.bfloat16)
        return leaving, kept[:middle] + arrived[:middle]

    half, late = planes // 2, 3 * planes // 4
    places = {
        "own": range(1),
        "near": range(1, half),
        "mid": range(half, late),
        "far": range(late, planes),
    }
    for group in GROUPS:
        places[group] = [at for member in group.split("+") for at in places[member]]
    results = {}

    def result(step):
        if step not in results:
            results[step] = build(*step.split())
        return results[step]

    def build(kind, name):
        if kind == "pack":
            return [packed[at] for at in places[name]]
        if kind == "z":
            inputs = result("pack " + name)
        elif kind == "y":
            inputs = result(("pack " if name == "own" else "z ") + name)
        elif kind == "c":
            own = result(("pack " if name == "own" else "z ") + name)
            inputs = [jnp.concatenate(both, axis=0) for both in zip(own, result("y " + name))]
        elif kind == "expert":
            inputs = []
            for member in name.split("+"):
                own = result(("pack " if member == "own" else "z ") + member)
                both = [jnp.concatenate(two, axis=0) for two in zip(own, result("y " + member))]
                for two in zip(both, result("c " + member)):
                    inputs += two
        elif kind == "rc":
            inputs = result("expert " + name)[1:]
        elif kind == "sum":
            kept, arrived = result("expert " + name)[0], result("rc " + name)[0]
            return fold(kept, arrived, len(places[name]))
        elif kind == "ry":
            inputs = result("sum " + name)[:1]
        elif kind == "answer":
            total = result("sum " + name)[1] + result("ry " + name)[0].astype(jnp.float32)
            total = total.astype(jnp.bfloat16)
            return [total[at * tall : (at + 1) * tall] for at in range(len(places[name]))]
        elif kind == "load":
            inputs = packed[:1]
        elif kind == "rz":
            inputs = [a for a, at in zip(result("answer " + name), places[name]) if at]
        earlier = [result(step)[-1] for step in ORDER.get(kind + " " + name, ())]
        if earlier:
            inputs = [after(inputs[0], *earlier)] + list(inputs[1:])
        if kind == "load":
            return load(inputs[0])
        if kind == "expert":
            return expert(len(places[name]), inputs, result("load all"))
        if kind in ("y", "ry"):
            return [partner(array, 2) for array in inputs]
        if kind in ("c", "rc"):
            if kind + " " + name not in SPLIT:
                return [partner(array, 1) for array in inputs]
            halves = [jnp.split(array, 2, axis=0) for array in inputs]
            if kind == "c":
                own = result(("pack " if name == "own" else "z ") + name)
                halves = [(one, two[1]) for one, two in zip(own, halves)]
            halves = [[partner(half, 1) for half in pair] for pair in halves]
            return [jnp.concatenate(pair, axis=0) for pair in halves]
        where = [at for at in places[name] if at]
        return [partner(array, at * SHARDS) for array, at in zip(inputs, where)]

    returned = {}
    for group in GROUPS:
        pieces = list(result("answer " + group))
        if group != "own":
            pieces[-len(result("rz " + group)) :] = result("rz " + group)
        returned.update(zip(places[group], pieces))
    returned = [returned[at] for at in range(planes)]

    return pl.pallas_call(
        functools.partial(mix_kernel, planes),
        out_shape=jax.ShapeDtypeStruct((tok_rows, features), jnp.bfloat16),
        in_specs=[vmem] * (planes + 1),
        out_specs=vmem,
        compiler_params=params,
    )(plan, *returned)


def solution(mesh):
    in_specs = (
        P(("groups", "expert"), None),
        P(("groups", "expert"), None),
        P(("groups", "expert"), None),
        P(("groups", "expert"), None),
        P("expert", None, None),
        P("expert", None, None),
        P("expert", None, None),
    )
    out_specs = P(("groups", "expert"), None)
    return jax.shard_map(shards, mesh=mesh, in_specs=in_specs, out_specs=out_specs, check_vma=False)
```

```python
import functools

import jax
import jax.numpy as jnp
from jax import lax
from jax.experimental import pallas as pl
from jax.experimental.pallas import tpu as pltpu
from jax.sharding import PartitionSpec as P

SHARDS = 4
QUARTERS = 4
GROUPS = ("own+near", "mid", "far")
SPLIT = ("c mid", "c near", "rc mid",)
ORDER = {
    "z far": ("y own",),
    "expert own+near": ("y own",),
    "expert far": ("rc mid",),
    "c own": ("c near",),
    "rz mid": ("rc far", "z near",),
    "c far": ("z near", "expert mid",),
    "ry own+near": ("y near",),
    "y far": ("z near",),
}
VMEM_BYTES = 16 * 1024 * 1024
LOAD_VMEM_BYTES = 40 * 1024 * 1024


def zero_one(condition):
    return jnp.where(condition, 1.0, 0.0).astype(jnp.bfloat16)


def after(array, *others):
    return lax.optimization_barrier((array, *others))[0]


def exact_dot(left, right):
    return jnp.dot(left, right, preferred_element_type=jnp.float32)


def spread(table_ref, pick, plane, rows, shape, axis):
    place = lax.broadcasted_iota(jnp.int32, shape, axis) % rows
    out = jnp.zeros(shape, jnp.int32)
    for row in range(rows):
        out = jnp.where(place == row, table_ref[pick, row] ^ plane, out)
    return out


def pack_kernel(capacity, planes, route_hbm, tok_hbm, scale_hbm, *rest):
    outs = rest[:planes]
    quarters_ref, tok_ref, scale_ref, route_ref, sems = rest[planes:]
    sources, targets = (route_hbm, scale_hbm, tok_hbm), (route_ref, scale_ref, tok_ref)
    copies = [
        pltpu.make_async_copy(source, target, sems.at[index])
        for index, (source, target) in enumerate(zip(sources, targets))
    ]
    for copy in copies:
        copy.start()
    rows, features = tok_ref.shape
    picks, width = route_ref.shape[0], features // QUARTERS
    copies[0].wait()
    plane = lax.axis_index("expert") // SHARDS
    columns = QUARTERS * rows
    numbers = lax.broadcasted_iota(jnp.int32, (planes, columns), 0)
    named = jnp.zeros((planes, columns), jnp.float32)
    for pick in range(picks):
        turned = spread(route_ref, pick, plane, rows, (1, columns), 1)
        named = named + jnp.where(turned == numbers, 1.0, 0.0)
    first = lax.broadcasted_iota(jnp.int32, (columns, columns), 0)
    second = lax.broadcasted_iota(jnp.int32, (columns, columns), 1)
    before = zero_one((first // rows == second // rows) & (first < second))
    position = exact_dot(named.astype(jnp.bfloat16), before)
    tall = QUARTERS * capacity
    slot_row = lax.broadcasted_iota(jnp.int32, (tall, columns), 0)
    slot_col = lax.broadcasted_iota(jnp.int32, (tall, columns), 1)
    same_quarter = slot_row // capacity == slot_col // rows
    slot = (slot_row % capacity).astype(jnp.float32)
    pick_out = [
        zero_one(
            same_quarter
            & (named[offset : offset + 1, :] > 0.5)
            & (position[offset : offset + 1, :] == slot)
        )
        for offset in range(planes)
    ]
    copies[1].wait()
    copies[2].wait()
    for block in range(features // 128):
        quarter, at = divmod(block * 128, width)
        codes = tok_ref[:, block * 128 : (block + 1) * 128].astype(jnp.float32)
        factors = scale_ref[:, block : block + 1]
        quarters_ref[quarter * rows : (quarter + 1) * rows, at : at + 128] = (
            codes * factors
        ).astype(jnp.bfloat16)
    moved = exact_dot(jnp.concatenate(pick_out, axis=0), quarters_ref[...])
    for offset in range(planes):
        outs[offset][...] = moved[offset * tall : (offset + 1) * tall, :].astype(jnp.bfloat16)


def order_matrix(capacity, turned):
    size = SHARDS * QUARTERS * capacity
    row = lax.broadcasted_iota(jnp.int32, (size, size), 1 if turned else 0)
    col = lax.broadcasted_iota(jnp.int32, (size, size), 0 if turned else 1)
    quarter, block, slot = row // (SHARDS * capacity), (row // capacity) % SHARDS, row % capacity
    return zero_one(col == (block * QUARTERS + quarter) * capacity + slot)


def load_kernel(gate_hbm, up_hbm, down_hbm, unused, gate_ref, up_ref, down_ref, sems):
    copies = [
        pltpu.make_async_copy(source, target, sems.at[index])
        for index, (source, target) in enumerate(
            ((gate_hbm, gate_ref), (up_hbm, up_ref), (down_hbm, down_ref))
        )
    ]
    for copy in copies:
        copy.start()
    for copy in copies:
        copy.wait()


def expert_kernel(capacity, offsets, *refs):
    count = 2 * offsets
    blocks = refs[:count]
    gate_ref, up_ref, down_ref, kept_ref, sent_ref, rows_ref, part_ref = refs[count:]
    group, tall = SHARDS * capacity, QUARTERS * capacity
    width = blocks[0].shape[1]
    spans = [slice(quarter * width, (quarter + 1) * width) for quarter in range(QUARTERS)]
    order = order_matrix(capacity, False)
    for offset in range(offsets):
        held = jnp.concatenate(
            [blocks[2 * offset][...], blocks[2 * offset + 1][...]], axis=0
        )
        sorted_rows = exact_dot(order, held).astype(jnp.bfloat16)
        for quarter in range(QUARTERS):
            rows_ref[quarter, offset * group : (offset + 1) * group, :] = sorted_rows[
                quarter * group : (quarter + 1) * group, :
            ]
    gate = jnp.zeros((offsets * group, gate_ref.shape[2]), jnp.float32)
    upward = jnp.zeros((offsets * group, gate_ref.shape[2]), jnp.float32)
    for quarter, span in enumerate(spans):
        gate = gate + exact_dot(rows_ref[quarter], gate_ref[0, span, :])
        upward = upward + exact_dot(rows_ref[quarter], up_ref[0, span, :])
    hidden = (gate / (1.0 + jnp.exp(-gate)) * upward).astype(jnp.bfloat16)
    for quarter, span in enumerate(spans):
        part_ref[quarter] = exact_dot(hidden, down_ref[0, :, span]).astype(jnp.bfloat16)
    back = order_matrix(capacity, True)
    for offset in range(offsets):
        held = jnp.concatenate(
            [
                part_ref[quarter, offset * group : (offset + 1) * group, :]
                for quarter in range(QUARTERS)
            ],
            axis=0,
        )
        answer = exact_dot(back, held).astype(jnp.bfloat16)
        for member in range(SHARDS):
            out_ref = sent_ref if member >= 2 else kept_ref
            at = (member % 2 * offsets + offset) * tall
            out_ref[at : at + tall, :] = answer[member * tall : (member + 1) * tall, :]


def plan_kernel(capacity, planes, rows, route_hbm, code_hbm, unused, plan_ref, *scratch):
    route_ref, code_ref, sems = scratch
    copies = [
        pltpu.make_async_copy(route_hbm, route_ref, sems.at[0]),
        pltpu.make_async_copy(code_hbm, code_ref, sems.at[1]),
    ]
    for copy in copies:
        copy.start()
    for copy in copies:
        copy.wait()
    picks = route_ref.shape[0]
    tall = QUARTERS * rows
    plane = lax.axis_index("expert") // SHARDS
    numbers = lax.broadcasted_iota(jnp.int32, (tall, planes), 1)
    named = jnp.zeros((tall, planes), jnp.float32)
    coarse = jnp.zeros((tall, planes), jnp.float32)
    fine = jnp.zeros((tall, planes), jnp.float32)
    for pick in range(picks):
        here = spread(route_ref, pick, plane, rows, (tall, 1), 0) == numbers
        codes = spread(code_ref, pick, 0, rows, (tall, 1), 0)
        named = named + jnp.where(here, 1.0, 0.0)
        coarse = coarse + jnp.where(here, (codes // 256).astype(jnp.float32) / 256.0, 0.0)
        fine = fine + jnp.where(here, (codes % 256).astype(jnp.float32) / 65536.0, 0.0)
    first = lax.broadcasted_iota(jnp.int32, (tall, tall), 0)
    second = lax.broadcasted_iota(jnp.int32, (tall, tall), 1)
    before = zero_one((first // rows == second // rows) & (second < first))
    position = exact_dot(before, named.astype(jnp.bfloat16))
    slot_row = lax.broadcasted_iota(jnp.int32, (tall, QUARTERS * capacity), 0)
    slot_col = lax.broadcasted_iota(jnp.int32, (tall, QUARTERS * capacity), 1)
    same_quarter = slot_row // rows == slot_col // capacity
    slot = (slot_col % capacity).astype(jnp.float32)
    for offset in range(planes):
        column = slice(offset, offset + 1)
        take = same_quarter & (named[:, column] > 0.5) & (position[:, column] == slot)
        for half, factor in enumerate((coarse, fine)):
            plan_ref[offset, half * tall : (half + 1) * tall, :] = jnp.where(
                take, factor[:, column], 0.0
            ).astype(jnp.bfloat16)


def mix_kernel(planes, plan_ref, *refs):
    returned, out_ref = refs[:planes], refs[planes]
    rows, features = out_ref.shape
    width, tall = features // QUARTERS, QUARTERS * rows
    total = jnp.zeros((2 * tall, width), jnp.float32)
    for at in range(0, planes, 4):
        some = range(at, min(at + 4, planes))
        plan = jnp.concatenate([plan_ref[offset] for offset in some], axis=1)
        answers = jnp.concatenate([returned[offset][...] for offset in some], axis=0)
        total = total + exact_dot(plan, answers)
    total = (total[:tall] + total[tall:]).astype(jnp.bfloat16)
    for quarter in range(QUARTERS):
        out_ref[:, quarter * width : (quarter + 1) * width] = total[
            quarter * rows : (quarter + 1) * rows, :
        ]


def shards(tokens, scales, routes, gate_codes, w_gate, w_up, w_down):
    tok_rows, features = tokens.shape
    picks_per = routes.shape[1]
    devices = lax.axis_size("expert")
    planes = devices // SHARDS
    capacity = 3 * tok_rows * picks_per // (2 * planes)
    width = features // QUARTERS
    tall = QUARTERS * capacity
    vmem = pl.BlockSpec(memory_space=pltpu.VMEM)
    hbm = pl.BlockSpec(memory_space=pl.ANY)
    params = pltpu.CompilerParams(vmem_limit_bytes=VMEM_BYTES)
    load_params = pltpu.CompilerParams(vmem_limit_bytes=LOAD_VMEM_BYTES)

    def in_hbm(array):
        return pltpu.with_memory_space_constraint(array, pltpu.HBM)

    def partner(array, distance):
        return lax.ppermute(array, "expert", [(i, i ^ distance) for i in range(devices)])

    block = jax.ShapeDtypeStruct((tall, width), jnp.bfloat16)
    packed = pl.pallas_call(
        functools.partial(pack_kernel, capacity, planes),
        out_shape=[block] * planes,
        in_specs=[hbm] * 3,
        out_specs=[vmem] * planes,
        scratch_shapes=[
            pltpu.VMEM((QUARTERS * tok_rows, width), jnp.bfloat16),
            pltpu.VMEM(tokens.shape, tokens.dtype),
            pltpu.VMEM(scales.shape, scales.dtype),
            pltpu.SMEM(routes.T.shape, routes.dtype),
            pltpu.SemaphoreType.DMA((3,)),
        ],
        compiler_params=params,
    )(in_hbm(routes.T), in_hbm(tokens), in_hbm(scales))
    plan = pl.pallas_call(
        functools.partial(plan_kernel, capacity, planes, tok_rows),
        out_shape=jax.ShapeDtypeStruct((planes, 2 * QUARTERS * tok_rows, tall), jnp.bfloat16),
        in_specs=[hbm] * 3,
        out_specs=vmem,
        scratch_shapes=[pltpu.SMEM(routes.T.shape, routes.dtype)] * 2
        + [pltpu.SemaphoreType.DMA((2,))],
        compiler_params=params,
    )(in_hbm(routes.T), in_hbm(gate_codes.T), packed[0])

    def expert(offsets, held, weights):
        rows = offsets * SHARDS * capacity
        half = jax.ShapeDtypeStruct((2 * offsets * tall, width), jnp.bfloat16)
        return pl.pallas_call(
            functools.partial(expert_kernel, capacity, offsets),
            out_shape=[half] * 2,
            in_specs=[vmem] * (offsets * 2 + 3),
            out_specs=[vmem] * 2,
            scratch_shapes=[pltpu.VMEM((QUARTERS, rows, width), jnp.bfloat16)] * 2,
            compiler_params=params,
            cost_estimate=pl.CostEstimate(
                flops=6 * rows * features * w_gate.shape[2],
                bytes_accessed=0,
                transcendentals=0,
            ),
        )(*held, *weights)

    def load(gate):
        return pl.pallas_call(
            load_kernel,
            out_shape=[jax.ShapeDtypeStruct(w.shape, w.dtype) for w in (w_gate, w_up, w_down)],
            in_specs=[hbm] * 4,
            out_specs=[vmem] * 3,
            scratch_shapes=[pltpu.SemaphoreType.DMA((3,))],
            compiler_params=load_params,
        )(in_hbm(w_gate), in_hbm(w_up), in_hbm(w_down), gate)

    def fold(kept, arrived, offsets):
        middle = offsets * tall
        kept, arrived = kept.astype(jnp.float32), arrived.astype(jnp.float32)
        leaving = (kept[middle:] + arrived[middle:]).astype(jnp.bfloat16)
        return leaving, kept[:middle] + arrived[:middle]

    half, late = planes // 2, 3 * planes // 4
    places = {
        "own": range(1),
        "near": range(1, half),
        "mid": range(half, late),
        "far": range(late, planes),
    }
    for group in GROUPS:
        places[group] = [at for member in group.split("+") for at in places[member]]
    results = {}

    def result(step):
        if step not in results:
            results[step] = build(*step.split())
        return results[step]

    def build(kind, name):
        if kind == "pack":
            return [packed[at] for at in places[name]]
        if kind == "z":
            inputs = result("pack " + name)
        elif kind == "y":
            inputs = result(("pack " if name == "own" else "z ") + name)
        elif kind == "c":
            own = result(("pack " if name == "own" else "z ") + name)
            inputs = [jnp.concatenate(both, axis=0) for both in zip(own, result("y " + name))]
        elif kind == "expert":
            inputs = []
            for member in name.split("+"):
                own = result(("pack " if member == "own" else "z ") + member)
                both = [jnp.concatenate(two, axis=0) for two in zip(own, result("y " + member))]
                for two in zip(both, result("c " + member)):
                    inputs += two
        elif kind == "rc":
            inputs = result("expert " + name)[1:]
        elif kind == "sum":
            kept, arrived = result("expert " + name)[0], result("rc " + name)[0]
            return fold(kept, arrived, len(places[name]))
        elif kind == "ry":
            inputs = result("sum " + name)[:1]
        elif kind == "answer":
            total = result("sum " + name)[1] + result("ry " + name)[0].astype(jnp.float32)
            total = total.astype(jnp.bfloat16)
            return [total[at * tall : (at + 1) * tall] for at in range(len(places[name]))]
        elif kind == "load":
            inputs = packed[:1]
        elif kind == "rz":
            inputs = [a for a, at in zip(result("answer " + name), places[name]) if at]
        earlier = [result(step)[-1] for step in ORDER.get(kind + " " + name, ())]
        if earlier:
            inputs = [after(inputs[0], *earlier)] + list(inputs[1:])
        if kind == "load":
            return load(inputs[0])
        if kind == "expert":
            return expert(len(places[name]), inputs, result("load all"))
        if kind in ("y", "ry"):
            return [partner(array, 2) for array in inputs]
        if kind in ("c", "rc"):
            if kind + " " + name not in SPLIT:
                return [partner(array, 1) for array in inputs]
            halves = [jnp.split(array, 2, axis=0) for array in inputs]
            if kind == "c":
                own = result(("pack " if name == "own" else "z ") + name)
                halves = [(one, two[1]) for one, two in zip(own, halves)]
            halves = [[partner(half, 1) for half in pair] for pair in halves]
            return [jnp.concatenate(pair, axis=0) for pair in halves]
        where = [at for at in places[name] if at]
        return [partner(array, at * SHARDS) for array, at in zip(inputs, where)]

    returned = {}
    for group in GROUPS:
        pieces = list(result("answer " + group))
        if group != "own":
            pieces[-len(result("rz " + group)) :] = result("rz " + group)
        returned.update(zip(places[group], pieces))
    returned = [returned[at] for at in range(planes)]

    return pl.pallas_call(
        functools.partial(mix_kernel, planes),
        out_shape=jax.ShapeDtypeStruct((tok_rows, features), jnp.bfloat16),
        in_specs=[vmem] * (planes + 1),
        out_specs=vmem,
        compiler_params=params,
    )(plan, *returned)


def solution(mesh):
    in_specs = (
        P(("groups", "expert"), None),
        P(("groups", "expert"), None),
        P(("groups", "expert"), None),
        P(("groups", "expert"), None),
        P("expert", None, None),
        P("expert", None, None),
        P("expert", None, None),
    )
    out_specs = P(("groups", "expert"), None)
    return jax.shard_map(shards, mesh=mesh, in_specs=in_specs, out_specs=out_specs, check_vma=False)
```

```python
import functools

import jax
import jax.numpy as jnp
from jax import lax
from jax.experimental import pallas as pl
from jax.experimental.pallas import tpu as pltpu
from jax.sharding import PartitionSpec as P

SHARDS = 4
QUARTERS = 4
GROUPS = ("own+near", "mid", "far")
FIRST = "mid"
SPLIT = ("c mid", "c near", "rc mid",)
DIRECT = ()
ORDER = {
    "z far": ("y own",),
    "expert own+near": ("y own",),
    "expert far": ("rc mid", "c own",),
    "rz far": ("load all",),
    "c own": ("c near",),
    "rc far": ("y far",),
    "rz mid": ("rc far",),
    "c far": ("z near",),
    "ry own+near": ("y near",),
    "y far": ("z near",),
}
VMEM_BYTES = 16 * 1024 * 1024
LOAD_VMEM_BYTES = 40 * 1024 * 1024


def zero_one(condition):
    return jnp.where(condition, 1.0, 0.0).astype(jnp.bfloat16)


def after(array, *others):
    return lax.optimization_barrier((array, *others))[0]


def exact_dot(left, right):
    return jnp.dot(left, right, preferred_element_type=jnp.float32)


def spread(table_ref, pick, plane, rows, shape, axis):
    place = lax.broadcasted_iota(jnp.int32, shape, axis) % rows
    out = jnp.zeros(shape, jnp.int32)
    for row in range(rows):
        out = jnp.where(place == row, table_ref[pick, row] ^ plane, out)
    return out


def pack_kernel(capacity, planes, route_hbm, tok_hbm, scale_hbm, *rest):
    outs = rest[:planes]
    quarters_ref, tok_ref, scale_ref, route_ref, sems = rest[planes:]
    sources, targets = (route_hbm, scale_hbm, tok_hbm), (route_ref, scale_ref, tok_ref)
    copies = [
        pltpu.make_async_copy(source, target, sems.at[index])
        for index, (source, target) in enumerate(zip(sources, targets))
    ]
    for copy in copies:
        copy.start()
    rows, features = tok_ref.shape
    picks, width = route_ref.shape[0], features // QUARTERS
    copies[0].wait()
    plane = lax.axis_index("expert") // SHARDS
    columns = QUARTERS * rows
    numbers = lax.broadcasted_iota(jnp.int32, (planes, columns), 0)
    named = jnp.zeros((planes, columns), jnp.float32)
    for pick in range(picks):
        turned = spread(route_ref, pick, plane, rows, (1, columns), 1)
        named = named + jnp.where(turned == numbers, 1.0, 0.0)
    first = lax.broadcasted_iota(jnp.int32, (columns, columns), 0)
    second = lax.broadcasted_iota(jnp.int32, (columns, columns), 1)
    before = zero_one((first // rows == second // rows) & (first < second))
    position = exact_dot(named.astype(jnp.bfloat16), before)
    tall = QUARTERS * capacity
    slot_row = lax.broadcasted_iota(jnp.int32, (tall, columns), 0)
    slot_col = lax.broadcasted_iota(jnp.int32, (tall, columns), 1)
    same_quarter = slot_row // capacity == slot_col // rows
    slot = (slot_row % capacity).astype(jnp.float32)
    pick_out = [
        zero_one(
            same_quarter
            & (named[offset : offset + 1, :] > 0.5)
            & (position[offset : offset + 1, :] == slot)
        )
        for offset in range(planes)
    ]
    copies[1].wait()
    copies[2].wait()
    for block in range(features // 128):
        quarter, at = divmod(block * 128, width)
        codes = tok_ref[:, block * 128 : (block + 1) * 128].astype(jnp.float32)
        factors = scale_ref[:, block : block + 1]
        quarters_ref[quarter * rows : (quarter + 1) * rows, at : at + 128] = (
            codes * factors
        ).astype(jnp.bfloat16)
    moved = exact_dot(jnp.concatenate(pick_out, axis=0), quarters_ref[...])
    for offset in range(planes):
        outs[offset][...] = moved[offset * tall : (offset + 1) * tall, :].astype(jnp.bfloat16)


def order_matrix(capacity, turned):
    size = SHARDS * QUARTERS * capacity
    row = lax.broadcasted_iota(jnp.int32, (size, size), 1 if turned else 0)
    col = lax.broadcasted_iota(jnp.int32, (size, size), 0 if turned else 1)
    quarter, block, slot = row // (SHARDS * capacity), (row // capacity) % SHARDS, row % capacity
    return zero_one(col == (block * QUARTERS + quarter) * capacity + slot)


def load_kernel(gate_hbm, up_hbm, unused, gate_ref, up_ref, sems):
    copies = [
        pltpu.make_async_copy(gate_hbm, gate_ref, sems.at[0]),
        pltpu.make_async_copy(up_hbm, up_ref, sems.at[1]),
    ]
    for copy in copies:
        copy.start()
    for copy in copies:
        copy.wait()


def expert_kernel(capacity, offsets, first, *refs):
    count = 2 * offsets
    blocks = refs[:count]
    if first:
        gate_ref, up_ref, down_hbm, kept_ref, sent_ref, down_ref, *scratch = refs[count:]
        rows_ref, part_ref, sem = scratch
        down_copy = pltpu.make_async_copy(down_hbm, down_ref, sem)
        down_copy.start()
    else:
        gate_ref, up_ref, down_ref, kept_ref, sent_ref, rows_ref, part_ref = refs[count:]
    group, tall = SHARDS * capacity, QUARTERS * capacity
    width = blocks[0].shape[1]
    spans = [slice(quarter * width, (quarter + 1) * width) for quarter in range(QUARTERS)]
    order = order_matrix(capacity, False)
    for offset in range(offsets):
        held = jnp.concatenate(
            [blocks[2 * offset][...], blocks[2 * offset + 1][...]], axis=0
        )
        sorted_rows = exact_dot(order, held).astype(jnp.bfloat16)
        for quarter in range(QUARTERS):
            rows_ref[quarter, offset * group : (offset + 1) * group, :] = sorted_rows[
                quarter * group : (quarter + 1) * group, :
            ]
    gate = jnp.zeros((offsets * group, gate_ref.shape[2]), jnp.float32)
    upward = jnp.zeros((offsets * group, gate_ref.shape[2]), jnp.float32)
    for quarter, span in enumerate(spans):
        gate = gate + exact_dot(rows_ref[quarter], gate_ref[0, span, :])
        upward = upward + exact_dot(rows_ref[quarter], up_ref[0, span, :])
    hidden = (gate / (1.0 + jnp.exp(-gate)) * upward).astype(jnp.bfloat16)
    if first:
        down_copy.wait()
    for quarter, span in enumerate(spans):
        part_ref[quarter] = exact_dot(hidden, down_ref[0, :, span]).astype(jnp.bfloat16)
    back = order_matrix(capacity, True)
    for offset in range(offsets):
        held = jnp.concatenate(
            [
                part_ref[quarter, offset * group : (offset + 1) * group, :]
                for quarter in range(QUARTERS)
            ],
            axis=0,
        )
        answer = exact_dot(back, held).astype(jnp.bfloat16)
        for member in range(SHARDS):
            out_ref = sent_ref if member >= 2 else kept_ref
            at = (member % 2 * offsets + offset) * tall
            out_ref[at : at + tall, :] = answer[member * tall : (member + 1) * tall, :]


def plan_kernel(capacity, planes, rows, route_hbm, code_hbm, unused, plan_ref, *scratch):
    route_ref, code_ref, sems = scratch
    copies = [
        pltpu.make_async_copy(route_hbm, route_ref, sems.at[0]),
        pltpu.make_async_copy(code_hbm, code_ref, sems.at[1]),
    ]
    for copy in copies:
        copy.start()
    for copy in copies:
        copy.wait()
    picks = route_ref.shape[0]
    tall = QUARTERS * rows
    plane = lax.axis_index("expert") // SHARDS
    numbers = lax.broadcasted_iota(jnp.int32, (tall, planes), 1)
    named = jnp.zeros((tall, planes), jnp.float32)
    coarse = jnp.zeros((tall, planes), jnp.float32)
    fine = jnp.zeros((tall, planes), jnp.float32)
    for pick in range(picks):
        here = spread(route_ref, pick, plane, rows, (tall, 1), 0) == numbers
        codes = spread(code_ref, pick, 0, rows, (tall, 1), 0)
        named = named + jnp.where(here, 1.0, 0.0)
        coarse = coarse + jnp.where(here, (codes // 256).astype(jnp.float32) / 256.0, 0.0)
        fine = fine + jnp.where(here, (codes % 256).astype(jnp.float32) / 65536.0, 0.0)
    first = lax.broadcasted_iota(jnp.int32, (tall, tall), 0)
    second = lax.broadcasted_iota(jnp.int32, (tall, tall), 1)
    before = zero_one((first // rows == second // rows) & (second < first))
    position = exact_dot(before, named.astype(jnp.bfloat16))
    slot_row = lax.broadcasted_iota(jnp.int32, (tall, QUARTERS * capacity), 0)
    slot_col = lax.broadcasted_iota(jnp.int32, (tall, QUARTERS * capacity), 1)
    same_quarter = slot_row // rows == slot_col // capacity
    slot = (slot_col % capacity).astype(jnp.float32)
    for offset in range(planes):
        column = slice(offset, offset + 1)
        take = same_quarter & (named[:, column] > 0.5) & (position[:, column] == slot)
        for half, factor in enumerate((coarse, fine)):
            plan_ref[offset, half * tall : (half + 1) * tall, :] = jnp.where(
                take, factor[:, column], 0.0
            ).astype(jnp.bfloat16)


def mix_kernel(planes, plan_ref, *refs):
    returned, out_ref = refs[:planes], refs[planes]
    rows, features = out_ref.shape
    width, tall = features // QUARTERS, QUARTERS * rows
    total = jnp.zeros((2 * tall, width), jnp.float32)
    for at in range(0, planes, 4):
        some = range(at, min(at + 4, planes))
        plan = jnp.concatenate([plan_ref[offset] for offset in some], axis=1)
        answers = jnp.concatenate([returned[offset][...] for offset in some], axis=0)
        total = total + exact_dot(plan, answers)
    total = (total[:tall] + total[tall:]).astype(jnp.bfloat16)
    for quarter in range(QUARTERS):
        out_ref[:, quarter * width : (quarter + 1) * width] = total[
            quarter * rows : (quarter + 1) * rows, :
        ]


def shards(tokens, scales, routes, gate_codes, w_gate, w_up, w_down):
    tok_rows, features = tokens.shape
    picks_per = routes.shape[1]
    devices = lax.axis_size("expert")
    planes = devices // SHARDS
    capacity = 3 * tok_rows * picks_per // (2 * planes)
    width = features // QUARTERS
    tall = QUARTERS * capacity
    vmem = pl.BlockSpec(memory_space=pltpu.VMEM)
    hbm = pl.BlockSpec(memory_space=pl.ANY)
    params = pltpu.CompilerParams(vmem_limit_bytes=VMEM_BYTES)
    load_params = pltpu.CompilerParams(vmem_limit_bytes=LOAD_VMEM_BYTES)

    def in_hbm(array):
        return pltpu.with_memory_space_constraint(array, pltpu.HBM)

    def partner(array, distance):
        return lax.ppermute(array, "expert", [(i, i ^ distance) for i in range(devices)])

    block = jax.ShapeDtypeStruct((tall, width), jnp.bfloat16)
    packed = pl.pallas_call(
        functools.partial(pack_kernel, capacity, planes),
        out_shape=[block] * planes,
        in_specs=[hbm] * 3,
        out_specs=[vmem] * planes,
        scratch_shapes=[
            pltpu.VMEM((QUARTERS * tok_rows, width), jnp.bfloat16),
            pltpu.VMEM(tokens.shape, tokens.dtype),
            pltpu.VMEM(scales.shape, scales.dtype),
            pltpu.SMEM(routes.T.shape, routes.dtype),
            pltpu.SemaphoreType.DMA((3,)),
        ],
        compiler_params=params,
    )(in_hbm(routes.T), in_hbm(tokens), in_hbm(scales))
    plan = pl.pallas_call(
        functools.partial(plan_kernel, capacity, planes, tok_rows),
        out_shape=jax.ShapeDtypeStruct((planes, 2 * QUARTERS * tok_rows, tall), jnp.bfloat16),
        in_specs=[hbm] * 3,
        out_specs=vmem,
        scratch_shapes=[pltpu.SMEM(routes.T.shape, routes.dtype)] * 2
        + [pltpu.SemaphoreType.DMA((2,))],
        compiler_params=params,
    )(in_hbm(routes.T), in_hbm(gate_codes.T), packed[0])

    held_down = []

    def expert(offsets, held, weights):
        rows = offsets * SHARDS * capacity
        first = not held_down
        half = jax.ShapeDtypeStruct((2 * offsets * tall, width), jnp.bfloat16)
        whole = jax.ShapeDtypeStruct(w_down.shape, w_down.dtype)
        kept, sent, *down = pl.pallas_call(
            functools.partial(expert_kernel, capacity, offsets, first),
            out_shape=[half] * 2 + [whole] * first,
            in_specs=[vmem] * (offsets * 2 + 2) + [hbm if first else vmem],
            out_specs=[vmem] * (2 + first),
            scratch_shapes=[pltpu.VMEM((QUARTERS, rows, width), jnp.bfloat16)] * 2
            + [pltpu.SemaphoreType.DMA] * first,
            compiler_params=load_params if first else params,
            cost_estimate=pl.CostEstimate(
                flops=6 * rows * features * w_gate.shape[2],
                bytes_accessed=0,
                transcendentals=0,
            ),
        )(*held, *weights, *(held_down or [in_hbm(w_down)]))
        held_down.extend(down)
        return kept, sent

    def load(gate):
        return pl.pallas_call(
            load_kernel,
            out_shape=[jax.ShapeDtypeStruct(w.shape, w.dtype) for w in (w_gate, w_up)],
            in_specs=[hbm] * 3,
            out_specs=[vmem] * 2,
            scratch_shapes=[pltpu.SemaphoreType.DMA((2,))],
            compiler_params=load_params,
        )(in_hbm(w_gate), in_hbm(w_up), gate)

    def fold(kept, arrived, offsets):
        middle = offsets * tall
        kept, arrived = kept.astype(jnp.float32), arrived.astype(jnp.float32)
        leaving = (kept[middle:] + arrived[middle:]).astype(jnp.bfloat16)
        return leaving, kept[:middle] + arrived[:middle]

    half, late = planes // 2, 3 * planes // 4
    places = {
        "own": range(1),
        "near": range(1, half),
        "mid": range(half, late),
        "far": range(late, planes),
    }
    for group in GROUPS:
        places[group] = [at for member in group.split("+") for at in places[member]]
    results = {}

    def result(step):
        if step not in results:
            results[step] = build(*step.split())
        return results[step]

    def build(kind, name):
        if kind == "pack":
            return [packed[at] for at in places[name]]
        if kind == "z":
            inputs = result("pack " + name)
        elif kind == "y":
            inputs = result(("pack " if name == "own" or name in DIRECT else "z ") + name)
        elif kind == "c":
            own = result(("pack " if name == "own" else "z ") + name)
            inputs = [jnp.concatenate(both, axis=0) for both in zip(own, result("y " + name))]
        elif kind == "expert":
            inputs = []
            for member in name.split("+"):
                own = result(("pack " if member == "own" else "z ") + member)
                both = [jnp.concatenate(two, axis=0) for two in zip(own, result("y " + member))]
                for two in zip(both, result("c " + member)):
                    inputs += two
        elif kind == "rc":
            inputs = result("expert " + name)[1:]
        elif kind == "sum":
            kept, arrived = result("expert " + name)[0], result("rc " + name)[0]
            return fold(kept, arrived, len(places[name]))
        elif kind == "ry":
            inputs = result("sum " + name)[:1]
        elif kind == "answer":
            total = result("sum " + name)[1] + result("ry " + name)[0].astype(jnp.float32)
            total = total.astype(jnp.bfloat16)
            return [total[at * tall : (at + 1) * tall] for at in range(len(places[name]))]
        elif kind == "load":
            inputs = packed[:1]
        elif kind == "rz":
            inputs = [a for a, at in zip(result("answer " + name), places[name]) if at]
        earlier = [result(step)[-1] for step in ORDER.get(kind + " " + name, ())]
        if earlier:
            inputs = [after(inputs[0], *earlier)] + list(inputs[1:])
        if kind == "load":
            return load(inputs[0])
        if kind == "expert":
            if name != FIRST:
                result("expert " + FIRST)
            return expert(len(places[name]), inputs, result("load all"))
        if kind == "y" and name in DIRECT:
            return [partner(array, at * SHARDS + 2) for array, at in zip(inputs, places[name])]
        if kind in ("y", "ry"):
            return [partner(array, 2) for array in inputs]
        if kind in ("c", "rc"):
            if kind + " " + name not in SPLIT:
                return [partner(array, 1) for array in inputs]
            halves = [jnp.split(array, 2, axis=0) for array in inputs]
            if kind == "c":
                own = result(("pack " if name == "own" else "z ") + name)
                halves = [(one, two[1]) for one, two in zip(own, halves)]
            halves = [[partner(half, 1) for half in pair] for pair in halves]
            return [jnp.concatenate(pair, axis=0) for pair in halves]
        where = [at for at in places[name] if at]
        return [partner(array, at * SHARDS) for array, at in zip(inputs, where)]

    returned = {}
    for group in GROUPS:
        pieces = list(result("answer " + group))
        if group != "own":
            pieces[-len(result("rz " + group)) :] = result("rz " + group)
        returned.update(zip(places[group], pieces))
    returned = [returned[at] for at in range(planes)]

    return pl.pallas_call(
        functools.partial(mix_kernel, planes),
        out_shape=jax.ShapeDtypeStruct((tok_rows, features), jnp.bfloat16),
        in_specs=[vmem] * (planes + 1),
        out_specs=vmem,
        compiler_params=params,
    )(plan, *returned)


def solution(mesh):
    in_specs = (
        P(("groups", "expert"), None),
        P(("groups", "expert"), None),
        P(("groups", "expert"), None),
        P(("groups", "expert"), None),
        P("expert", None, None),
        P("expert", None, None),
        P("expert", None, None),
    )
    out_specs = P(("groups", "expert"), None)
    return jax.shard_map(shards, mesh=mesh, in_specs=in_specs, out_specs=out_specs, check_vma=False)
```

```python
import functools

import jax
import jax.numpy as jnp
from jax import lax
from jax.experimental import pallas as pl
from jax.experimental.pallas import tpu as pltpu
from jax.sharding import PartitionSpec as P

SHARDS = 4
QUARTERS = 4
GROUPS = ("own+near", "mid", "far")
SPLIT = ("c mid", "c near", "rc mid",)
DIRECT = ()
ORDER = {
    "z far": ("y own",),
    "expert own+near": ("y own",),
    "expert far": ("rc mid", "c own",),
    "rz far": ("load all",),
    "c own": ("c near",),
    "rc far": ("y far",),
    "rz mid": ("rc far",),
    "c far": ("z near",),
    "ry own+near": ("y near",),
    "y far": ("z near",),
}
VMEM_BYTES = 16 * 1024 * 1024
LOAD_VMEM_BYTES = 40 * 1024 * 1024


def zero_one(condition):
    return jnp.where(condition, 1.0, 0.0).astype(jnp.bfloat16)


def after(array, *others):
    return lax.optimization_barrier((array, *others))[0]


def exact_dot(left, right):
    return jnp.dot(left, right, preferred_element_type=jnp.float32)


def spread(table_ref, pick, plane, rows, shape, axis):
    place = lax.broadcasted_iota(jnp.int32, shape, axis) % rows
    out = jnp.zeros(shape, jnp.int32)
    for row in range(rows):
        out = jnp.where(place == row, table_ref[pick, row] ^ plane, out)
    return out


def pack_kernel(capacity, planes, route_hbm, tok_hbm, scale_hbm, *rest):
    outs = rest[:planes]
    quarters_ref, tok_ref, scale_ref, route_ref, sems = rest[planes:]
    sources, targets = (route_hbm, scale_hbm, tok_hbm), (route_ref, scale_ref, tok_ref)
    copies = [
        pltpu.make_async_copy(source, target, sems.at[index])
        for index, (source, target) in enumerate(zip(sources, targets))
    ]
    for copy in copies:
        copy.start()
    rows, features = tok_ref.shape
    picks, width = route_ref.shape[0], features // QUARTERS
    copies[0].wait()
    plane = lax.axis_index("expert") // SHARDS
    columns = QUARTERS * rows
    numbers = lax.broadcasted_iota(jnp.int32, (planes, columns), 0)
    named = jnp.zeros((planes, columns), jnp.float32)
    for pick in range(picks):
        turned = spread(route_ref, pick, plane, rows, (1, columns), 1)
        named = named + jnp.where(turned == numbers, 1.0, 0.0)
    first = lax.broadcasted_iota(jnp.int32, (columns, columns), 0)
    second = lax.broadcasted_iota(jnp.int32, (columns, columns), 1)
    before = zero_one((first // rows == second // rows) & (first < second))
    position = exact_dot(named.astype(jnp.bfloat16), before)
    tall = QUARTERS * capacity
    slot_row = lax.broadcasted_iota(jnp.int32, (tall, columns), 0)
    slot_col = lax.broadcasted_iota(jnp.int32, (tall, columns), 1)
    same_quarter = slot_row // capacity == slot_col // rows
    slot = (slot_row % capacity).astype(jnp.float32)
    pick_out = [
        zero_one(
            same_quarter
            & (named[offset : offset + 1, :] > 0.5)
            & (position[offset : offset + 1, :] == slot)
        )
        for offset in range(planes)
    ]
    copies[1].wait()
    copies[2].wait()
    for block in range(features // 128):
        quarter, at = divmod(block * 128, width)
        codes = tok_ref[:, block * 128 : (block + 1) * 128].astype(jnp.float32)
        factors = scale_ref[:, block : block + 1]
        quarters_ref[quarter * rows : (quarter + 1) * rows, at : at + 128] = (
            codes * factors
        ).astype(jnp.bfloat16)
    moved = exact_dot(jnp.concatenate(pick_out, axis=0), quarters_ref[...])
    for offset in range(planes):
        outs[offset][...] = moved[offset * tall : (offset + 1) * tall, :].astype(jnp.bfloat16)


def order_matrix(capacity, turned):
    size = SHARDS * QUARTERS * capacity
    row = lax.broadcasted_iota(jnp.int32, (size, size), 1 if turned else 0)
    col = lax.broadcasted_iota(jnp.int32, (size, size), 0 if turned else 1)
    quarter, block, slot = row // (SHARDS * capacity), (row // capacity) % SHARDS, row % capacity
    return zero_one(col == (block * QUARTERS + quarter) * capacity + slot)


def load_kernel(gate_hbm, up_hbm, down_hbm, unused, both_ref, down_ref, sems):
    hidden = gate_hbm.shape[2]
    copies = [
        pltpu.make_async_copy(gate_hbm.at[0], both_ref.at[:, pl.ds(0, hidden)], sems.at[0]),
        pltpu.make_async_copy(up_hbm.at[0], both_ref.at[:, pl.ds(hidden, hidden)], sems.at[1]),
        pltpu.make_async_copy(down_hbm, down_ref, sems.at[2]),
    ]
    for copy in copies:
        copy.start()
    for copy in copies:
        copy.wait()


def expert_kernel(capacity, offsets, *refs):
    count = 2 * offsets
    blocks = refs[:count]
    both_ref, down_ref, kept_ref, sent_ref, rows_ref, part_ref = refs[count:]
    group, tall = SHARDS * capacity, QUARTERS * capacity
    width = blocks[0].shape[1]
    spans = [slice(quarter * width, (quarter + 1) * width) for quarter in range(QUARTERS)]
    order = order_matrix(capacity, False)
    for offset in range(offsets):
        held = jnp.concatenate(
            [blocks[2 * offset][...], blocks[2 * offset + 1][...]], axis=0
        )
        sorted_rows = exact_dot(order, held).astype(jnp.bfloat16)
        for quarter in range(QUARTERS):
            rows_ref[quarter, offset * group : (offset + 1) * group, :] = sorted_rows[
                quarter * group : (quarter + 1) * group, :
            ]
    both = jnp.zeros((offsets * group, both_ref.shape[1]), jnp.float32)
    for quarter, span in enumerate(spans):
        both = both + exact_dot(rows_ref[quarter], both_ref[span, :])
    gate, upward = jnp.split(both, 2, axis=1)
    hidden = (gate / (1.0 + jnp.exp(-gate)) * upward).astype(jnp.bfloat16)
    for quarter, span in enumerate(spans):
        part_ref[quarter] = exact_dot(hidden, down_ref[0, :, span]).astype(jnp.bfloat16)
    back = order_matrix(capacity, True)
    for offset in range(offsets):
        held = jnp.concatenate(
            [
                part_ref[quarter, offset * group : (offset + 1) * group, :]
                for quarter in range(QUARTERS)
            ],
            axis=0,
        )
        answer = exact_dot(back, held).astype(jnp.bfloat16)
        for member in range(SHARDS):
            out_ref = sent_ref if member >= 2 else kept_ref
            at = (member % 2 * offsets + offset) * tall
            out_ref[at : at + tall, :] = answer[member * tall : (member + 1) * tall, :]


def plan_kernel(capacity, planes, rows, route_hbm, code_hbm, unused, plan_ref, *scratch):
    route_ref, code_ref, sems = scratch
    copies = [
        pltpu.make_async_copy(route_hbm, route_ref, sems.at[0]),
        pltpu.make_async_copy(code_hbm, code_ref, sems.at[1]),
    ]
    for copy in copies:
        copy.start()
    for copy in copies:
        copy.wait()
    picks = route_ref.shape[0]
    tall = QUARTERS * rows
    plane = lax.axis_index("expert") // SHARDS
    numbers = lax.broadcasted_iota(jnp.int32, (tall, planes), 1)
    named = jnp.zeros((tall, planes), jnp.float32)
    coarse = jnp.zeros((tall, planes), jnp.float32)
    fine = jnp.zeros((tall, planes), jnp.float32)
    for pick in range(picks):
        here = spread(route_ref, pick, plane, rows, (tall, 1), 0) == numbers
        codes = spread(code_ref, pick, 0, rows, (tall, 1), 0)
        named = named + jnp.where(here, 1.0, 0.0)
        coarse = coarse + jnp.where(here, (codes // 256).astype(jnp.float32) / 256.0, 0.0)
        fine = fine + jnp.where(here, (codes % 256).astype(jnp.float32) / 65536.0, 0.0)
    first = lax.broadcasted_iota(jnp.int32, (tall, tall), 0)
    second = lax.broadcasted_iota(jnp.int32, (tall, tall), 1)
    before = zero_one((first // rows == second // rows) & (second < first))
    position = exact_dot(before, named.astype(jnp.bfloat16))
    slot_row = lax.broadcasted_iota(jnp.int32, (tall, QUARTERS * capacity), 0)
    slot_col = lax.broadcasted_iota(jnp.int32, (tall, QUARTERS * capacity), 1)
    same_quarter = slot_row // rows == slot_col // capacity
    slot = (slot_col % capacity).astype(jnp.float32)
    for offset in range(planes):
        column = slice(offset, offset + 1)
        take = same_quarter & (named[:, column] > 0.5) & (position[:, column] == slot)
        for half, factor in enumerate((coarse, fine)):
            plan_ref[offset, half * tall : (half + 1) * tall, :] = jnp.where(
                take, factor[:, column], 0.0
            ).astype(jnp.bfloat16)


def mix_kernel(planes, plan_ref, *refs):
    returned, out_ref = refs[:planes], refs[planes]
    rows, features = out_ref.shape
    width, tall = features // QUARTERS, QUARTERS * rows
    total = jnp.zeros((2 * tall, width), jnp.float32)
    for at in range(0, planes, 4):
        some = range(at, min(at + 4, planes))
        plan = jnp.concatenate([plan_ref[offset] for offset in some], axis=1)
        answers = jnp.concatenate([returned[offset][...] for offset in some], axis=0)
        total = total + exact_dot(plan, answers)
    total = (total[:tall] + total[tall:]).astype(jnp.bfloat16)
    for quarter in range(QUARTERS):
        out_ref[:, quarter * width : (quarter + 1) * width] = total[
            quarter * rows : (quarter + 1) * rows, :
        ]


def shards(tokens, scales, routes, gate_codes, w_gate, w_up, w_down):
    tok_rows, features = tokens.shape
    picks_per = routes.shape[1]
    devices = lax.axis_size("expert")
    planes = devices // SHARDS
    capacity = 3 * tok_rows * picks_per // (2 * planes)
    width = features // QUARTERS
    tall = QUARTERS * capacity
    vmem = pl.BlockSpec(memory_space=pltpu.VMEM)
    hbm = pl.BlockSpec(memory_space=pl.ANY)
    params = pltpu.CompilerParams(vmem_limit_bytes=VMEM_BYTES)
    load_params = pltpu.CompilerParams(vmem_limit_bytes=LOAD_VMEM_BYTES)

    def in_hbm(array):
        return pltpu.with_memory_space_constraint(array, pltpu.HBM)

    def partner(array, distance):
        return lax.ppermute(array, "expert", [(i, i ^ distance) for i in range(devices)])

    block = jax.ShapeDtypeStruct((tall, width), jnp.bfloat16)
    packed = pl.pallas_call(
        functools.partial(pack_kernel, capacity, planes),
        out_shape=[block] * planes,
        in_specs=[hbm] * 3,
        out_specs=[vmem] * planes,
        scratch_shapes=[
            pltpu.VMEM((QUARTERS * tok_rows, width), jnp.bfloat16),
            pltpu.VMEM(tokens.shape, tokens.dtype),
            pltpu.VMEM(scales.shape, scales.dtype),
            pltpu.SMEM(routes.T.shape, routes.dtype),
            pltpu.SemaphoreType.DMA((3,)),
        ],
        compiler_params=params,
    )(in_hbm(routes.T), in_hbm(tokens), in_hbm(scales))
    plan = pl.pallas_call(
        functools.partial(plan_kernel, capacity, planes, tok_rows),
        out_shape=jax.ShapeDtypeStruct((planes, 2 * QUARTERS * tok_rows, tall), jnp.bfloat16),
        in_specs=[hbm] * 3,
        out_specs=vmem,
        scratch_shapes=[pltpu.SMEM(routes.T.shape, routes.dtype)] * 2
        + [pltpu.SemaphoreType.DMA((2,))],
        compiler_params=params,
    )(in_hbm(routes.T), in_hbm(gate_codes.T), packed[0])

    def expert(offsets, held, weights):
        rows = offsets * SHARDS * capacity
        half = jax.ShapeDtypeStruct((2 * offsets * tall, width), jnp.bfloat16)
        return pl.pallas_call(
            functools.partial(expert_kernel, capacity, offsets),
            out_shape=[half] * 2,
            in_specs=[vmem] * (offsets * 2 + 2),
            out_specs=[vmem] * 2,
            scratch_shapes=[pltpu.VMEM((QUARTERS, rows, width), jnp.bfloat16)] * 2,
            compiler_params=params,
            cost_estimate=pl.CostEstimate(
                flops=6 * rows * features * w_gate.shape[2],
                bytes_accessed=0,
                transcendentals=0,
            ),
        )(*held, *weights)

    def load(gate):
        return pl.pallas_call(
            load_kernel,
            out_shape=[
                jax.ShapeDtypeStruct((features, 2 * w_gate.shape[2]), w_gate.dtype),
                jax.ShapeDtypeStruct(w_down.shape, w_down.dtype),
            ],
            in_specs=[hbm] * 4,
            out_specs=[vmem] * 2,
            scratch_shapes=[pltpu.SemaphoreType.DMA((3,))],
            compiler_params=load_params,
        )(in_hbm(w_gate), in_hbm(w_up), in_hbm(w_down), gate)

    def fold(kept, arrived, offsets):
        middle = offsets * tall
        kept, arrived = kept.astype(jnp.float32), arrived.astype(jnp.float32)
        leaving = (kept[middle:] + arrived[middle:]).astype(jnp.bfloat16)
        return leaving, kept[:middle] + arrived[:middle]

    half, late = planes // 2, 3 * planes // 4
    places = {
        "own": range(1),
        "near": range(1, half),
        "mid": range(half, late),
        "far": range(late, planes),
    }
    for group in GROUPS:
        places[group] = [at for member in group.split("+") for at in places[member]]
    results = {}

    def result(step):
        if step not in results:
            results[step] = build(*step.split())
        return results[step]

    def build(kind, name):
        if kind == "pack":
            return [packed[at] for at in places[name]]
        if kind == "z":
            inputs = result("pack " + name)
        elif kind == "y":
            inputs = result(("pack " if name == "own" or name in DIRECT else "z ") + name)
        elif kind == "c":
            own = result(("pack " if name == "own" else "z ") + name)
            inputs = [jnp.concatenate(both, axis=0) for both in zip(own, result("y " + name))]
        elif kind == "expert":
            inputs = []
            for member in name.split("+"):
                own = result(("pack " if member == "own" else "z ") + member)
                both = [jnp.concatenate(two, axis=0) for two in zip(own, result("y " + member))]
                for two in zip(both, result("c " + member)):
                    inputs += two
        elif kind == "rc":
            inputs = result("expert " + name)[1:]
        elif kind == "sum":
            kept, arrived = result("expert " + name)[0], result("rc " + name)[0]
            return fold(kept, arrived, len(places[name]))
        elif kind == "ry":
            inputs = result("sum " + name)[:1]
        elif kind == "answer":
            total = result("sum " + name)[1] + result("ry " + name)[0].astype(jnp.float32)
            total = total.astype(jnp.bfloat16)
            return [total[at * tall : (at + 1) * tall] for at in range(len(places[name]))]
        elif kind == "load":
            inputs = packed[:1]
        elif kind == "rz":
            inputs = [a for a, at in zip(result("answer " + name), places[name]) if at]
        earlier = [result(step)[-1] for step in ORDER.get(kind + " " + name, ())]
        if earlier:
            inputs = [after(inputs[0], *earlier)] + list(inputs[1:])
        if kind == "load":
            return load(inputs[0])
        if kind == "expert":
            return expert(len(places[name]), inputs, result("load all"))
        if kind == "y" and name in DIRECT:
            return [partner(array, at * SHARDS + 2) for array, at in zip(inputs, places[name])]
        if kind in ("y", "ry"):
            return [partner(array, 2) for array in inputs]
        if kind in ("c", "rc"):
            if kind + " " + name not in SPLIT:
                return [partner(array, 1) for array in inputs]
            halves = [jnp.split(array, 2, axis=0) for array in inputs]
            if kind == "c":
                own = result(("pack " if name == "own" else "z ") + name)
                halves = [(one, two[1]) for one, two in zip(own, halves)]
            halves = [[partner(half, 1) for half in pair] for pair in halves]
            return [jnp.concatenate(pair, axis=0) for pair in halves]
        where = [at for at in places[name] if at]
        return [partner(array, at * SHARDS) for array, at in zip(inputs, where)]

    returned = {}
    for group in GROUPS:
        pieces = list(result("answer " + group))
        if group != "own":
            pieces[-len(result("rz " + group)) :] = result("rz " + group)
        returned.update(zip(places[group], pieces))
    returned = [returned[at] for at in range(planes)]

    return pl.pallas_call(
        functools.partial(mix_kernel, planes),
        out_shape=jax.ShapeDtypeStruct((tok_rows, features), jnp.bfloat16),
        in_specs=[vmem] * (planes + 1),
        out_specs=vmem,
        compiler_params=params,
    )(plan, *returned)


def solution(mesh):
    in_specs = (
        P(("groups", "expert"), None),
        P(("groups", "expert"), None),
        P(("groups", "expert"), None),
        P(("groups", "expert"), None),
        P("expert", None, None),
        P("expert", None, None),
        P("expert", None, None),
    )
    out_specs = P(("groups", "expert"), None)
    return jax.shard_map(shards, mesh=mesh, in_specs=in_specs, out_specs=out_specs, check_vma=False)
```

```python
import functools

import jax
import jax.numpy as jnp
from jax import lax
from jax.experimental import pallas as pl
from jax.experimental.pallas import tpu as pltpu
from jax.sharding import PartitionSpec as P

SHARDS = 4
QUARTERS = 4
GROUPS = ("own+near", "mid", "far")
SPLIT = ("c mid", "c near",)
DIRECT = ()
ORDER = {
    "z far": ("y own",),
    "expert own+near": ("c far",),
    "expert far": ("rc mid",),
    "rz far": ("c far",),
    "rz mid": ("rc far",),
    "c far": ("z near",),
    "y far": ("z near",),
    "ry mid": ("y near",),
}
VMEM_BYTES = 16 * 1024 * 1024
LOAD_VMEM_BYTES = 40 * 1024 * 1024


def zero_one(condition):
    return jnp.where(condition, 1.0, 0.0).astype(jnp.bfloat16)


def after(array, *others):
    return lax.optimization_barrier((array, *others))[0]


def exact_dot(left, right):
    return jnp.dot(left, right, preferred_element_type=jnp.float32)


def spread(table_ref, pick, plane, rows, shape, axis):
    place = lax.broadcasted_iota(jnp.int32, shape, axis) % rows
    out = jnp.zeros(shape, jnp.int32)
    for row in range(rows):
        out = jnp.where(place == row, table_ref[pick, row] ^ plane, out)
    return out


def pack_kernel(capacity, planes, route_hbm, tok_hbm, scale_hbm, *rest):
    outs = rest[:planes]
    quarters_ref, tok_ref, scale_ref, route_ref, sems = rest[planes:]
    sources, targets = (route_hbm, scale_hbm, tok_hbm), (route_ref, scale_ref, tok_ref)
    copies = [
        pltpu.make_async_copy(source, target, sems.at[index])
        for index, (source, target) in enumerate(zip(sources, targets))
    ]
    for copy in copies:
        copy.start()
    rows, features = tok_ref.shape
    picks, width = route_ref.shape[0], features // QUARTERS
    copies[0].wait()
    plane = lax.axis_index("expert") // SHARDS
    columns = QUARTERS * rows
    numbers = lax.broadcasted_iota(jnp.int32, (planes, columns), 0)
    named = jnp.zeros((planes, columns), jnp.float32)
    for pick in range(picks):
        turned = spread(route_ref, pick, plane, rows, (1, columns), 1)
        named = named + jnp.where(turned == numbers, 1.0, 0.0)
    first = lax.broadcasted_iota(jnp.int32, (columns, columns), 0)
    second = lax.broadcasted_iota(jnp.int32, (columns, columns), 1)
    before = zero_one((first // rows == second // rows) & (first < second))
    position = exact_dot(named.astype(jnp.bfloat16), before)
    tall = QUARTERS * capacity
    slot_row = lax.broadcasted_iota(jnp.int32, (tall, columns), 0)
    slot_col = lax.broadcasted_iota(jnp.int32, (tall, columns), 1)
    same_quarter = slot_row // capacity == slot_col // rows
    slot = (slot_row % capacity).astype(jnp.float32)
    pick_out = [
        zero_one(
            same_quarter
            & (named[offset : offset + 1, :] > 0.5)
            & (position[offset : offset + 1, :] == slot)
        )
        for offset in range(planes)
    ]
    copies[1].wait()
    copies[2].wait()
    for block in range(features // 128):
        quarter, at = divmod(block * 128, width)
        codes = tok_ref[:, block * 128 : (block + 1) * 128].astype(jnp.float32)
        factors = scale_ref[:, block : block + 1]
        quarters_ref[quarter * rows : (quarter + 1) * rows, at : at + 128] = (
            codes * factors
        ).astype(jnp.bfloat16)
    moved = exact_dot(jnp.concatenate(pick_out, axis=0), quarters_ref[...])
    for offset in range(planes):
        outs[offset][...] = moved[offset * tall : (offset + 1) * tall, :].astype(jnp.bfloat16)


def order_matrix(capacity, turned):
    size = SHARDS * QUARTERS * capacity
    row = lax.broadcasted_iota(jnp.int32, (size, size), 1 if turned else 0)
    col = lax.broadcasted_iota(jnp.int32, (size, size), 0 if turned else 1)
    quarter, block, slot = row // (SHARDS * capacity), (row // capacity) % SHARDS, row % capacity
    return zero_one(col == (block * QUARTERS + quarter) * capacity + slot)


def load_kernel(gate_hbm, up_hbm, down_hbm, unused, gate_ref, up_ref, down_ref, sems):
    copies = [
        pltpu.make_async_copy(source, target, sems.at[index])
        for index, (source, target) in enumerate(
            ((gate_hbm, gate_ref), (up_hbm, up_ref), (down_hbm, down_ref))
        )
    ]
    for copy in copies:
        copy.start()
    for copy in copies:
        copy.wait()


def expert_kernel(capacity, offsets, *refs):
    count = 2 * offsets
    blocks = refs[:count]
    gate_ref, up_ref, down_ref, kept_ref, sent_ref, rows_ref, part_ref = refs[count:]
    group, tall = SHARDS * capacity, QUARTERS * capacity
    width = blocks[0].shape[1]
    spans = [slice(quarter * width, (quarter + 1) * width) for quarter in range(QUARTERS)]
    order = order_matrix(capacity, False)
    for offset in range(offsets):
        held = jnp.concatenate(
            [blocks[2 * offset][...], blocks[2 * offset + 1][...]], axis=0
        )
        sorted_rows = exact_dot(order, held).astype(jnp.bfloat16)
        for quarter in range(QUARTERS):
            rows_ref[quarter, offset * group : (offset + 1) * group, :] = sorted_rows[
                quarter * group : (quarter + 1) * group, :
            ]
    gate = jnp.zeros((offsets * group, gate_ref.shape[2]), jnp.float32)
    upward = jnp.zeros((offsets * group, gate_ref.shape[2]), jnp.float32)
    for quarter, span in enumerate(spans):
        gate = gate + exact_dot(rows_ref[quarter], gate_ref[0, span, :])
        upward = upward + exact_dot(rows_ref[quarter], up_ref[0, span, :])
    hidden = (gate / (1.0 + jnp.exp(-gate)) * upward).astype(jnp.bfloat16)
    for quarter, span in enumerate(spans):
        part_ref[quarter] = exact_dot(hidden, down_ref[0, :, span]).astype(jnp.bfloat16)
    back = order_matrix(capacity, True)
    for offset in range(offsets):
        held = jnp.concatenate(
            [
                part_ref[quarter, offset * group : (offset + 1) * group, :]
                for quarter in range(QUARTERS)
            ],
            axis=0,
        )
        answer = exact_dot(back, held).astype(jnp.bfloat16)
        for member in range(SHARDS):
            out_ref = sent_ref if member >= 2 else kept_ref
            at = (member % 2 * offsets + offset) * tall
            out_ref[at : at + tall, :] = answer[member * tall : (member + 1) * tall, :]


def plan_kernel(capacity, planes, rows, route_hbm, code_hbm, unused, plan_ref, *scratch):
    route_ref, code_ref, sems = scratch
    copies = [
        pltpu.make_async_copy(route_hbm, route_ref, sems.at[0]),
        pltpu.make_async_copy(code_hbm, code_ref, sems.at[1]),
    ]
    for copy in copies:
        copy.start()
    for copy in copies:
        copy.wait()
    picks = route_ref.shape[0]
    tall = QUARTERS * rows
    plane = lax.axis_index("expert") // SHARDS
    numbers = lax.broadcasted_iota(jnp.int32, (tall, planes), 1)
    named = jnp.zeros((tall, planes), jnp.float32)
    coarse = jnp.zeros((tall, planes), jnp.float32)
    fine = jnp.zeros((tall, planes), jnp.float32)
    for pick in range(picks):
        here = spread(route_ref, pick, plane, rows, (tall, 1), 0) == numbers
        codes = spread(code_ref, pick, 0, rows, (tall, 1), 0)
        named = named + jnp.where(here, 1.0, 0.0)
        coarse = coarse + jnp.where(here, (codes // 256).astype(jnp.float32) / 256.0, 0.0)
        fine = fine + jnp.where(here, (codes % 256).astype(jnp.float32) / 65536.0, 0.0)
    first = lax.broadcasted_iota(jnp.int32, (tall, tall), 0)
    second = lax.broadcasted_iota(jnp.int32, (tall, tall), 1)
    before = zero_one((first // rows == second // rows) & (second < first))
    position = exact_dot(before, named.astype(jnp.bfloat16))
    slot_row = lax.broadcasted_iota(jnp.int32, (tall, QUARTERS * capacity), 0)
    slot_col = lax.broadcasted_iota(jnp.int32, (tall, QUARTERS * capacity), 1)
    same_quarter = slot_row // rows == slot_col // capacity
    slot = (slot_col % capacity).astype(jnp.float32)
    for offset in range(planes):
        column = slice(offset, offset + 1)
        take = same_quarter & (named[:, column] > 0.5) & (position[:, column] == slot)
        for half, factor in enumerate((coarse, fine)):
            plan_ref[offset, half * tall : (half + 1) * tall, :] = jnp.where(
                take, factor[:, column], 0.0
            ).astype(jnp.bfloat16)


def mix_kernel(planes, plan_ref, *refs):
    returned, out_ref = refs[:planes], refs[planes]
    rows, features = out_ref.shape
    width, tall = features // QUARTERS, QUARTERS * rows
    total = jnp.zeros((2 * tall, width), jnp.float32)
    for at in range(0, planes, 4):
        some = range(at, min(at + 4, planes))
        plan = jnp.concatenate([plan_ref[offset] for offset in some], axis=1)
        answers = jnp.concatenate([returned[offset][...] for offset in some], axis=0)
        total = total + exact_dot(plan, answers)
    total = (total[:tall] + total[tall:]).astype(jnp.bfloat16)
    for quarter in range(QUARTERS):
        out_ref[:, quarter * width : (quarter + 1) * width] = total[
            quarter * rows : (quarter + 1) * rows, :
        ]


def shards(tokens, scales, routes, gate_codes, w_gate, w_up, w_down):
    tok_rows, features = tokens.shape
    picks_per = routes.shape[1]
    devices = lax.axis_size("expert")
    planes = devices // SHARDS
    capacity = 3 * tok_rows * picks_per // (2 * planes)
    width = features // QUARTERS
    tall = QUARTERS * capacity
    vmem = pl.BlockSpec(memory_space=pltpu.VMEM)
    hbm = pl.BlockSpec(memory_space=pl.ANY)
    params = pltpu.CompilerParams(vmem_limit_bytes=VMEM_BYTES)
    load_params = pltpu.CompilerParams(vmem_limit_bytes=LOAD_VMEM_BYTES)

    def in_hbm(array):
        return pltpu.with_memory_space_constraint(array, pltpu.HBM)

    def partner(array, distance):
        return lax.ppermute(array, "expert", [(i, i ^ distance) for i in range(devices)])

    block = jax.ShapeDtypeStruct((tall, width), jnp.bfloat16)
    packed = pl.pallas_call(
        functools.partial(pack_kernel, capacity, planes),
        out_shape=[block] * planes,
        in_specs=[hbm] * 3,
        out_specs=[vmem] * planes,
        scratch_shapes=[
            pltpu.VMEM((QUARTERS * tok_rows, width), jnp.bfloat16),
            pltpu.VMEM(tokens.shape, tokens.dtype),
            pltpu.VMEM(scales.shape, scales.dtype),
            pltpu.SMEM(routes.T.shape, routes.dtype),
            pltpu.SemaphoreType.DMA((3,)),
        ],
        compiler_params=params,
    )(in_hbm(routes.T), in_hbm(tokens), in_hbm(scales))
    plan = pl.pallas_call(
        functools.partial(plan_kernel, capacity, planes, tok_rows),
        out_shape=jax.ShapeDtypeStruct((planes, 2 * QUARTERS * tok_rows, tall), jnp.bfloat16),
        in_specs=[hbm] * 3,
        out_specs=vmem,
        scratch_shapes=[pltpu.SMEM(routes.T.shape, routes.dtype)] * 2
        + [pltpu.SemaphoreType.DMA((2,))],
        compiler_params=params,
    )(in_hbm(routes.T), in_hbm(gate_codes.T), packed[0])

    def expert(offsets, held, weights):
        rows = offsets * SHARDS * capacity
        half = jax.ShapeDtypeStruct((2 * offsets * tall, width), jnp.bfloat16)
        return pl.pallas_call(
            functools.partial(expert_kernel, capacity, offsets),
            out_shape=[half] * 2,
            in_specs=[vmem] * (offsets * 2 + 3),
            out_specs=[vmem] * 2,
            scratch_shapes=[pltpu.VMEM((QUARTERS, rows, width), jnp.bfloat16)] * 2,
            compiler_params=params,
            cost_estimate=pl.CostEstimate(
                flops=6 * rows * features * w_gate.shape[2],
                bytes_accessed=0,
                transcendentals=0,
            ),
        )(*held, *weights)

    def load(gate):
        return pl.pallas_call(
            load_kernel,
            out_shape=[jax.ShapeDtypeStruct(w.shape, w.dtype) for w in (w_gate, w_up, w_down)],
            in_specs=[hbm] * 4,
            out_specs=[vmem] * 3,
            scratch_shapes=[pltpu.SemaphoreType.DMA((3,))],
            compiler_params=load_params,
        )(in_hbm(w_gate), in_hbm(w_up), in_hbm(w_down), gate)

    def fold(kept, arrived, offsets):
        middle = offsets * tall
        kept, arrived = kept.astype(jnp.float32), arrived.astype(jnp.float32)
        leaving = (kept[middle:] + arrived[middle:]).astype(jnp.bfloat16)
        return leaving, kept[:middle] + arrived[:middle]

    half, late = planes // 2, 3 * planes // 4
    places = {
        "own": range(1),
        "near": range(1, half),
        "mid": range(half, late),
        "far": range(late, planes),
    }
    for group in GROUPS:
        places[group] = [at for member in group.split("+") for at in places[member]]
    results = {}

    def result(step):
        if step not in results:
            results[step] = build(*step.split())
        return results[step]

    def build(kind, name):
        if kind == "pack":
            return [packed[at] for at in places[name]]
        if kind == "z":
            inputs = result("pack " + name)
        elif kind == "y":
            inputs = result(("pack " if name == "own" or name in DIRECT else "z ") + name)
        elif kind == "c":
            own = result(("pack " if name == "own" else "z ") + name)
            inputs = [jnp.concatenate(both, axis=0) for both in zip(own, result("y " + name))]
        elif kind == "expert":
            inputs = []
            for member in name.split("+"):
                own = result(("pack " if member == "own" else "z ") + member)
                both = [jnp.concatenate(two, axis=0) for two in zip(own, result("y " + member))]
                for two in zip(both, result("c " + member)):
                    inputs += two
        elif kind == "rc":
            inputs = result("expert " + name)[1:]
        elif kind == "sum":
            kept, arrived = result("expert " + name)[0], result("rc " + name)[0]
            return fold(kept, arrived, len(places[name]))
        elif kind == "ry":
            inputs = result("sum " + name)[:1]
        elif kind == "answer":
            total = result("sum " + name)[1] + result("ry " + name)[0].astype(jnp.float32)
            total = total.astype(jnp.bfloat16)
            return [total[at * tall : (at + 1) * tall] for at in range(len(places[name]))]
        elif kind == "load":
            inputs = packed[:1]
        elif kind == "rz":
            inputs = [a for a, at in zip(result("answer " + name), places[name]) if at]
        earlier = [result(step)[-1] for step in ORDER.get(kind + " " + name, ())]
        if earlier:
            inputs = [after(inputs[0], *earlier)] + list(inputs[1:])
        if kind == "load":
            return load(inputs[0])
        if kind == "expert":
            return expert(len(places[name]), inputs, result("load all"))
        if kind == "y" and name in DIRECT:
            return [partner(array, at * SHARDS + 2) for array, at in zip(inputs, places[name])]
        if kind in ("y", "ry"):
            return [partner(array, 2) for array in inputs]
        if kind in ("c", "rc"):
            if kind + " " + name not in SPLIT:
                return [partner(array, 1) for array in inputs]
            halves = [jnp.split(array, 2, axis=0) for array in inputs]
            if kind == "c":
                own = result(("pack " if name == "own" else "z ") + name)
                halves = [(one, two[1]) for one, two in zip(own, halves)]
            halves = [[partner(half, 1) for half in pair] for pair in halves]
            return [jnp.concatenate(pair, axis=0) for pair in halves]
        where = [at for at in places[name] if at]
        return [partner(array, at * SHARDS) for array, at in zip(inputs, where)]

    returned = {}
    for group in GROUPS:
        pieces = list(result("answer " + group))
        if group != "own":
            pieces[-len(result("rz " + group)) :] = result("rz " + group)
        returned.update(zip(places[group], pieces))
    returned = [returned[at] for at in range(planes)]

    return pl.pallas_call(
        functools.partial(mix_kernel, planes),
        out_shape=jax.ShapeDtypeStruct((tok_rows, features), jnp.bfloat16),
        in_specs=[vmem] * (planes + 1),
        out_specs=vmem,
        compiler_params=params,
    )(plan, *returned)


def solution(mesh):
    in_specs = (
        P(("groups", "expert"), None),
        P(("groups", "expert"), None),
        P(("groups", "expert"), None),
        P(("groups", "expert"), None),
        P("expert", None, None),
        P("expert", None, None),
        P("expert", None, None),
    )
    out_specs = P(("groups", "expert"), None)
    return jax.shard_map(shards, mesh=mesh, in_specs=in_specs, out_specs=out_specs, check_vma=False)
```

```python
import functools

import jax
import jax.numpy as jnp
from jax import lax
from jax.experimental import pallas as pl
from jax.experimental.pallas import tpu as pltpu
from jax.sharding import PartitionSpec as P

SHARDS = 4
QUARTERS = 4
GROUPS = ("own+near", "mid", "far")
SPLIT = ("c mid", "c near", "rc mid",)
DIRECT = ()
ORDER = {
    "z far": ("y own",),
    "expert own+near": ("y own",),
    "expert far": ("rc mid",),
    "c own": ("c near",),
    "rz mid": ("rc far", "z near",),
    "c far": ("z near", "expert mid",),
    "ry own+near": ("y near",),
    "y far": ("z near",),
}
VMEM_BYTES = 16 * 1024 * 1024
LOAD_VMEM_BYTES = 40 * 1024 * 1024


def zero_one(condition):
    return jnp.where(condition, 1.0, 0.0).astype(jnp.bfloat16)


def after(array, *others):
    return lax.optimization_barrier((array, *others))[0]


def exact_dot(left, right):
    return jnp.dot(left, right, preferred_element_type=jnp.float32)


def spread(table_ref, pick, plane, rows, shape, axis):
    place = lax.broadcasted_iota(jnp.int32, shape, axis) % rows
    out = jnp.zeros(shape, jnp.int32)
    for row in range(rows):
        out = jnp.where(place == row, table_ref[pick, row] ^ plane, out)
    return out


def pack_kernel(capacity, planes, route_hbm, tok_hbm, scale_hbm, *rest):
    outs = rest[:planes]
    quarters_ref, tok_ref, scale_ref, route_ref, sems = rest[planes:]
    sources, targets = (route_hbm, scale_hbm, tok_hbm), (route_ref, scale_ref, tok_ref)
    copies = [
        pltpu.make_async_copy(source, target, sems.at[index])
        for index, (source, target) in enumerate(zip(sources, targets))
    ]
    for copy in copies:
        copy.start()
    rows, features = tok_ref.shape
    picks, width = route_ref.shape[0], features // QUARTERS
    copies[0].wait()
    plane = lax.axis_index("expert") // SHARDS
    columns = QUARTERS * rows
    numbers = lax.broadcasted_iota(jnp.int32, (planes, columns), 0)
    named = jnp.zeros((planes, columns), jnp.float32)
    for pick in range(picks):
        turned = spread(route_ref, pick, plane, rows, (1, columns), 1)
        named = named + jnp.where(turned == numbers, 1.0, 0.0)
    first = lax.broadcasted_iota(jnp.int32, (columns, columns), 0)
    second = lax.broadcasted_iota(jnp.int32, (columns, columns), 1)
    before = zero_one((first // rows == second // rows) & (first < second))
    position = exact_dot(named.astype(jnp.bfloat16), before)
    tall = QUARTERS * capacity
    slot_row = lax.broadcasted_iota(jnp.int32, (tall, columns), 0)
    slot_col = lax.broadcasted_iota(jnp.int32, (tall, columns), 1)
    same_quarter = slot_row // capacity == slot_col // rows
    slot = (slot_row % capacity).astype(jnp.float32)
    pick_out = [
        zero_one(
            same_quarter
            & (named[offset : offset + 1, :] > 0.5)
            & (position[offset : offset + 1, :] == slot)
        )
        for offset in range(planes)
    ]
    copies[1].wait()
    copies[2].wait()
    for block in range(features // 128):
        quarter, at = divmod(block * 128, width)
        codes = tok_ref[:, block * 128 : (block + 1) * 128].astype(jnp.float32)
        factors = scale_ref[:, block : block + 1]
        quarters_ref[quarter * rows : (quarter + 1) * rows, at : at + 128] = (
            codes * factors
        ).astype(jnp.bfloat16)
    moved = exact_dot(jnp.concatenate(pick_out, axis=0), quarters_ref[...])
    for offset in range(planes):
        outs[offset][...] = moved[offset * tall : (offset + 1) * tall, :].astype(jnp.bfloat16)


def order_matrix(capacity):
    size = SHARDS * QUARTERS * capacity
    row = lax.broadcasted_iota(jnp.int32, (size, size), 1)
    col = lax.broadcasted_iota(jnp.int32, (size, size), 0)
    quarter, block, slot = row // (SHARDS * capacity), (row // capacity) % SHARDS, row % capacity
    return zero_one(col == (block * QUARTERS + quarter) * capacity + slot)


def load_kernel(gate_hbm, up_hbm, down_hbm, unused, gate_ref, up_ref, down_ref, sems):
    copies = [
        pltpu.make_async_copy(source, target, sems.at[index])
        for index, (source, target) in enumerate(
            ((gate_hbm, gate_ref), (up_hbm, up_ref), (down_hbm, down_ref))
        )
    ]
    for copy in copies:
        copy.start()
    for copy in copies:
        copy.wait()


def expert_kernel(capacity, offsets, *refs):
    count = 2 * offsets
    blocks = refs[:count]
    gate_ref, up_ref, down_ref, kept_ref, sent_ref, rows_ref, part_ref = refs[count:]
    group, tall = SHARDS * capacity, QUARTERS * capacity
    width = blocks[0].shape[1]
    spans = [slice(quarter * width, (quarter + 1) * width) for quarter in range(QUARTERS)]
    for index, block in enumerate(blocks):
        rows_ref[index * 2 * tall : (index + 1) * 2 * tall, :] = block[...]

    def project(weight_ref):
        total = jnp.zeros((offsets * group, weight_ref.shape[2]), jnp.float32)
        for quarter, span in enumerate(spans):
            every = exact_dot(rows_ref[...], weight_ref[0, span, :])
            starts = [
                member * tall + quarter * capacity for member in range(offsets * SHARDS)
            ]
            total = total + jnp.concatenate(
                [every[start : start + capacity, :] for start in starts], axis=0
            )
        return total

    gate, upward = project(gate_ref), project(up_ref)
    hidden = (gate / (1.0 + jnp.exp(-gate)) * upward).astype(jnp.bfloat16)
    for quarter, span in enumerate(spans):
        part_ref[quarter] = exact_dot(hidden, down_ref[0, :, span]).astype(jnp.bfloat16)
    back = order_matrix(capacity)
    for offset in range(offsets):
        held = jnp.concatenate(
            [
                part_ref[quarter, offset * group : (offset + 1) * group, :]
                for quarter in range(QUARTERS)
            ],
            axis=0,
        )
        answer = exact_dot(back, held).astype(jnp.bfloat16)
        for member in range(SHARDS):
            out_ref = sent_ref if member >= 2 else kept_ref
            at = (member % 2 * offsets + offset) * tall
            out_ref[at : at + tall, :] = answer[member * tall : (member + 1) * tall, :]


def plan_kernel(capacity, planes, rows, route_hbm, code_hbm, unused, plan_ref, *scratch):
    route_ref, code_ref, sems = scratch
    copies = [
        pltpu.make_async_copy(route_hbm, route_ref, sems.at[0]),
        pltpu.make_async_copy(code_hbm, code_ref, sems.at[1]),
    ]
    for copy in copies:
        copy.start()
    for copy in copies:
        copy.wait()
    picks = route_ref.shape[0]
    tall = QUARTERS * rows
    plane = lax.axis_index("expert") // SHARDS
    numbers = lax.broadcasted_iota(jnp.int32, (tall, planes), 1)
    named = jnp.zeros((tall, planes), jnp.float32)
    coarse = jnp.zeros((tall, planes), jnp.float32)
    fine = jnp.zeros((tall, planes), jnp.float32)
    for pick in range(picks):
        here = spread(route_ref, pick, plane, rows, (tall, 1), 0) == numbers
        codes = spread(code_ref, pick, 0, rows, (tall, 1), 0)
        named = named + jnp.where(here, 1.0, 0.0)
        coarse = coarse + jnp.where(here, (codes // 256).astype(jnp.float32) / 256.0, 0.0)
        fine = fine + jnp.where(here, (codes % 256).astype(jnp.float32) / 65536.0, 0.0)
    first = lax.broadcasted_iota(jnp.int32, (tall, tall), 0)
    second = lax.broadcasted_iota(jnp.int32, (tall, tall), 1)
    before = zero_one((first // rows == second // rows) & (second < first))
    position = exact_dot(before, named.astype(jnp.bfloat16))
    slot_row = lax.broadcasted_iota(jnp.int32, (tall, QUARTERS * capacity), 0)
    slot_col = lax.broadcasted_iota(jnp.int32, (tall, QUARTERS * capacity), 1)
    same_quarter = slot_row // rows == slot_col // capacity
    slot = (slot_col % capacity).astype(jnp.float32)
    for offset in range(planes):
        column = slice(offset, offset + 1)
        take = same_quarter & (named[:, column] > 0.5) & (position[:, column] == slot)
        for half, factor in enumerate((coarse, fine)):
            plan_ref[offset, half * tall : (half + 1) * tall, :] = jnp.where(
                take, factor[:, column], 0.0
            ).astype(jnp.bfloat16)


def mix_kernel(planes, plan_ref, *refs):
    returned, out_ref = refs[:planes], refs[planes]
    rows, features = out_ref.shape
    width, tall = features // QUARTERS, QUARTERS * rows
    total = jnp.zeros((2 * tall, width), jnp.float32)
    for at in range(0, planes, 4):
        some = range(at, min(at + 4, planes))
        plan = jnp.concatenate([plan_ref[offset] for offset in some], axis=1)
        answers = jnp.concatenate([returned[offset][...] for offset in some], axis=0)
        total = total + exact_dot(plan, answers)
    total = (total[:tall] + total[tall:]).astype(jnp.bfloat16)
    for quarter in range(QUARTERS):
        out_ref[:, quarter * width : (quarter + 1) * width] = total[
            quarter * rows : (quarter + 1) * rows, :
        ]


def shards(tokens, scales, routes, gate_codes, w_gate, w_up, w_down):
    tok_rows, features = tokens.shape
    picks_per = routes.shape[1]
    devices = lax.axis_size("expert")
    planes = devices // SHARDS
    capacity = 3 * tok_rows * picks_per // (2 * planes)
    width = features // QUARTERS
    tall = QUARTERS * capacity
    vmem = pl.BlockSpec(memory_space=pltpu.VMEM)
    hbm = pl.BlockSpec(memory_space=pl.ANY)
    params = pltpu.CompilerParams(vmem_limit_bytes=VMEM_BYTES)
    load_params = pltpu.CompilerParams(vmem_limit_bytes=LOAD_VMEM_BYTES)

    def in_hbm(array):
        return pltpu.with_memory_space_constraint(array, pltpu.HBM)

    def partner(array, distance):
        return lax.ppermute(array, "expert", [(i, i ^ distance) for i in range(devices)])

    block = jax.ShapeDtypeStruct((tall, width), jnp.bfloat16)
    packed = pl.pallas_call(
        functools.partial(pack_kernel, capacity, planes),
        out_shape=[block] * planes,
        in_specs=[hbm] * 3,
        out_specs=[vmem] * planes,
        scratch_shapes=[
            pltpu.VMEM((QUARTERS * tok_rows, width), jnp.bfloat16),
            pltpu.VMEM(tokens.shape, tokens.dtype),
            pltpu.VMEM(scales.shape, scales.dtype),
            pltpu.SMEM(routes.T.shape, routes.dtype),
            pltpu.SemaphoreType.DMA((3,)),
        ],
        compiler_params=params,
    )(in_hbm(routes.T), in_hbm(tokens), in_hbm(scales))
    plan = pl.pallas_call(
        functools.partial(plan_kernel, capacity, planes, tok_rows),
        out_shape=jax.ShapeDtypeStruct((planes, 2 * QUARTERS * tok_rows, tall), jnp.bfloat16),
        in_specs=[hbm] * 3,
        out_specs=vmem,
        scratch_shapes=[pltpu.SMEM(routes.T.shape, routes.dtype)] * 2
        + [pltpu.SemaphoreType.DMA((2,))],
        compiler_params=params,
    )(in_hbm(routes.T), in_hbm(gate_codes.T), packed[0])

    def expert(offsets, held, weights):
        rows = offsets * SHARDS * capacity
        half = jax.ShapeDtypeStruct((2 * offsets * tall, width), jnp.bfloat16)
        return pl.pallas_call(
            functools.partial(expert_kernel, capacity, offsets),
            out_shape=[half] * 2,
            in_specs=[vmem] * (offsets * 2 + 3),
            out_specs=[vmem] * 2,
            scratch_shapes=[
                pltpu.VMEM((QUARTERS * rows, width), jnp.bfloat16),
                pltpu.VMEM((QUARTERS, rows, width), jnp.bfloat16),
            ],
            compiler_params=params,
            cost_estimate=pl.CostEstimate(
                flops=6 * rows * features * w_gate.shape[2],
                bytes_accessed=0,
                transcendentals=0,
            ),
        )(*held, *weights)

    def load(gate):
        return pl.pallas_call(
            load_kernel,
            out_shape=[jax.ShapeDtypeStruct(w.shape, w.dtype) for w in (w_gate, w_up, w_down)],
            in_specs=[hbm] * 4,
            out_specs=[vmem] * 3,
            scratch_shapes=[pltpu.SemaphoreType.DMA((3,))],
            compiler_params=load_params,
        )(in_hbm(w_gate), in_hbm(w_up), in_hbm(w_down), gate)

    def fold(kept, arrived, offsets):
        middle = offsets * tall
        kept, arrived = kept.astype(jnp.float32), arrived.astype(jnp.float32)
        leaving = (kept[middle:] + arrived[middle:]).astype(jnp.bfloat16)
        return leaving, kept[:middle] + arrived[:middle]

    half, late = planes // 2, 3 * planes // 4
    places = {
        "own": range(1),
        "near": range(1, half),
        "mid": range(half, late),
        "far": range(late, planes),
    }
    for group in GROUPS:
        places[group] = [at for member in group.split("+") for at in places[member]]
    results = {}

    def result(step):
        if step not in results:
            results[step] = build(*step.split())
        return results[step]

    def build(kind, name):
        if kind == "pack":
            return [packed[at] for at in places[name]]
        if kind == "z":
            inputs = result("pack " + name)
        elif kind == "y":
            inputs = result(("pack " if name == "own" or name in DIRECT else "z ") + name)
        elif kind == "c":
            own = result(("pack " if name == "own" else "z ") + name)
            inputs = [jnp.concatenate(both, axis=0) for both in zip(own, result("y " + name))]
        elif kind == "expert":
            inputs = []
            for member in name.split("+"):
                own = result(("pack " if member == "own" else "z ") + member)
                both = [jnp.concatenate(two, axis=0) for two in zip(own, result("y " + member))]
                for two in zip(both, result("c " + member)):
                    inputs += two
        elif kind == "rc":
            inputs = result("expert " + name)[1:]
        elif kind == "sum":
            kept, arrived = result("expert " + name)[0], result("rc " + name)[0]
            return fold(kept, arrived, len(places[name]))
        elif kind == "ry":
            inputs = result("sum " + name)[:1]
        elif kind == "answer":
            total = result("sum " + name)[1] + result("ry " + name)[0].astype(jnp.float32)
            total = total.astype(jnp.bfloat16)
            return [total[at * tall : (at + 1) * tall] for at in range(len(places[name]))]
        elif kind == "load":
            inputs = packed[:1]
        elif kind == "rz":
            inputs = [a for a, at in zip(result("answer " + name), places[name]) if at]
        earlier = [result(step)[-1] for step in ORDER.get(kind + " " + name, ())]
        if earlier:
            inputs = [after(inputs[0], *earlier)] + list(inputs[1:])
        if kind == "load":
            return load(inputs[0])
        if kind == "expert":
            return expert(len(places[name]), inputs, result("load all"))
        if kind == "y" and name in DIRECT:
            return [partner(array, at * SHARDS + 2) for array, at in zip(inputs, places[name])]
        if kind in ("y", "ry"):
            return [partner(array, 2) for array in inputs]
        if kind in ("c", "rc"):
            if kind + " " + name not in SPLIT:
                return [partner(array, 1) for array in inputs]
            halves = [jnp.split(array, 2, axis=0) for array in inputs]
            if kind == "c":
                own = result(("pack " if name == "own" else "z ") + name)
                halves = [(one, two[1]) for one, two in zip(own, halves)]
            halves = [[partner(half, 1) for half in pair] for pair in halves]
            return [jnp.concatenate(pair, axis=0) for pair in halves]
        where = [at for at in places[name] if at]
        return [partner(array, at * SHARDS) for array, at in zip(inputs, where)]

    returned = {}
    for group in GROUPS:
        pieces = list(result("answer " + group))
        if group != "own":
            pieces[-len(result("rz " + group)) :] = result("rz " + group)
        returned.update(zip(places[group], pieces))
    returned = [returned[at] for at in range(planes)]

    return pl.pallas_call(
        functools.partial(mix_kernel, planes),
        out_shape=jax.ShapeDtypeStruct((tok_rows, features), jnp.bfloat16),
        in_specs=[vmem] * (planes + 1),
        out_specs=vmem,
        compiler_params=params,
    )(plan, *returned)


def solution(mesh):
    in_specs = (
        P(("groups", "expert"), None),
        P(("groups", "expert"), None),
        P(("groups", "expert"), None),
        P(("groups", "expert"), None),
        P("expert", None, None),
        P("expert", None, None),
        P("expert", None, None),
    )
    out_specs = P(("groups", "expert"), None)
    return jax.shard_map(shards, mesh=mesh, in_specs=in_specs, out_specs=out_specs, check_vma=False)
```

```python
import functools

import jax
import jax.numpy as jnp
from jax import lax
from jax.experimental import pallas as pl
from jax.experimental.pallas import tpu as pltpu
from jax.sharding import PartitionSpec as P

SHARDS = 4
QUARTERS = 4
GROUPS = ("own", "near", "mid", "far")
SPLIT = ("c mid",)
DIRECT = ()
ORDER = {
    "z mid": ("z near",),
    "y far": ("z far",),
    "expert far": ("z near",),
    "rc far": ("load all",),
    "expert near": ("c mid",),
    "c mid": ("rc far",),
    "rc near": ("z far",),
    "expert mid": ("expert near",),
    "ry near": ("c far", "y near", "z far",),
    "rc mid": ("expert near", "z mid",),
    "c own": ("rc near", "z mid", "rc mid",),
    "rz far": ("rc far", "ry far", "expert mid",),
    "ry mid": ("load all",),
    "rz near": ("rc own", "y far", "y own",),
    "rc own": ("c mid",),
}
VMEM_BYTES = 16 * 1024 * 1024
LOAD_VMEM_BYTES = 40 * 1024 * 1024


def zero_one(condition):
    return jnp.where(condition, 1.0, 0.0).astype(jnp.bfloat16)


def after(array, *others):
    return lax.optimization_barrier((array, *others))[0]


def exact_dot(left, right):
    return jnp.dot(left, right, preferred_element_type=jnp.float32)


def spread(table_ref, pick, plane, rows, shape, axis):
    place = lax.broadcasted_iota(jnp.int32, shape, axis) % rows
    out = jnp.zeros(shape, jnp.int32)
    for row in range(rows):
        out = jnp.where(place == row, table_ref[pick, row] ^ plane, out)
    return out


def pack_kernel(capacity, planes, route_hbm, tok_hbm, scale_hbm, *rest):
    outs = rest[:planes]
    quarters_ref, tok_ref, scale_ref, route_ref, sems = rest[planes:]
    sources, targets = (route_hbm, scale_hbm, tok_hbm), (route_ref, scale_ref, tok_ref)
    copies = [
        pltpu.make_async_copy(source, target, sems.at[index])
        for index, (source, target) in enumerate(zip(sources, targets))
    ]
    for copy in copies:
        copy.start()
    rows, features = tok_ref.shape
    picks, width = route_ref.shape[0], features // QUARTERS
    for copy in copies:
        copy.wait()
    plane = lax.axis_index("expert") // SHARDS
    columns = QUARTERS * rows
    numbers = lax.broadcasted_iota(jnp.int32, (planes, columns), 0)
    named = jnp.zeros((planes, columns), jnp.float32)
    for pick in range(picks):
        turned = spread(route_ref, pick, plane, rows, (1, columns), 1)
        named = named + jnp.where(turned == numbers, 1.0, 0.0)
    first = lax.broadcasted_iota(jnp.int32, (columns, columns), 0)
    second = lax.broadcasted_iota(jnp.int32, (columns, columns), 1)
    before = zero_one((first // rows == second // rows) & (first < second))
    position = exact_dot(named.astype(jnp.bfloat16), before)
    tall = QUARTERS * capacity
    slot_row = lax.broadcasted_iota(jnp.int32, (tall, columns), 0)
    slot_col = lax.broadcasted_iota(jnp.int32, (tall, columns), 1)
    same_quarter = slot_row // capacity == slot_col // rows
    slot = (slot_row % capacity).astype(jnp.float32)
    pick_out = [
        zero_one(
            same_quarter
            & (named[offset : offset + 1, :] > 0.5)
            & (position[offset : offset + 1, :] == slot)
        )
        for offset in range(planes)
    ]
    for block in range(features // 128):
        quarter, at = divmod(block * 128, width)
        codes = tok_ref[:, block * 128 : (block + 1) * 128].astype(jnp.float32)
        factors = scale_ref[:, block : block + 1]
        quarters_ref[quarter * rows : (quarter + 1) * rows, at : at + 128] = (
            codes * factors
        ).astype(jnp.bfloat16)
    moved = exact_dot(jnp.concatenate(pick_out, axis=0), quarters_ref[...])
    for offset in range(planes):
        outs[offset][...] = moved[offset * tall : (offset + 1) * tall, :].astype(jnp.bfloat16)


def order_matrix(capacity, turned):
    size = SHARDS * QUARTERS * capacity
    row = lax.broadcasted_iota(jnp.int32, (size, size), 1 if turned else 0)
    col = lax.broadcasted_iota(jnp.int32, (size, size), 0 if turned else 1)
    quarter, block, slot = row // (SHARDS * capacity), (row // capacity) % SHARDS, row % capacity
    return zero_one(col == (block * QUARTERS + quarter) * capacity + slot)


def load_kernel(gate_hbm, up_hbm, down_hbm, unused, gate_ref, up_ref, down_ref, sems):
    copies = [
        pltpu.make_async_copy(source, target, sems.at[index])
        for index, (source, target) in enumerate(
            ((gate_hbm, gate_ref), (up_hbm, up_ref), (down_hbm, down_ref))
        )
    ]
    for copy in copies:
        copy.start()
    for copy in copies:
        copy.wait()


def expert_kernel(capacity, offsets, *refs):
    count = 2 * offsets
    blocks = refs[:count]
    gate_ref, up_ref, down_ref, kept_ref, sent_ref, rows_ref, part_ref = refs[count:]
    group, tall = SHARDS * capacity, QUARTERS * capacity
    width = blocks[0].shape[1]
    spans = [slice(quarter * width, (quarter + 1) * width) for quarter in range(QUARTERS)]
    order = order_matrix(capacity, False)
    for offset in range(offsets):
        held = jnp.concatenate(
            [blocks[2 * offset][...], blocks[2 * offset + 1][...]], axis=0
        )
        sorted_rows = exact_dot(order, held).astype(jnp.bfloat16)
        for quarter in range(QUARTERS):
            rows_ref[quarter, offset * group : (offset + 1) * group, :] = sorted_rows[
                quarter * group : (quarter + 1) * group, :
            ]
    gate = jnp.zeros((offsets * group, gate_ref.shape[2]), jnp.float32)
    upward = jnp.zeros((offsets * group, gate_ref.shape[2]), jnp.float32)
    for quarter, span in enumerate(spans):
        gate = gate + exact_dot(rows_ref[quarter], gate_ref[0, span, :])
        upward = upward + exact_dot(rows_ref[quarter], up_ref[0, span, :])
    hidden = (gate / (1.0 + jnp.exp(-gate)) * upward).astype(jnp.bfloat16)
    for quarter, span in enumerate(spans):
        part_ref[quarter] = exact_dot(hidden, down_ref[0, :, span]).astype(jnp.bfloat16)
    back = order_matrix(capacity, True)
    for offset in range(offsets):
        held = jnp.concatenate(
            [
                part_ref[quarter, offset * group : (offset + 1) * group, :]
                for quarter in range(QUARTERS)
            ],
            axis=0,
        )
        answer = exact_dot(back, held).astype(jnp.bfloat16)
        for member in range(SHARDS):
            out_ref = sent_ref if member >= 2 else kept_ref
            at = (member % 2 * offsets + offset) * tall
            out_ref[at : at + tall, :] = answer[member * tall : (member + 1) * tall, :]


def plan_kernel(capacity, planes, rows, route_hbm, code_hbm, unused, plan_ref, *scratch):
    route_ref, code_ref, sems = scratch
    copies = [
        pltpu.make_async_copy(route_hbm, route_ref, sems.at[0]),
        pltpu.make_async_copy(code_hbm, code_ref, sems.at[1]),
    ]
    for copy in copies:
        copy.start()
    for copy in copies:
        copy.wait()
    picks = route_ref.shape[0]
    tall = QUARTERS * rows
    plane = lax.axis_index("expert") // SHARDS
    numbers = lax.broadcasted_iota(jnp.int32, (tall, planes), 1)
    named = jnp.zeros((tall, planes), jnp.float32)
    coarse = jnp.zeros((tall, planes), jnp.float32)
    fine = jnp.zeros((tall, planes), jnp.float32)
    for pick in range(picks):
        here = spread(route_ref, pick, plane, rows, (tall, 1), 0) == numbers
        codes = spread(code_ref, pick, 0, rows, (tall, 1), 0)
        named = named + jnp.where(here, 1.0, 0.0)
        coarse = coarse + jnp.where(here, (codes // 256).astype(jnp.float32) / 256.0, 0.0)
        fine = fine + jnp.where(here, (codes % 256).astype(jnp.float32) / 65536.0, 0.0)
    first = lax.broadcasted_iota(jnp.int32, (tall, tall), 0)
    second = lax.broadcasted_iota(jnp.int32, (tall, tall), 1)
    before = zero_one((first // rows == second // rows) & (second < first))
    position = exact_dot(before, named.astype(jnp.bfloat16))
    slot_row = lax.broadcasted_iota(jnp.int32, (tall, QUARTERS * capacity), 0)
    slot_col = lax.broadcasted_iota(jnp.int32, (tall, QUARTERS * capacity), 1)
    same_quarter = slot_row // rows == slot_col // capacity
    slot = (slot_col % capacity).astype(jnp.float32)
    for offset in range(planes):
        column = slice(offset, offset + 1)
        take = same_quarter & (named[:, column] > 0.5) & (position[:, column] == slot)
        for half, factor in enumerate((coarse, fine)):
            plan_ref[offset, half * tall : (half + 1) * tall, :] = jnp.where(
                take, factor[:, column], 0.0
            ).astype(jnp.bfloat16)


def mix_kernel(planes, plan_ref, *refs):
    returned, out_ref = refs[:planes], refs[planes]
    rows, features = out_ref.shape
    width, tall = features // QUARTERS, QUARTERS * rows
    total = jnp.zeros((2 * tall, width), jnp.float32)
    for at in range(0, planes, 4):
        some = range(at, min(at + 4, planes))
        plan = jnp.concatenate([plan_ref[offset] for offset in some], axis=1)
        answers = jnp.concatenate([returned[offset][...] for offset in some], axis=0)
        total = total + exact_dot(plan, answers)
    total = (total[:tall] + total[tall:]).astype(jnp.bfloat16)
    for quarter in range(QUARTERS):
        out_ref[:, quarter * width : (quarter + 1) * width] = total[
            quarter * rows : (quarter + 1) * rows, :
        ]


def shards(tokens, scales, routes, gate_codes, w_gate, w_up, w_down):
    tok_rows, features = tokens.shape
    picks_per = routes.shape[1]
    devices = lax.axis_size("expert")
    planes = devices // SHARDS
    capacity = 3 * tok_rows * picks_per // (2 * planes)
    width = features // QUARTERS
    tall = QUARTERS * capacity
    vmem = pl.BlockSpec(memory_space=pltpu.VMEM)
    hbm = pl.BlockSpec(memory_space=pl.ANY)
    params = pltpu.CompilerParams(vmem_limit_bytes=VMEM_BYTES)
    load_params = pltpu.CompilerParams(vmem_limit_bytes=LOAD_VMEM_BYTES)

    def in_hbm(array):
        return pltpu.with_memory_space_constraint(array, pltpu.HBM)

    def partner(array, distance):
        return lax.ppermute(array, "expert", [(i, i ^ distance) for i in range(devices)])

    block = jax.ShapeDtypeStruct((tall, width), jnp.bfloat16)
    packed = pl.pallas_call(
        functools.partial(pack_kernel, capacity, planes),
        out_shape=[block] * planes,
        in_specs=[hbm] * 3,
        out_specs=[vmem] * planes,
        scratch_shapes=[
            pltpu.VMEM((QUARTERS * tok_rows, width), jnp.bfloat16),
            pltpu.VMEM(tokens.shape, tokens.dtype),
            pltpu.VMEM(scales.shape, scales.dtype),
            pltpu.SMEM(routes.T.shape, routes.dtype),
            pltpu.SemaphoreType.DMA((3,)),
        ],
        compiler_params=params,
    )(in_hbm(routes.T), in_hbm(tokens), in_hbm(scales))
    plan = pl.pallas_call(
        functools.partial(plan_kernel, capacity, planes, tok_rows),
        out_shape=jax.ShapeDtypeStruct((planes, 2 * QUARTERS * tok_rows, tall), jnp.bfloat16),
        in_specs=[hbm] * 3,
        out_specs=vmem,
        scratch_shapes=[pltpu.SMEM(routes.T.shape, routes.dtype)] * 2
        + [pltpu.SemaphoreType.DMA((2,))],
        compiler_params=params,
    )(in_hbm(routes.T), in_hbm(gate_codes.T), packed[0])

    def expert(offsets, held, weights):
        rows = offsets * SHARDS * capacity
        half = jax.ShapeDtypeStruct((2 * offsets * tall, width), jnp.bfloat16)
        return pl.pallas_call(
            functools.partial(expert_kernel, capacity, offsets),
            out_shape=[half] * 2,
            in_specs=[vmem] * (offsets * 2 + 3),
            out_specs=[vmem] * 2,
            scratch_shapes=[pltpu.VMEM((QUARTERS, rows, width), jnp.bfloat16)] * 2,
            compiler_params=params,
            cost_estimate=pl.CostEstimate(
                flops=6 * rows * features * w_gate.shape[2],
                bytes_accessed=0,
                transcendentals=0,
            ),
        )(*held, *weights)

    def load(gate):
        return pl.pallas_call(
            load_kernel,
            out_shape=[jax.ShapeDtypeStruct(w.shape, w.dtype) for w in (w_gate, w_up, w_down)],
            in_specs=[hbm] * 4,
            out_specs=[vmem] * 3,
            scratch_shapes=[pltpu.SemaphoreType.DMA((3,))],
            compiler_params=load_params,
        )(in_hbm(w_gate), in_hbm(w_up), in_hbm(w_down), gate)

    def fold(kept, arrived, offsets):
        middle = offsets * tall
        kept, arrived = kept.astype(jnp.float32), arrived.astype(jnp.float32)
        leaving = (kept[middle:] + arrived[middle:]).astype(jnp.bfloat16)
        return leaving, kept[:middle] + arrived[:middle]

    half, late = planes // 2, 3 * planes // 4
    places = {
        "own": range(1),
        "near": range(1, half),
        "mid": range(half, late),
        "far": range(late, planes),
    }
    for group in GROUPS:
        places[group] = [at for member in group.split("+") for at in places[member]]
    results = {}

    def result(step):
        if step not in results:
            results[step] = build(*step.split())
        return results[step]

    def build(kind, name):
        if kind == "pack":
            return [packed[at] for at in places[name]]
        if kind == "z":
            inputs = result("pack " + name)
        elif kind == "y":
            inputs = result(("pack " if name == "own" or name in DIRECT else "z ") + name)
        elif kind == "c":
            own = result(("pack " if name == "own" else "z ") + name)
            inputs = [jnp.concatenate(both, axis=0) for both in zip(own, result("y " + name))]
        elif kind == "expert":
            inputs = []
            for member in name.split("+"):
                own = result(("pack " if member == "own" else "z ") + member)
                both = [jnp.concatenate(two, axis=0) for two in zip(own, result("y " + member))]
                for two in zip(both, result("c " + member)):
                    inputs += two
        elif kind == "rc":
            inputs = result("expert " + name)[1:]
        elif kind == "sum":
            kept, arrived = result("expert " + name)[0], result("rc " + name)[0]
            return fold(kept, arrived, len(places[name]))
        elif kind == "ry":
            inputs = result("sum " + name)[:1]
        elif kind == "answer":
            total = result("sum " + name)[1] + result("ry " + name)[0].astype(jnp.float32)
            total = total.astype(jnp.bfloat16)
            return [total[at * tall : (at + 1) * tall] for at in range(len(places[name]))]
        elif kind == "load":
            inputs = packed[:1]
        elif kind == "rz":
            inputs = [a for a, at in zip(result("answer " + name), places[name]) if at]
        earlier = [result(step)[-1] for step in ORDER.get(kind + " " + name, ())]
        if earlier:
            inputs = [after(inputs[0], *earlier)] + list(inputs[1:])
        if kind == "load":
            return load(inputs[0])
        if kind == "expert":
            return expert(len(places[name]), inputs, result("load all"))
        if kind == "y" and name in DIRECT:
            return [partner(array, at * SHARDS + 2) for array, at in zip(inputs, places[name])]
        if kind in ("y", "ry"):
            return [partner(array, 2) for array in inputs]
        if kind in ("c", "rc"):
            if kind + " " + name not in SPLIT:
                return [partner(array, 1) for array in inputs]
            halves = [jnp.split(array, 2, axis=0) for array in inputs]
            if kind == "c":
                own = result(("pack " if name == "own" else "z ") + name)
                halves = [(one, two[1]) for one, two in zip(own, halves)]
            halves = [[partner(half, 1) for half in pair] for pair in halves]
            return [jnp.concatenate(pair, axis=0) for pair in halves]
        where = [at for at in places[name] if at]
        return [partner(array, at * SHARDS) for array, at in zip(inputs, where)]

    returned = {}
    for group in GROUPS:
        pieces = list(result("answer " + group))
        if group != "own":
            pieces[-len(result("rz " + group)) :] = result("rz " + group)
        returned.update(zip(places[group], pieces))
    returned = [returned[at] for at in range(planes)]

    return pl.pallas_call(
        functools.partial(mix_kernel, planes),
        out_shape=jax.ShapeDtypeStruct((tok_rows, features), jnp.bfloat16),
        in_specs=[vmem] * (planes + 1),
        out_specs=vmem,
        compiler_params=params,
    )(plan, *returned)


def solution(mesh):
    in_specs = (
        P(("groups", "expert"), None),
        P(("groups", "expert"), None),
        P(("groups", "expert"), None),
        P(("groups", "expert"), None),
        P("expert", None, None),
        P("expert", None, None),
        P("expert", None, None),
    )
    out_specs = P(("groups", "expert"), None)
    return jax.shard_map(shards, mesh=mesh, in_specs=in_specs, out_specs=out_specs, check_vma=False)
```

```python
import functools

import jax
import jax.numpy as jnp
from jax import lax
from jax.experimental import pallas as pl
from jax.experimental.pallas import tpu as pltpu
from jax.sharding import PartitionSpec as P

SHARDS = 4
QUARTERS = 4
GROUPS = ("own+near", "mid", "far")
SPLIT = ("c mid", "c near",)
DIRECT = ()
ORDER = {
    "z far": ("y own",),
    "expert own+near": ("y own",),
    "expert far": ("rc mid",),
    "c own": ("c near",),
    "rz mid": ("rc far", "z near",),
    "c far": ("z near", "expert mid",),
    "ry own+near": ("y near",),
    "y far": ("z near",),
}
VMEM_BYTES = 16 * 1024 * 1024
LOAD_VMEM_BYTES = 40 * 1024 * 1024


def zero_one(condition):
    return jnp.where(condition, 1.0, 0.0).astype(jnp.bfloat16)


def after(array, *others):
    return lax.optimization_barrier((array, *others))[0]


def exact_dot(left, right):
    return jnp.dot(left, right, preferred_element_type=jnp.float32)


def spread(table_ref, pick, plane, rows, shape, axis):
    place = lax.broadcasted_iota(jnp.int32, shape, axis) % rows
    out = jnp.zeros(shape, jnp.int32)
    for row in range(rows):
        out = jnp.where(place == row, table_ref[pick, row] ^ plane, out)
    return out


def pack_kernel(capacity, planes, route_hbm, tok_hbm, scale_hbm, *rest):
    outs = rest[:planes]
    quarters_ref, tok_ref, scale_ref, route_ref, sems = rest[planes:]
    sources, targets = (route_hbm, scale_hbm, tok_hbm), (route_ref, scale_ref, tok_ref)
    copies = [
        pltpu.make_async_copy(source, target, sems.at[index])
        for index, (source, target) in enumerate(zip(sources, targets))
    ]
    for copy in copies:
        copy.start()
    rows, features = tok_ref.shape
    picks, width = route_ref.shape[0], features // QUARTERS
    copies[0].wait()
    plane = lax.axis_index("expert") // SHARDS
    columns = QUARTERS * rows
    numbers = lax.broadcasted_iota(jnp.int32, (planes, columns), 0)
    named = jnp.zeros((planes, columns), jnp.float32)
    for pick in range(picks):
        turned = spread(route_ref, pick, plane, rows, (1, columns), 1)
        named = named + jnp.where(turned == numbers, 1.0, 0.0)
    first = lax.broadcasted_iota(jnp.int32, (columns, columns), 0)
    second = lax.broadcasted_iota(jnp.int32, (columns, columns), 1)
    before = zero_one((first // rows == second // rows) & (first < second))
    position = exact_dot(named.astype(jnp.bfloat16), before)
    tall = QUARTERS * capacity
    slot_row = lax.broadcasted_iota(jnp.int32, (tall, columns), 0)
    slot_col = lax.broadcasted_iota(jnp.int32, (tall, columns), 1)
    same_quarter = slot_row // capacity == slot_col // rows
    slot = (slot_row % capacity).astype(jnp.float32)
    pick_out = [
        zero_one(
            same_quarter
            & (named[offset : offset + 1, :] > 0.5)
            & (position[offset : offset + 1, :] == slot)
        )
        for offset in range(planes)
    ]
    copies[1].wait()
    copies[2].wait()
    for block in range(features // 128):
        quarter, at = divmod(block * 128, width)
        codes = tok_ref[:, block * 128 : (block + 1) * 128].astype(jnp.float32)
        factors = scale_ref[:, block : block + 1]
        quarters_ref[quarter * rows : (quarter + 1) * rows, at : at + 128] = (
            codes * factors
        ).astype(jnp.bfloat16)
    moved = exact_dot(jnp.concatenate(pick_out, axis=0), quarters_ref[...])
    for offset in range(planes):
        outs[offset][...] = moved[offset * tall : (offset + 1) * tall, :].astype(jnp.bfloat16)


def order_matrix(capacity, turned):
    size = SHARDS * QUARTERS * capacity
    row = lax.broadcasted_iota(jnp.int32, (size, size), 1 if turned else 0)
    col = lax.broadcasted_iota(jnp.int32, (size, size), 0 if turned else 1)
    quarter, block, slot = row // (SHARDS * capacity), (row // capacity) % SHARDS, row % capacity
    return zero_one(col == (block * QUARTERS + quarter) * capacity + slot)


def load_kernel(gate_hbm, up_hbm, down_hbm, unused, gate_ref, up_ref, down_ref, sems):
    copies = [
        pltpu.make_async_copy(source, target, sems.at[index])
        for index, (source, target) in enumerate(
            ((gate_hbm, gate_ref), (up_hbm, up_ref), (down_hbm, down_ref))
        )
    ]
    for copy in copies:
        copy.start()
    for copy in copies:
        copy.wait()


def expert_kernel(capacity, offsets, *refs):
    count = 2 * offsets
    blocks = refs[:count]
    gate_ref, up_ref, down_ref, kept_ref, sent_ref, rows_ref, part_ref = refs[count:]
    group, tall = SHARDS * capacity, QUARTERS * capacity
    width = blocks[0].shape[1]
    spans = [slice(quarter * width, (quarter + 1) * width) for quarter in range(QUARTERS)]
    order = order_matrix(capacity, False)
    for offset in range(offsets):
        held = jnp.concatenate(
            [blocks[2 * offset][...], blocks[2 * offset + 1][...]], axis=0
        )
        sorted_rows = exact_dot(order, held).astype(jnp.bfloat16)
        for quarter in range(QUARTERS):
            rows_ref[quarter, offset * group : (offset + 1) * group, :] = sorted_rows[
                quarter * group : (quarter + 1) * group, :
            ]
    gate = jnp.zeros((offsets * group, gate_ref.shape[2]), jnp.float32)
    upward = jnp.zeros((offsets * group, gate_ref.shape[2]), jnp.float32)
    for quarter, span in enumerate(spans):
        gate = gate + exact_dot(rows_ref[quarter], gate_ref[0, span, :])
        upward = upward + exact_dot(rows_ref[quarter], up_ref[0, span, :])
    hidden = (gate / (1.0 + jnp.exp(-gate)) * upward).astype(jnp.bfloat16)
    for quarter, span in enumerate(spans):
        part_ref[quarter] = exact_dot(hidden, down_ref[0, :, span]).astype(jnp.bfloat16)
    back = order_matrix(capacity, True)
    for offset in range(offsets):
        held = jnp.concatenate(
            [
                part_ref[quarter, offset * group : (offset + 1) * group, :]
                for quarter in range(QUARTERS)
            ],
            axis=0,
        )
        answer = exact_dot(back, held).astype(jnp.bfloat16)
        for member in range(SHARDS):
            out_ref = sent_ref if member >= 2 else kept_ref
            at = (member % 2 * offsets + offset) * tall
            out_ref[at : at + tall, :] = answer[member * tall : (member + 1) * tall, :]


def plan_kernel(capacity, planes, rows, route_hbm, code_hbm, unused, plan_ref, *scratch):
    route_ref, code_ref, sems = scratch
    copies = [
        pltpu.make_async_copy(route_hbm, route_ref, sems.at[0]),
        pltpu.make_async_copy(code_hbm, code_ref, sems.at[1]),
    ]
    for copy in copies:
        copy.start()
    for copy in copies:
        copy.wait()
    picks = route_ref.shape[0]
    tall = QUARTERS * rows
    plane = lax.axis_index("expert") // SHARDS
    numbers = lax.broadcasted_iota(jnp.int32, (tall, planes), 1)
    named = jnp.zeros((tall, planes), jnp.float32)
    coarse = jnp.zeros((tall, planes), jnp.float32)
    fine = jnp.zeros((tall, planes), jnp.float32)
    for pick in range(picks):
        here = spread(route_ref, pick, plane, rows, (tall, 1), 0) == numbers
        codes = spread(code_ref, pick, 0, rows, (tall, 1), 0)
        named = named + jnp.where(here, 1.0, 0.0)
        coarse = coarse + jnp.where(here, (codes // 256).astype(jnp.float32) / 256.0, 0.0)
        fine = fine + jnp.where(here, (codes % 256).astype(jnp.float32) / 65536.0, 0.0)
    first = lax.broadcasted_iota(jnp.int32, (tall, tall), 0)
    second = lax.broadcasted_iota(jnp.int32, (tall, tall), 1)
    before = zero_one((first // rows == second // rows) & (second < first))
    position = exact_dot(before, named.astype(jnp.bfloat16))
    slot_row = lax.broadcasted_iota(jnp.int32, (tall, QUARTERS * capacity), 0)
    slot_col = lax.broadcasted_iota(jnp.int32, (tall, QUARTERS * capacity), 1)
    same_quarter = slot_row // rows == slot_col // capacity
    slot = (slot_col % capacity).astype(jnp.float32)
    for offset in range(planes):
        column = slice(offset, offset + 1)
        take = same_quarter & (named[:, column] > 0.5) & (position[:, column] == slot)
        for half, factor in enumerate((coarse, fine)):
            plan_ref[offset, half * tall : (half + 1) * tall, :] = jnp.where(
                take, factor[:, column], 0.0
            ).astype(jnp.bfloat16)


def mix_kernel(planes, plan_ref, *refs):
    returned, out_ref = refs[:planes], refs[planes]
    rows, features = out_ref.shape
    width, tall = features // QUARTERS, QUARTERS * rows
    total = jnp.zeros((2 * tall, width), jnp.float32)
    for at in range(0, planes, 4):
        some = range(at, min(at + 4, planes))
        plan = jnp.concatenate([plan_ref[offset] for offset in some], axis=1)
        answers = jnp.concatenate([returned[offset][...] for offset in some], axis=0)
        total = total + exact_dot(plan, answers)
    total = (total[:tall] + total[tall:]).astype(jnp.bfloat16)
    for quarter in range(QUARTERS):
        out_ref[:, quarter * width : (quarter + 1) * width] = total[
            quarter * rows : (quarter + 1) * rows, :
        ]


def shards(tokens, scales, routes, gate_codes, w_gate, w_up, w_down):
    tok_rows, features = tokens.shape
    picks_per = routes.shape[1]
    devices = lax.axis_size("expert")
    planes = devices // SHARDS
    capacity = 3 * tok_rows * picks_per // (2 * planes)
    width = features // QUARTERS
    tall = QUARTERS * capacity
    vmem = pl.BlockSpec(memory_space=pltpu.VMEM)
    hbm = pl.BlockSpec(memory_space=pl.ANY)
    params = pltpu.CompilerParams(vmem_limit_bytes=VMEM_BYTES)
    load_params = pltpu.CompilerParams(vmem_limit_bytes=LOAD_VMEM_BYTES)

    def in_hbm(array):
        return pltpu.with_memory_space_constraint(array, pltpu.HBM)

    def partner(array, distance):
        return lax.ppermute(array, "expert", [(i, i ^ distance) for i in range(devices)])

    block = jax.ShapeDtypeStruct((tall, width), jnp.bfloat16)
    packed = pl.pallas_call(
        functools.partial(pack_kernel, capacity, planes),
        out_shape=[block] * planes,
        in_specs=[hbm] * 3,
        out_specs=[vmem] * planes,
        scratch_shapes=[
            pltpu.VMEM((QUARTERS * tok_rows, width), jnp.bfloat16),
            pltpu.VMEM(tokens.shape, tokens.dtype),
            pltpu.VMEM(scales.shape, scales.dtype),
            pltpu.SMEM(routes.T.shape, routes.dtype),
            pltpu.SemaphoreType.DMA((3,)),
        ],
        compiler_params=params,
    )(in_hbm(routes.T), in_hbm(tokens), in_hbm(scales))
    plan = pl.pallas_call(
        functools.partial(plan_kernel, capacity, planes, tok_rows),
        out_shape=jax.ShapeDtypeStruct((planes, 2 * QUARTERS * tok_rows, tall), jnp.bfloat16),
        in_specs=[hbm] * 3,
        out_specs=vmem,
        scratch_shapes=[pltpu.SMEM(routes.T.shape, routes.dtype)] * 2
        + [pltpu.SemaphoreType.DMA((2,))],
        compiler_params=params,
    )(in_hbm(routes.T), in_hbm(gate_codes.T), packed[0])

    def expert(offsets, held, weights):
        rows = offsets * SHARDS * capacity
        half = jax.ShapeDtypeStruct((2 * offsets * tall, width), jnp.bfloat16)
        return pl.pallas_call(
            functools.partial(expert_kernel, capacity, offsets),
            out_shape=[half] * 2,
            in_specs=[vmem] * (offsets * 2 + 3),
            out_specs=[vmem] * 2,
            scratch_shapes=[pltpu.VMEM((QUARTERS, rows, width), jnp.bfloat16)] * 2,
            compiler_params=params,
            cost_estimate=pl.CostEstimate(
                flops=6 * rows * features * w_gate.shape[2],
                bytes_accessed=0,
                transcendentals=0,
            ),
        )(*held, *weights)

    def load(gate):
        return pl.pallas_call(
            load_kernel,
            out_shape=[jax.ShapeDtypeStruct(w.shape, w.dtype) for w in (w_gate, w_up, w_down)],
            in_specs=[hbm] * 4,
            out_specs=[vmem] * 3,
            scratch_shapes=[pltpu.SemaphoreType.DMA((3,))],
            compiler_params=load_params,
        )(in_hbm(w_gate), in_hbm(w_up), in_hbm(w_down), gate)

    def fold(kept, arrived, offsets):
        middle = offsets * tall
        kept, arrived = kept.astype(jnp.float32), arrived.astype(jnp.float32)
        leaving = (kept[middle:] + arrived[middle:]).astype(jnp.bfloat16)
        return leaving, kept[:middle] + arrived[:middle]

    half, late = planes // 2, 3 * planes // 4
    places = {
        "own": range(1),
        "near": range(1, half),
        "mid": range(half, late),
        "far": range(late, planes),
    }
    for group in GROUPS:
        places[group] = [at for member in group.split("+") for at in places[member]]
    results = {}

    def result(step):
        if step not in results:
            results[step] = build(*step.split())
        return results[step]

    def build(kind, name):
        if kind == "pack":
            return [packed[at] for at in places[name]]
        if kind == "z":
            inputs = result("pack " + name)
        elif kind == "y":
            inputs = result(("pack " if name == "own" or name in DIRECT else "z ") + name)
        elif kind == "c":
            own = result(("pack " if name == "own" else "z ") + name)
            inputs = [jnp.concatenate(both, axis=0) for both in zip(own, result("y " + name))]
        elif kind == "expert":
            inputs = []
            for member in name.split("+"):
                own = result(("pack " if member == "own" else "z ") + member)
                both = [jnp.concatenate(two, axis=0) for two in zip(own, result("y " + member))]
                for two in zip(both, result("c " + member)):
                    inputs += two
        elif kind == "rc":
            inputs = result("expert " + name)[1:]
        elif kind == "sum":
            kept, arrived = result("expert " + name)[0], result("rc " + name)[0]
            return fold(kept, arrived, len(places[name]))
        elif kind == "ry":
            inputs = result("sum " + name)[:1]
        elif kind == "answer":
            total = result("sum " + name)[1] + result("ry " + name)[0].astype(jnp.float32)
            total = total.astype(jnp.bfloat16)
            return [total[at * tall : (at + 1) * tall] for at in range(len(places[name]))]
        elif kind == "load":
            inputs = packed[:1]
        elif kind == "rz":
            inputs = [a for a, at in zip(result("answer " + name), places[name]) if at]
        earlier = [result(step)[-1] for step in ORDER.get(kind + " " + name, ())]
        if earlier:
            inputs = [after(inputs[0], *earlier)] + list(inputs[1:])
        if kind == "load":
            return load(inputs[0])
        if kind == "expert":
            return expert(len(places[name]), inputs, result("load all"))
        if kind == "y" and name in DIRECT:
            return [partner(array, at * SHARDS + 2) for array, at in zip(inputs, places[name])]
        if kind in ("y", "ry"):
            return [partner(array, 2) for array in inputs]
        if kind in ("c", "rc"):
            if kind + " " + name not in SPLIT:
                return [partner(array, 1) for array in inputs]
            halves = [jnp.split(array, 2, axis=0) for array in inputs]
            if kind == "c":
                own = result(("pack " if name == "own" else "z ") + name)
                halves = [(one, two[1]) for one, two in zip(own, halves)]
            halves = [[partner(half, 1) for half in pair] for pair in halves]
            return [jnp.concatenate(pair, axis=0) for pair in halves]
        where = [at for at in places[name] if at]
        return [partner(array, at * SHARDS) for array, at in zip(inputs, where)]

    returned = {}
    for group in GROUPS:
        pieces = list(result("answer " + group))
        if group != "own":
            pieces[-len(result("rz " + group)) :] = result("rz " + group)
        returned.update(zip(places[group], pieces))
    returned = [returned[at] for at in range(planes)]

    return pl.pallas_call(
        functools.partial(mix_kernel, planes),
        out_shape=jax.ShapeDtypeStruct((tok_rows, features), jnp.bfloat16),
        in_specs=[vmem] * (planes + 1),
        out_specs=vmem,
        compiler_params=params,
    )(plan, *returned)


def solution(mesh):
    in_specs = (
        P(("groups", "expert"), None),
        P(("groups", "expert"), None),
        P(("groups", "expert"), None),
        P(("groups", "expert"), None),
        P("expert", None, None),
        P("expert", None, None),
        P("expert", None, None),
    )
    out_specs = P(("groups", "expert"), None)
    return jax.shard_map(shards, mesh=mesh, in_specs=in_specs, out_specs=out_specs, check_vma=False)
```

```python
import functools

import jax
import jax.numpy as jnp
from jax import lax
from jax.experimental import pallas as pl
from jax.experimental.pallas import tpu as pltpu
from jax.sharding import PartitionSpec as P

SHARDS = 4
QUARTERS = 4
GROUPS = ("own+near", "mid", "far")
SPLIT = ("c mid", "c near",)
DIRECT = ()
ORDER = {
    "z far": ("y own",),
    "expert far": ("rc mid", "c own",),
    "c own": ("c near",),
    "rz mid": ("rc far",),
    "c far": ("z near",),
    "ry own+near": ("y near",),
    "y far": ("z near",),
}
VMEM_BYTES = 16 * 1024 * 1024
LOAD_VMEM_BYTES = 40 * 1024 * 1024


def zero_one(condition):
    return jnp.where(condition, 1.0, 0.0).astype(jnp.bfloat16)


def after(array, *others):
    return lax.optimization_barrier((array, *others))[0]


def exact_dot(left, right):
    return jnp.dot(left, right, preferred_element_type=jnp.float32)


def spread(table_ref, pick, plane, rows, shape, axis):
    place = lax.broadcasted_iota(jnp.int32, shape, axis) % rows
    out = jnp.zeros(shape, jnp.int32)
    for row in range(rows):
        out = jnp.where(place == row, table_ref[pick, row] ^ plane, out)
    return out


def pack_kernel(capacity, planes, route_hbm, tok_hbm, scale_hbm, *rest):
    outs = rest[:planes]
    quarters_ref, tok_ref, scale_ref, route_ref, sems = rest[planes:]
    sources, targets = (route_hbm, scale_hbm, tok_hbm), (route_ref, scale_ref, tok_ref)
    copies = [
        pltpu.make_async_copy(source, target, sems.at[index])
        for index, (source, target) in enumerate(zip(sources, targets))
    ]
    for copy in copies:
        copy.start()
    rows, features = tok_ref.shape
    picks, width = route_ref.shape[0], features // QUARTERS
    copies[0].wait()
    plane = lax.axis_index("expert") // SHARDS
    columns = QUARTERS * rows
    numbers = lax.broadcasted_iota(jnp.int32, (planes, columns), 0)
    named = jnp.zeros((planes, columns), jnp.float32)
    for pick in range(picks):
        turned = spread(route_ref, pick, plane, rows, (1, columns), 1)
        named = named + jnp.where(turned == numbers, 1.0, 0.0)
    first = lax.broadcasted_iota(jnp.int32, (columns, columns), 0)
    second = lax.broadcasted_iota(jnp.int32, (columns, columns), 1)
    before = zero_one((first // rows == second // rows) & (first < second))
    position = exact_dot(named.astype(jnp.bfloat16), before)
    tall = QUARTERS * capacity
    slot_row = lax.broadcasted_iota(jnp.int32, (tall, columns), 0)
    slot_col = lax.broadcasted_iota(jnp.int32, (tall, columns), 1)
    same_quarter = slot_row // capacity == slot_col // rows
    slot = (slot_row % capacity).astype(jnp.float32)
    pick_out = [
        zero_one(
            same_quarter
            & (named[offset : offset + 1, :] > 0.5)
            & (position[offset : offset + 1, :] == slot)
        )
        for offset in range(planes)
    ]
    copies[1].wait()
    copies[2].wait()
    for block in range(features // 128):
        quarter, at = divmod(block * 128, width)
        codes = tok_ref[:, block * 128 : (block + 1) * 128].astype(jnp.float32)
        factors = scale_ref[:, block : block + 1]
        quarters_ref[quarter * rows : (quarter + 1) * rows, at : at + 128] = (
            codes * factors
        ).astype(jnp.bfloat16)
    moved = exact_dot(jnp.concatenate(pick_out, axis=0), quarters_ref[...])
    for offset in range(planes):
        outs[offset][...] = moved[offset * tall : (offset + 1) * tall, :].astype(jnp.bfloat16)


def order_matrix(capacity, turned):
    size = SHARDS * QUARTERS * capacity
    row = lax.broadcasted_iota(jnp.int32, (size, size), 1 if turned else 0)
    col = lax.broadcasted_iota(jnp.int32, (size, size), 0 if turned else 1)
    quarter, block, slot = row // (SHARDS * capacity), (row // capacity) % SHARDS, row % capacity
    return zero_one(col == (block * QUARTERS + quarter) * capacity + slot)


def load_kernel(gate_hbm, up_hbm, down_hbm, unused, gate_ref, up_ref, down_ref, sems):
    copies = [
        pltpu.make_async_copy(source, target, sems.at[index])
        for index, (source, target) in enumerate(
            ((gate_hbm, gate_ref), (up_hbm, up_ref), (down_hbm, down_ref))
        )
    ]
    for copy in copies:
        copy.start()
    for copy in copies:
        copy.wait()


def expert_kernel(capacity, offsets, *refs):
    count = 2 * offsets
    blocks = refs[:count]
    gate_ref, up_ref, down_ref, kept_ref, sent_ref, rows_ref, part_ref = refs[count:]
    group, tall = SHARDS * capacity, QUARTERS * capacity
    width = blocks[0].shape[1]
    spans = [slice(quarter * width, (quarter + 1) * width) for quarter in range(QUARTERS)]
    order = order_matrix(capacity, False)
    for offset in range(offsets):
        held = jnp.concatenate(
            [blocks[2 * offset][...], blocks[2 * offset + 1][...]], axis=0
        )
        sorted_rows = exact_dot(order, held).astype(jnp.bfloat16)
        for quarter in range(QUARTERS):
            rows_ref[quarter, offset * group : (offset + 1) * group, :] = sorted_rows[
                quarter * group : (quarter + 1) * group, :
            ]
    gate = jnp.zeros((offsets * group, gate_ref.shape[2]), jnp.float32)
    upward = jnp.zeros((offsets * group, gate_ref.shape[2]), jnp.float32)
    for quarter, span in enumerate(spans):
        gate = gate + exact_dot(rows_ref[quarter], gate_ref[0, span, :])
        upward = upward + exact_dot(rows_ref[quarter], up_ref[0, span, :])
    hidden = (gate / (1.0 + jnp.exp(-gate)) * upward).astype(jnp.bfloat16)
    for quarter, span in enumerate(spans):
        part_ref[quarter] = exact_dot(hidden, down_ref[0, :, span]).astype(jnp.bfloat16)
    back = order_matrix(capacity, True)
    for offset in range(offsets):
        held = jnp.concatenate(
            [
                part_ref[quarter, offset * group : (offset + 1) * group, :]
                for quarter in range(QUARTERS)
            ],
            axis=0,
        )
        answer = exact_dot(back, held).astype(jnp.bfloat16)
        for member in range(SHARDS):
            out_ref = sent_ref if member >= 2 else kept_ref
            at = (member % 2 * offsets + offset) * tall
            out_ref[at : at + tall, :] = answer[member * tall : (member + 1) * tall, :]


def plan_kernel(capacity, planes, rows, route_hbm, code_hbm, unused, plan_ref, *scratch):
    route_ref, code_ref, sems = scratch
    copies = [
        pltpu.make_async_copy(route_hbm, route_ref, sems.at[0]),
        pltpu.make_async_copy(code_hbm, code_ref, sems.at[1]),
    ]
    for copy in copies:
        copy.start()
    for copy in copies:
        copy.wait()
    picks = route_ref.shape[0]
    tall = QUARTERS * rows
    plane = lax.axis_index("expert") // SHARDS
    numbers = lax.broadcasted_iota(jnp.int32, (tall, planes), 1)
    named = jnp.zeros((tall, planes), jnp.float32)
    coarse = jnp.zeros((tall, planes), jnp.float32)
    fine = jnp.zeros((tall, planes), jnp.float32)
    for pick in range(picks):
        here = spread(route_ref, pick, plane, rows, (tall, 1), 0) == numbers
        codes = spread(code_ref, pick, 0, rows, (tall, 1), 0)
        named = named + jnp.where(here, 1.0, 0.0)
        coarse = coarse + jnp.where(here, (codes // 256).astype(jnp.float32) / 256.0, 0.0)
        fine = fine + jnp.where(here, (codes % 256).astype(jnp.float32) / 65536.0, 0.0)
    first = lax.broadcasted_iota(jnp.int32, (tall, tall), 0)
    second = lax.broadcasted_iota(jnp.int32, (tall, tall), 1)
    before = zero_one((first // rows == second // rows) & (second < first))
    position = exact_dot(before, named.astype(jnp.bfloat16))
    slot_row = lax.broadcasted_iota(jnp.int32, (tall, QUARTERS * capacity), 0)
    slot_col = lax.broadcasted_iota(jnp.int32, (tall, QUARTERS * capacity), 1)
    same_quarter = slot_row // rows == slot_col // capacity
    slot = (slot_col % capacity).astype(jnp.float32)
    for offset in range(planes):
        column = slice(offset, offset + 1)
        take = same_quarter & (named[:, column] > 0.5) & (position[:, column] == slot)
        for half, factor in enumerate((coarse, fine)):
            plan_ref[offset, half * tall : (half + 1) * tall, :] = jnp.where(
                take, factor[:, column], 0.0
            ).astype(jnp.bfloat16)


def mix_kernel(planes, plan_ref, *refs):
    returned, out_ref = refs[:planes], refs[planes]
    rows, features = out_ref.shape
    width, tall = features // QUARTERS, QUARTERS * rows
    total = jnp.zeros((2 * tall, width), jnp.float32)
    for at in range(0, planes, 4):
        some = range(at, min(at + 4, planes))
        plan = jnp.concatenate([plan_ref[offset] for offset in some], axis=1)
        answers = jnp.concatenate([returned[offset][...] for offset in some], axis=0)
        total = total + exact_dot(plan, answers)
    total = (total[:tall] + total[tall:]).astype(jnp.bfloat16)
    for quarter in range(QUARTERS):
        out_ref[:, quarter * width : (quarter + 1) * width] = total[
            quarter * rows : (quarter + 1) * rows, :
        ]


def shards(tokens, scales, routes, gate_codes, w_gate, w_up, w_down):
    tok_rows, features = tokens.shape
    picks_per = routes.shape[1]
    devices = lax.axis_size("expert")
    planes = devices // SHARDS
    capacity = 3 * tok_rows * picks_per // (2 * planes)
    width = features // QUARTERS
    tall = QUARTERS * capacity
    vmem = pl.BlockSpec(memory_space=pltpu.VMEM)
    hbm = pl.BlockSpec(memory_space=pl.ANY)
    params = pltpu.CompilerParams(vmem_limit_bytes=VMEM_BYTES)
    load_params = pltpu.CompilerParams(vmem_limit_bytes=LOAD_VMEM_BYTES)

    def in_hbm(array):
        return pltpu.with_memory_space_constraint(array, pltpu.HBM)

    def partner(array, distance):
        return lax.ppermute(array, "expert", [(i, i ^ distance) for i in range(devices)])

    block = jax.ShapeDtypeStruct((tall, width), jnp.bfloat16)
    packed = pl.pallas_call(
        functools.partial(pack_kernel, capacity, planes),
        out_shape=[block] * planes,
        in_specs=[hbm] * 3,
        out_specs=[vmem] * planes,
        scratch_shapes=[
            pltpu.VMEM((QUARTERS * tok_rows, width), jnp.bfloat16),
            pltpu.VMEM(tokens.shape, tokens.dtype),
            pltpu.VMEM(scales.shape, scales.dtype),
            pltpu.SMEM(routes.T.shape, routes.dtype),
            pltpu.SemaphoreType.DMA((3,)),
        ],
        compiler_params=params,
    )(in_hbm(routes.T), in_hbm(tokens), in_hbm(scales))
    plan = pl.pallas_call(
        functools.partial(plan_kernel, capacity, planes, tok_rows),
        out_shape=jax.ShapeDtypeStruct((planes, 2 * QUARTERS * tok_rows, tall), jnp.bfloat16),
        in_specs=[hbm] * 3,
        out_specs=vmem,
        scratch_shapes=[pltpu.SMEM(routes.T.shape, routes.dtype)] * 2
        + [pltpu.SemaphoreType.DMA((2,))],
        compiler_params=params,
    )(in_hbm(routes.T), in_hbm(gate_codes.T), packed[0])

    def expert(offsets, held, weights):
        rows = offsets * SHARDS * capacity
        half = jax.ShapeDtypeStruct((2 * offsets * tall, width), jnp.bfloat16)
        return pl.pallas_call(
            functools.partial(expert_kernel, capacity, offsets),
            out_shape=[half] * 2,
            in_specs=[vmem] * (offsets * 2 + 3),
            out_specs=[vmem] * 2,
            scratch_shapes=[pltpu.VMEM((QUARTERS, rows, width), jnp.bfloat16)] * 2,
            compiler_params=params,
            cost_estimate=pl.CostEstimate(
                flops=6 * rows * features * w_gate.shape[2],
                bytes_accessed=0,
                transcendentals=0,
            ),
        )(*held, *weights)

    def load(gate):
        return pl.pallas_call(
            load_kernel,
            out_shape=[jax.ShapeDtypeStruct(w.shape, w.dtype) for w in (w_gate, w_up, w_down)],
            in_specs=[hbm] * 4,
            out_specs=[vmem] * 3,
            scratch_shapes=[pltpu.SemaphoreType.DMA((3,))],
            compiler_params=load_params,
        )(in_hbm(w_gate), in_hbm(w_up), in_hbm(w_down), gate)

    def fold(kept, arrived, offsets):
        middle = offsets * tall
        kept, arrived = kept.astype(jnp.float32), arrived.astype(jnp.float32)
        leaving = (kept[middle:] + arrived[middle:]).astype(jnp.bfloat16)
        return leaving, kept[:middle] + arrived[:middle]

    half, late = planes // 2, 3 * planes // 4
    places = {
        "own": range(1),
        "near": range(1, half),
        "mid": range(half, late),
        "far": range(late, planes),
    }
    for group in GROUPS:
        places[group] = [at for member in group.split("+") for at in places[member]]
    results = {}

    def result(step):
        if step not in results:
            results[step] = build(*step.split())
        return results[step]

    def build(kind, name):
        if kind == "pack":
            return [packed[at] for at in places[name]]
        if kind == "z":
            inputs = result("pack " + name)
        elif kind == "y":
            inputs = result(("pack " if name == "own" or name in DIRECT else "z ") + name)
        elif kind == "c":
            own = result(("pack " if name == "own" else "z ") + name)
            inputs = [jnp.concatenate(both, axis=0) for both in zip(own, result("y " + name))]
        elif kind == "expert":
            inputs = []
            for member in name.split("+"):
                own = result(("pack " if member == "own" else "z ") + member)
                both = [jnp.concatenate(two, axis=0) for two in zip(own, result("y " + member))]
                for two in zip(both, result("c " + member)):
                    inputs += two
        elif kind == "rc":
            inputs = result("expert " + name)[1:]
        elif kind == "sum":
            kept, arrived = result("expert " + name)[0], result("rc " + name)[0]
            return fold(kept, arrived, len(places[name]))
        elif kind == "ry":
            inputs = result("sum " + name)[:1]
        elif kind == "answer":
            total = result("sum " + name)[1] + result("ry " + name)[0].astype(jnp.float32)
            total = total.astype(jnp.bfloat16)
            return [total[at * tall : (at + 1) * tall] for at in range(len(places[name]))]
        elif kind == "load":
            inputs = packed[:1]
        elif kind == "rz":
            inputs = [a for a, at in zip(result("answer " + name), places[name]) if at]
        earlier = [result(step)[-1] for step in ORDER.get(kind + " " + name, ())]
        if earlier:
            inputs = [after(inputs[0], *earlier)] + list(inputs[1:])
        if kind == "load":
            return load(inputs[0])
        if kind == "expert":
            return expert(len(places[name]), inputs, result("load all"))
        if kind == "y" and name in DIRECT:
            return [partner(array, at * SHARDS + 2) for array, at in zip(inputs, places[name])]
        if kind in ("y", "ry"):
            return [partner(array, 2) for array in inputs]
        if kind in ("c", "rc"):
            if kind + " " + name not in SPLIT:
                return [partner(array, 1) for array in inputs]
            halves = [jnp.split(array, 2, axis=0) for array in inputs]
            if kind == "c":
                own = result(("pack " if name == "own" else "z ") + name)
                halves = [(one, two[1]) for one, two in zip(own, halves)]
            halves = [[partner(half, 1) for half in pair] for pair in halves]
            return [jnp.concatenate(pair, axis=0) for pair in halves]
        where = [at for at in places[name] if at]
        return [partner(array, at * SHARDS) for array, at in zip(inputs, where)]

    returned = {}
    for group in GROUPS:
        pieces = list(result("answer " + group))
        if group != "own":
            pieces[-len(result("rz " + group)) :] = result("rz " + group)
        returned.update(zip(places[group], pieces))
    returned = [returned[at] for at in range(planes)]

    return pl.pallas_call(
        functools.partial(mix_kernel, planes),
        out_shape=jax.ShapeDtypeStruct((tok_rows, features), jnp.bfloat16),
        in_specs=[vmem] * (planes + 1),
        out_specs=vmem,
        compiler_params=params,
    )(plan, *returned)


def solution(mesh):
    in_specs = (
        P(("groups", "expert"), None),
        P(("groups", "expert"), None),
        P(("groups", "expert"), None),
        P(("groups", "expert"), None),
        P("expert", None, None),
        P("expert", None, None),
        P("expert", None, None),
    )
    out_specs = P(("groups", "expert"), None)
    return jax.shard_map(shards, mesh=mesh, in_specs=in_specs, out_specs=out_specs, check_vma=False)
```

```python
import functools

import jax
import jax.numpy as jnp
from jax import lax
from jax.experimental import pallas as pl
from jax.experimental.pallas import tpu as pltpu
from jax.sharding import PartitionSpec as P

SHARDS = 4
QUARTERS = 4
GROUPS = ("own+near", "mid", "far")
SPLIT = ("c mid", "c near",)
DIRECT = ()
APART = ("own+near",)
ORDER = {
    "z far": ("y own",),
    "expert own+near": ("y own",),
    "expert far": ("rc mid",),
    "c own": ("c near",),
    "rz mid": ("rc far", "z near",),
    "c far": ("z near", "expert mid",),
    "ry own+near": ("y near",),
    "y far": ("z near",),
}
VMEM_BYTES = 16 * 1024 * 1024
LOAD_VMEM_BYTES = 40 * 1024 * 1024


def zero_one(condition):
    return jnp.where(condition, 1.0, 0.0).astype(jnp.bfloat16)


def after(array, *others):
    return lax.optimization_barrier((array, *others))[0]


def exact_dot(left, right):
    return jnp.dot(left, right, preferred_element_type=jnp.float32)


def spread(table_ref, pick, plane, rows, shape, axis):
    place = lax.broadcasted_iota(jnp.int32, shape, axis) % rows
    out = jnp.zeros(shape, jnp.int32)
    for row in range(rows):
        out = jnp.where(place == row, table_ref[pick, row] ^ plane, out)
    return out


def pack_kernel(capacity, planes, route_hbm, tok_hbm, scale_hbm, *rest):
    outs = rest[:planes]
    quarters_ref, tok_ref, scale_ref, route_ref, sems = rest[planes:]
    sources, targets = (route_hbm, scale_hbm, tok_hbm), (route_ref, scale_ref, tok_ref)
    copies = [
        pltpu.make_async_copy(source, target, sems.at[index])
        for index, (source, target) in enumerate(zip(sources, targets))
    ]
    for copy in copies:
        copy.start()
    rows, features = tok_ref.shape
    picks, width = route_ref.shape[0], features // QUARTERS
    copies[0].wait()
    plane = lax.axis_index("expert") // SHARDS
    columns = QUARTERS * rows
    numbers = lax.broadcasted_iota(jnp.int32, (planes, columns), 0)
    named = jnp.zeros((planes, columns), jnp.float32)
    for pick in range(picks):
        turned = spread(route_ref, pick, plane, rows, (1, columns), 1)
        named = named + jnp.where(turned == numbers, 1.0, 0.0)
    first = lax.broadcasted_iota(jnp.int32, (columns, columns), 0)
    second = lax.broadcasted_iota(jnp.int32, (columns, columns), 1)
    before = zero_one((first // rows == second // rows) & (first < second))
    position = exact_dot(named.astype(jnp.bfloat16), before)
    tall = QUARTERS * capacity
    slot_row = lax.broadcasted_iota(jnp.int32, (tall, columns), 0)
    slot_col = lax.broadcasted_iota(jnp.int32, (tall, columns), 1)
    same_quarter = slot_row // capacity == slot_col // rows
    slot = (slot_row % capacity).astype(jnp.float32)
    pick_out = [
        zero_one(
            same_quarter
            & (named[offset : offset + 1, :] > 0.5)
            & (position[offset : offset + 1, :] == slot)
        )
        for offset in range(planes)
    ]
    copies[1].wait()
    copies[2].wait()
    for block in range(features // 128):
        quarter, at = divmod(block * 128, width)
        codes = tok_ref[:, block * 128 : (block + 1) * 128].astype(jnp.float32)
        factors = scale_ref[:, block : block + 1]
        quarters_ref[quarter * rows : (quarter + 1) * rows, at : at + 128] = (
            codes * factors
        ).astype(jnp.bfloat16)
    moved = exact_dot(jnp.concatenate(pick_out, axis=0), quarters_ref[...])
    for offset in range(planes):
        outs[offset][...] = moved[offset * tall : (offset + 1) * tall, :].astype(jnp.bfloat16)


def order_matrix(capacity, turned):
    size = SHARDS * QUARTERS * capacity
    row = lax.broadcasted_iota(jnp.int32, (size, size), 1 if turned else 0)
    col = lax.broadcasted_iota(jnp.int32, (size, size), 0 if turned else 1)
    quarter, block, slot = row // (SHARDS * capacity), (row // capacity) % SHARDS, row % capacity
    return zero_one(col == (block * QUARTERS + quarter) * capacity + slot)


def load_kernel(gate_hbm, up_hbm, down_hbm, unused, gate_ref, up_ref, down_ref, sems):
    copies = [
        pltpu.make_async_copy(source, target, sems.at[index])
        for index, (source, target) in enumerate(
            ((gate_hbm, gate_ref), (up_hbm, up_ref), (down_hbm, down_ref))
        )
    ]
    for copy in copies:
        copy.start()
    for copy in copies:
        copy.wait()


def expert_kernel(capacity, offsets, *refs):
    count = 2 * offsets
    blocks = refs[:count]
    gate_ref, up_ref, down_ref, kept_ref, sent_ref, rows_ref, part_ref = refs[count:]
    group, tall = SHARDS * capacity, QUARTERS * capacity
    width = blocks[0].shape[1]
    spans = [slice(quarter * width, (quarter + 1) * width) for quarter in range(QUARTERS)]
    order = order_matrix(capacity, False)
    for offset in range(offsets):
        held = jnp.concatenate(
            [blocks[2 * offset][...], blocks[2 * offset + 1][...]], axis=0
        )
        sorted_rows = exact_dot(order, held).astype(jnp.bfloat16)
        for quarter in range(QUARTERS):
            rows_ref[quarter, offset * group : (offset + 1) * group, :] = sorted_rows[
                quarter * group : (quarter + 1) * group, :
            ]
    gate = jnp.zeros((offsets * group, gate_ref.shape[2]), jnp.float32)
    upward = jnp.zeros((offsets * group, gate_ref.shape[2]), jnp.float32)
    for quarter, span in enumerate(spans):
        gate = gate + exact_dot(rows_ref[quarter], gate_ref[0, span, :])
        upward = upward + exact_dot(rows_ref[quarter], up_ref[0, span, :])
    hidden = (gate / (1.0 + jnp.exp(-gate)) * upward).astype(jnp.bfloat16)
    for quarter, span in enumerate(spans):
        part_ref[quarter] = exact_dot(hidden, down_ref[0, :, span]).astype(jnp.bfloat16)
    back = order_matrix(capacity, True)
    for offset in range(offsets):
        held = jnp.concatenate(
            [
                part_ref[quarter, offset * group : (offset + 1) * group, :]
                for quarter in range(QUARTERS)
            ],
            axis=0,
        )
        answer = exact_dot(back, held).astype(jnp.bfloat16)
        for member in range(SHARDS):
            out_ref = sent_ref if member >= 2 else kept_ref
            at = (member % 2 * offsets + offset) * tall
            out_ref[at : at + tall, :] = answer[member * tall : (member + 1) * tall, :]


def plan_kernel(capacity, planes, rows, route_hbm, code_hbm, unused, plan_ref, *scratch):
    route_ref, code_ref, sems = scratch
    copies = [
        pltpu.make_async_copy(route_hbm, route_ref, sems.at[0]),
        pltpu.make_async_copy(code_hbm, code_ref, sems.at[1]),
    ]
    for copy in copies:
        copy.start()
    for copy in copies:
        copy.wait()
    picks = route_ref.shape[0]
    tall = QUARTERS * rows
    plane = lax.axis_index("expert") // SHARDS
    numbers = lax.broadcasted_iota(jnp.int32, (tall, planes), 1)
    named = jnp.zeros((tall, planes), jnp.float32)
    coarse = jnp.zeros((tall, planes), jnp.float32)
    fine = jnp.zeros((tall, planes), jnp.float32)
    for pick in range(picks):
        here = spread(route_ref, pick, plane, rows, (tall, 1), 0) == numbers
        codes = spread(code_ref, pick, 0, rows, (tall, 1), 0)
        named = named + jnp.where(here, 1.0, 0.0)
        coarse = coarse + jnp.where(here, (codes // 256).astype(jnp.float32) / 256.0, 0.0)
        fine = fine + jnp.where(here, (codes % 256).astype(jnp.float32) / 65536.0, 0.0)
    first = lax.broadcasted_iota(jnp.int32, (tall, tall), 0)
    second = lax.broadcasted_iota(jnp.int32, (tall, tall), 1)
    before = zero_one((first // rows == second // rows) & (second < first))
    position = exact_dot(before, named.astype(jnp.bfloat16))
    slot_row = lax.broadcasted_iota(jnp.int32, (tall, QUARTERS * capacity), 0)
    slot_col = lax.broadcasted_iota(jnp.int32, (tall, QUARTERS * capacity), 1)
    same_quarter = slot_row // rows == slot_col // capacity
    slot = (slot_col % capacity).astype(jnp.float32)
    for offset in range(planes):
        column = slice(offset, offset + 1)
        take = same_quarter & (named[:, column] > 0.5) & (position[:, column] == slot)
        for half, factor in enumerate((coarse, fine)):
            plan_ref[offset, half * tall : (half + 1) * tall, :] = jnp.where(
                take, factor[:, column], 0.0
            ).astype(jnp.bfloat16)


def mix_kernel(planes, plan_ref, *refs):
    stay_ref, across_ref, *others, out_ref = refs
    own = (stay_ref[...] + across_ref[...].astype(jnp.float32)).astype(jnp.bfloat16)
    rows, features = out_ref.shape
    width, tall = features // QUARTERS, QUARTERS * rows
    total = jnp.zeros((2 * tall, width), jnp.float32)
    for at in range(0, planes, 4):
        some = range(at, min(at + 4, planes))
        plan = jnp.concatenate([plan_ref[offset] for offset in some], axis=1)
        answers = [others[offset - 1][...] if offset else own for offset in some]
        answers = jnp.concatenate(answers, axis=0)
        total = total + exact_dot(plan, answers)
    total = (total[:tall] + total[tall:]).astype(jnp.bfloat16)
    for quarter in range(QUARTERS):
        out_ref[:, quarter * width : (quarter + 1) * width] = total[
            quarter * rows : (quarter + 1) * rows, :
        ]


def shards(tokens, scales, routes, gate_codes, w_gate, w_up, w_down):
    tok_rows, features = tokens.shape
    picks_per = routes.shape[1]
    devices = lax.axis_size("expert")
    planes = devices // SHARDS
    capacity = 3 * tok_rows * picks_per // (2 * planes)
    width = features // QUARTERS
    tall = QUARTERS * capacity
    vmem = pl.BlockSpec(memory_space=pltpu.VMEM)
    hbm = pl.BlockSpec(memory_space=pl.ANY)
    params = pltpu.CompilerParams(vmem_limit_bytes=VMEM_BYTES)
    load_params = pltpu.CompilerParams(vmem_limit_bytes=LOAD_VMEM_BYTES)

    def in_hbm(array):
        return pltpu.with_memory_space_constraint(array, pltpu.HBM)

    def partner(array, distance):
        return lax.ppermute(array, "expert", [(i, i ^ distance) for i in range(devices)])

    block = jax.ShapeDtypeStruct((tall, width), jnp.bfloat16)
    packed = pl.pallas_call(
        functools.partial(pack_kernel, capacity, planes),
        out_shape=[block] * planes,
        in_specs=[hbm] * 3,
        out_specs=[vmem] * planes,
        scratch_shapes=[
            pltpu.VMEM((QUARTERS * tok_rows, width), jnp.bfloat16),
            pltpu.VMEM(tokens.shape, tokens.dtype),
            pltpu.VMEM(scales.shape, scales.dtype),
            pltpu.SMEM(routes.T.shape, routes.dtype),
            pltpu.SemaphoreType.DMA((3,)),
        ],
        compiler_params=params,
    )(in_hbm(routes.T), in_hbm(tokens), in_hbm(scales))
    plan = pl.pallas_call(
        functools.partial(plan_kernel, capacity, planes, tok_rows),
        out_shape=jax.ShapeDtypeStruct((planes, 2 * QUARTERS * tok_rows, tall), jnp.bfloat16),
        in_specs=[hbm] * 3,
        out_specs=vmem,
        scratch_shapes=[pltpu.SMEM(routes.T.shape, routes.dtype)] * 2
        + [pltpu.SemaphoreType.DMA((2,))],
        compiler_params=params,
    )(in_hbm(routes.T), in_hbm(gate_codes.T), packed[0])

    def expert(offsets, held, weights):
        rows = offsets * SHARDS * capacity
        half = jax.ShapeDtypeStruct((2 * offsets * tall, width), jnp.bfloat16)
        return pl.pallas_call(
            functools.partial(expert_kernel, capacity, offsets),
            out_shape=[half] * 2,
            in_specs=[vmem] * (offsets * 2 + 3),
            out_specs=[vmem] * 2,
            scratch_shapes=[pltpu.VMEM((QUARTERS, rows, width), jnp.bfloat16)] * 2,
            compiler_params=params,
            cost_estimate=pl.CostEstimate(
                flops=6 * rows * features * w_gate.shape[2],
                bytes_accessed=0,
                transcendentals=0,
            ),
        )(*held, *weights)

    def load(gate):
        return pl.pallas_call(
            load_kernel,
            out_shape=[jax.ShapeDtypeStruct(w.shape, w.dtype) for w in (w_gate, w_up, w_down)],
            in_specs=[hbm] * 4,
            out_specs=[vmem] * 3,
            scratch_shapes=[pltpu.SemaphoreType.DMA((3,))],
            compiler_params=load_params,
        )(in_hbm(w_gate), in_hbm(w_up), in_hbm(w_down), gate)

    def fold(kept, arrived, offsets):
        middle = offsets * tall
        kept, arrived = kept.astype(jnp.float32), arrived.astype(jnp.float32)
        leaving = (kept[middle:] + arrived[middle:]).astype(jnp.bfloat16)
        return leaving, kept[:middle] + arrived[:middle]

    half, late = planes // 2, 3 * planes // 4
    places = {
        "own": range(1),
        "near": range(1, half),
        "mid": range(half, late),
        "far": range(late, planes),
    }
    for group in GROUPS:
        places[group] = [at for member in group.split("+") for at in places[member]]
    results = {}

    def result(step):
        if step not in results:
            results[step] = build(*step.split())
        return results[step]

    def build(kind, name):
        if kind == "pack":
            return [packed[at] for at in places[name]]
        if kind == "z":
            inputs = result("pack " + name)
        elif kind == "y":
            inputs = result(("pack " if name == "own" or name in DIRECT else "z ") + name)
        elif kind == "c":
            own = result(("pack " if name == "own" else "z ") + name)
            inputs = [jnp.concatenate(both, axis=0) for both in zip(own, result("y " + name))]
        elif kind == "expert":
            inputs = []
            for member in name.split("+"):
                own = result(("pack " if member == "own" else "z ") + member)
                both = [jnp.concatenate(two, axis=0) for two in zip(own, result("y " + member))]
                for two in zip(both, result("c " + member)):
                    inputs += two
        elif kind == "rc":
            inputs = result("expert " + name)[1:]
        elif kind == "sum":
            kept, arrived = result("expert " + name)[0], result("rc " + name)[0]
            return fold(kept, arrived, len(places[name]))
        elif kind == "ry":
            leaving, count = result("sum " + name)[0], len(places[name])
            inputs = jnp.split(leaving, count, axis=0) if name in APART else [leaving]
        elif kind == "answer":
            stay, count = result("sum " + name)[1], len(places[name])
            if name not in APART:
                total = stay + result("ry " + name)[0].astype(jnp.float32)
                return jnp.split(total.astype(jnp.bfloat16), count, axis=0)
            pieces = list(zip(jnp.split(stay, count, axis=0), result("ry " + name)))
            return [None] + [
                (one + two.astype(jnp.float32)).astype(jnp.bfloat16) for one, two in pieces[1:]
            ]
        elif kind == "last":
            stay = jnp.split(result("sum " + name)[1], len(places[name]), axis=0)[0]
            return [stay, result("ry " + name)[0]]
        elif kind == "load":
            inputs = packed[:1]
        elif kind == "rz":
            inputs = [a for a, at in zip(result("answer " + name), places[name]) if at]
        earlier = [result(step)[-1] for step in ORDER.get(kind + " " + name, ())]
        if earlier:
            inputs = [after(inputs[0], *earlier)] + list(inputs[1:])
        if kind == "load":
            return load(inputs[0])
        if kind == "expert":
            return expert(len(places[name]), inputs, result("load all"))
        if kind == "y" and name in DIRECT:
            return [partner(array, at * SHARDS + 2) for array, at in zip(inputs, places[name])]
        if kind in ("y", "ry"):
            return [partner(array, 2) for array in inputs]
        if kind in ("c", "rc"):
            if kind + " " + name not in SPLIT:
                return [partner(array, 1) for array in inputs]
            halves = [jnp.split(array, 2, axis=0) for array in inputs]
            if kind == "c":
                own = result(("pack " if name == "own" else "z ") + name)
                halves = [(one, two[1]) for one, two in zip(own, halves)]
            halves = [[partner(half, 1) for half in pair] for pair in halves]
            return [jnp.concatenate(pair, axis=0) for pair in halves]
        where = [at for at in places[name] if at]
        return [partner(array, at * SHARDS) for array, at in zip(inputs, where)]

    returned = {}
    for group in GROUPS:
        pieces = list(result("answer " + group))
        if group != "own":
            pieces[-len(result("rz " + group)) :] = result("rz " + group)
        returned.update(zip(places[group], pieces))
    returned = result("last " + APART[0]) + [returned[at] for at in range(1, planes)]

    return pl.pallas_call(
        functools.partial(mix_kernel, planes),
        out_shape=jax.ShapeDtypeStruct((tok_rows, features), jnp.bfloat16),
        in_specs=[vmem] * (planes + 2),
        out_specs=vmem,
        compiler_params=params,
    )(plan, *returned)


def solution(mesh):
    in_specs = (
        P(("groups", "expert"), None),
        P(("groups", "expert"), None),
        P(("groups", "expert"), None),
        P(("groups", "expert"), None),
        P("expert", None, None),
        P("expert", None, None),
        P("expert", None, None),
    )
    out_specs = P(("groups", "expert"), None)
    return jax.shard_map(shards, mesh=mesh, in_specs=in_specs, out_specs=out_specs, check_vma=False)
```

```python
import functools

import jax
import jax.numpy as jnp
from jax import lax
from jax.experimental import pallas as pl
from jax.experimental.pallas import tpu as pltpu
from jax.sharding import PartitionSpec as P

SHARDS = 4
QUARTERS = 4
GROUPS = ("own+near", "mid", "far")
SPLIT = ("c mid", "c near",)
DIRECT = ()
APART = ("own+near",)
ORDER = {
    "z far": ("y own",),
    "expert own+near": ("y own", "z mid",),
    "expert far": ("rc mid",),
    "rz far": ("rc own+near",),
    "c own": ("c near",),
    "rz mid": ("rc far", "z near",),
    "c far": ("z near", "expert mid",),
    "y far": ("z near",),
    "rz own+near": ("rc mid",),
    "c near": ("expert mid",),
}
VMEM_BYTES = 16 * 1024 * 1024
LOAD_VMEM_BYTES = 40 * 1024 * 1024


def zero_one(condition):
    return jnp.where(condition, 1.0, 0.0).astype(jnp.bfloat16)


def after(array, *others):
    return lax.optimization_barrier((array, *others))[0]


def exact_dot(left, right):
    return jnp.dot(left, right, preferred_element_type=jnp.float32)


def spread(table_ref, pick, plane, rows, shape, axis):
    place = lax.broadcasted_iota(jnp.int32, shape, axis) % rows
    out = jnp.zeros(shape, jnp.int32)
    for row in range(rows):
        out = jnp.where(place == row, table_ref[pick, row] ^ plane, out)
    return out


def pack_kernel(capacity, planes, route_hbm, tok_hbm, scale_hbm, *rest):
    outs = rest[:planes]
    quarters_ref, tok_ref, scale_ref, route_ref, sems = rest[planes:]
    sources, targets = (route_hbm, scale_hbm, tok_hbm), (route_ref, scale_ref, tok_ref)
    copies = [
        pltpu.make_async_copy(source, target, sems.at[index])
        for index, (source, target) in enumerate(zip(sources, targets))
    ]
    for copy in copies:
        copy.start()
    rows, features = tok_ref.shape
    picks, width = route_ref.shape[0], features // QUARTERS
    copies[0].wait()
    plane = lax.axis_index("expert") // SHARDS
    columns = QUARTERS * rows
    numbers = lax.broadcasted_iota(jnp.int32, (planes, columns), 0)
    named = jnp.zeros((planes, columns), jnp.float32)
    for pick in range(picks):
        turned = spread(route_ref, pick, plane, rows, (1, columns), 1)
        named = named + jnp.where(turned == numbers, 1.0, 0.0)
    first = lax.broadcasted_iota(jnp.int32, (columns, columns), 0)
    second = lax.broadcasted_iota(jnp.int32, (columns, columns), 1)
    before = zero_one((first // rows == second // rows) & (first < second))
    position = exact_dot(named.astype(jnp.bfloat16), before)
    tall = QUARTERS * capacity
    slot_row = lax.broadcasted_iota(jnp.int32, (tall, columns), 0)
    slot_col = lax.broadcasted_iota(jnp.int32, (tall, columns), 1)
    same_quarter = slot_row // capacity == slot_col // rows
    slot = (slot_row % capacity).astype(jnp.float32)
    pick_out = [
        zero_one(
            same_quarter
            & (named[offset : offset + 1, :] > 0.5)
            & (position[offset : offset + 1, :] == slot)
        )
        for offset in range(planes)
    ]
    copies[1].wait()
    copies[2].wait()
    for block in range(features // 128):
        quarter, at = divmod(block * 128, width)
        codes = tok_ref[:, block * 128 : (block + 1) * 128].astype(jnp.float32)
        factors = scale_ref[:, block : block + 1]
        quarters_ref[quarter * rows : (quarter + 1) * rows, at : at + 128] = (
            codes * factors
        ).astype(jnp.bfloat16)
    moved = exact_dot(jnp.concatenate(pick_out, axis=0), quarters_ref[...])
    for offset in range(planes):
        outs[offset][...] = moved[offset * tall : (offset + 1) * tall, :].astype(jnp.bfloat16)


def order_matrix(capacity, turned):
    size = SHARDS * QUARTERS * capacity
    row = lax.broadcasted_iota(jnp.int32, (size, size), 1 if turned else 0)
    col = lax.broadcasted_iota(jnp.int32, (size, size), 0 if turned else 1)
    quarter, block, slot = row // (SHARDS * capacity), (row // capacity) % SHARDS, row % capacity
    return zero_one(col == (block * QUARTERS + quarter) * capacity + slot)


def load_kernel(gate_hbm, up_hbm, down_hbm, unused, gate_ref, up_ref, down_ref, sems):
    copies = [
        pltpu.make_async_copy(source, target, sems.at[index])
        for index, (source, target) in enumerate(
            ((gate_hbm, gate_ref), (up_hbm, up_ref), (down_hbm, down_ref))
        )
    ]
    for copy in copies:
        copy.start()
    for copy in copies:
        copy.wait()


def expert_kernel(capacity, offsets, *refs):
    count = 2 * offsets
    blocks = refs[:count]
    gate_ref, up_ref, down_ref, kept_ref, sent_ref, rows_ref, part_ref = refs[count:]
    group, tall = SHARDS * capacity, QUARTERS * capacity
    width = blocks[0].shape[1]
    spans = [slice(quarter * width, (quarter + 1) * width) for quarter in range(QUARTERS)]
    order = order_matrix(capacity, False)
    for offset in range(offsets):
        held = jnp.concatenate(
            [blocks[2 * offset][...], blocks[2 * offset + 1][...]], axis=0
        )
        sorted_rows = exact_dot(order, held).astype(jnp.bfloat16)
        for quarter in range(QUARTERS):
            rows_ref[quarter, offset * group : (offset + 1) * group, :] = sorted_rows[
                quarter * group : (quarter + 1) * group, :
            ]
    gate = jnp.zeros((offsets * group, gate_ref.shape[2]), jnp.float32)
    upward = jnp.zeros((offsets * group, gate_ref.shape[2]), jnp.float32)
    for quarter, span in enumerate(spans):
        gate = gate + exact_dot(rows_ref[quarter], gate_ref[0, span, :])
        upward = upward + exact_dot(rows_ref[quarter], up_ref[0, span, :])
    hidden = (gate / (1.0 + jnp.exp(-gate)) * upward).astype(jnp.bfloat16)
    for quarter, span in enumerate(spans):
        part_ref[quarter] = exact_dot(hidden, down_ref[0, :, span]).astype(jnp.bfloat16)
    back = order_matrix(capacity, True)
    for offset in range(offsets):
        held = jnp.concatenate(
            [
                part_ref[quarter, offset * group : (offset + 1) * group, :]
                for quarter in range(QUARTERS)
            ],
            axis=0,
        )
        answer = exact_dot(back, held).astype(jnp.bfloat16)
        for member in range(SHARDS):
            out_ref = sent_ref if member >= 2 else kept_ref
            at = (member % 2 * offsets + offset) * tall
            out_ref[at : at + tall, :] = answer[member * tall : (member + 1) * tall, :]


def plan_kernel(capacity, planes, rows, route_hbm, code_hbm, unused, plan_ref, *scratch):
    route_ref, code_ref, sems = scratch
    copies = [
        pltpu.make_async_copy(route_hbm, route_ref, sems.at[0]),
        pltpu.make_async_copy(code_hbm, code_ref, sems.at[1]),
    ]
    for copy in copies:
        copy.start()
    for copy in copies:
        copy.wait()
    picks = route_ref.shape[0]
    tall = QUARTERS * rows
    plane = lax.axis_index("expert") // SHARDS
    numbers = lax.broadcasted_iota(jnp.int32, (tall, planes), 1)
    named = jnp.zeros((tall, planes), jnp.float32)
    coarse = jnp.zeros((tall, planes), jnp.float32)
    fine = jnp.zeros((tall, planes), jnp.float32)
    for pick in range(picks):
        here = spread(route_ref, pick, plane, rows, (tall, 1), 0) == numbers
        codes = spread(code_ref, pick, 0, rows, (tall, 1), 0)
        named = named + jnp.where(here, 1.0, 0.0)
        coarse = coarse + jnp.where(here, (codes // 256).astype(jnp.float32) / 256.0, 0.0)
        fine = fine + jnp.where(here, (codes % 256).astype(jnp.float32) / 65536.0, 0.0)
    first = lax.broadcasted_iota(jnp.int32, (tall, tall), 0)
    second = lax.broadcasted_iota(jnp.int32, (tall, tall), 1)
    before = zero_one((first // rows == second // rows) & (second < first))
    position = exact_dot(before, named.astype(jnp.bfloat16))
    slot_row = lax.broadcasted_iota(jnp.int32, (tall, QUARTERS * capacity), 0)
    slot_col = lax.broadcasted_iota(jnp.int32, (tall, QUARTERS * capacity), 1)
    same_quarter = slot_row // rows == slot_col // capacity
    slot = (slot_col % capacity).astype(jnp.float32)
    for offset in range(planes):
        column = slice(offset, offset + 1)
        take = same_quarter & (named[:, column] > 0.5) & (position[:, column] == slot)
        for half, factor in enumerate((coarse, fine)):
            plan_ref[offset, half * tall : (half + 1) * tall, :] = jnp.where(
                take, factor[:, column], 0.0
            ).astype(jnp.bfloat16)


def mix_kernel(planes, plan_ref, *refs):
    stay_ref, across_ref, *others, out_ref = refs
    own = (stay_ref[...] + across_ref[...].astype(jnp.float32)).astype(jnp.bfloat16)
    rows, features = out_ref.shape
    width, tall = features // QUARTERS, QUARTERS * rows
    total = jnp.zeros((2 * tall, width), jnp.float32)
    for at in range(0, planes, 4):
        some = range(at, min(at + 4, planes))
        plan = jnp.concatenate([plan_ref[offset] for offset in some], axis=1)
        answers = [others[offset - 1][...] if offset else own for offset in some]
        answers = jnp.concatenate(answers, axis=0)
        total = total + exact_dot(plan, answers)
    total = (total[:tall] + total[tall:]).astype(jnp.bfloat16)
    for quarter in range(QUARTERS):
        out_ref[:, quarter * width : (quarter + 1) * width] = total[
            quarter * rows : (quarter + 1) * rows, :
        ]


def shards(tokens, scales, routes, gate_codes, w_gate, w_up, w_down):
    tok_rows, features = tokens.shape
    picks_per = routes.shape[1]
    devices = lax.axis_size("expert")
    planes = devices // SHARDS
    capacity = 3 * tok_rows * picks_per // (2 * planes)
    width = features // QUARTERS
    tall = QUARTERS * capacity
    vmem = pl.BlockSpec(memory_space=pltpu.VMEM)
    hbm = pl.BlockSpec(memory_space=pl.ANY)
    params = pltpu.CompilerParams(vmem_limit_bytes=VMEM_BYTES)
    load_params = pltpu.CompilerParams(vmem_limit_bytes=LOAD_VMEM_BYTES)

    def in_hbm(array):
        return pltpu.with_memory_space_constraint(array, pltpu.HBM)

    def partner(array, distance):
        return lax.ppermute(array, "expert", [(i, i ^ distance) for i in range(devices)])

    block = jax.ShapeDtypeStruct((tall, width), jnp.bfloat16)
    packed = pl.pallas_call(
        functools.partial(pack_kernel, capacity, planes),
        out_shape=[block] * planes,
        in_specs=[hbm] * 3,
        out_specs=[vmem] * planes,
        scratch_shapes=[
            pltpu.VMEM((QUARTERS * tok_rows, width), jnp.bfloat16),
            pltpu.VMEM(tokens.shape, tokens.dtype),
            pltpu.VMEM(scales.shape, scales.dtype),
            pltpu.SMEM(routes.T.shape, routes.dtype),
            pltpu.SemaphoreType.DMA((3,)),
        ],
        compiler_params=params,
    )(in_hbm(routes.T), in_hbm(tokens), in_hbm(scales))
    plan = pl.pallas_call(
        functools.partial(plan_kernel, capacity, planes, tok_rows),
        out_shape=jax.ShapeDtypeStruct((planes, 2 * QUARTERS * tok_rows, tall), jnp.bfloat16),
        in_specs=[hbm] * 3,
        out_specs=vmem,
        scratch_shapes=[pltpu.SMEM(routes.T.shape, routes.dtype)] * 2
        + [pltpu.SemaphoreType.DMA((2,))],
        compiler_params=params,
    )(in_hbm(routes.T), in_hbm(gate_codes.T), packed[0])

    def expert(offsets, held, weights):
        rows = offsets * SHARDS * capacity
        half = jax.ShapeDtypeStruct((2 * offsets * tall, width), jnp.bfloat16)
        return pl.pallas_call(
            functools.partial(expert_kernel, capacity, offsets),
            out_shape=[half] * 2,
            in_specs=[vmem] * (offsets * 2 + 3),
            out_specs=[vmem] * 2,
            scratch_shapes=[pltpu.VMEM((QUARTERS, rows, width), jnp.bfloat16)] * 2,
            compiler_params=params,
            cost_estimate=pl.CostEstimate(
                flops=6 * rows * features * w_gate.shape[2],
                bytes_accessed=0,
                transcendentals=0,
            ),
        )(*held, *weights)

    def load(gate):
        return pl.pallas_call(
            load_kernel,
            out_shape=[jax.ShapeDtypeStruct(w.shape, w.dtype) for w in (w_gate, w_up, w_down)],
            in_specs=[hbm] * 4,
            out_specs=[vmem] * 3,
            scratch_shapes=[pltpu.SemaphoreType.DMA((3,))],
            compiler_params=load_params,
        )(in_hbm(w_gate), in_hbm(w_up), in_hbm(w_down), gate)

    def fold(kept, arrived, offsets):
        middle = offsets * tall
        kept, arrived = kept.astype(jnp.float32), arrived.astype(jnp.float32)
        leaving = (kept[middle:] + arrived[middle:]).astype(jnp.bfloat16)
        return leaving, kept[:middle] + arrived[:middle]

    half, late = planes // 2, 3 * planes // 4
    places = {
        "own": range(1),
        "near": range(1, half),
        "mid": range(half, late),
        "far": range(late, planes),
    }
    for group in GROUPS:
        places[group] = [at for member in group.split("+") for at in places[member]]
    results = {}

    def result(step):
        if step not in results:
            results[step] = build(*step.split())
        return results[step]

    def build(kind, name):
        if kind == "pack":
            return [packed[at] for at in places[name]]
        if kind == "z":
            inputs = result("pack " + name)
        elif kind == "y":
            inputs = result(("pack " if name == "own" or name in DIRECT else "z ") + name)
        elif kind == "c":
            own = result(("pack " if name == "own" else "z ") + name)
            inputs = [jnp.concatenate(both, axis=0) for both in zip(own, result("y " + name))]
        elif kind == "expert":
            inputs = []
            for member in name.split("+"):
                own = result(("pack " if member == "own" else "z ") + member)
                both = [jnp.concatenate(two, axis=0) for two in zip(own, result("y " + member))]
                for two in zip(both, result("c " + member)):
                    inputs += two
        elif kind == "rc":
            inputs = result("expert " + name)[1:]
        elif kind == "sum":
            kept, arrived = result("expert " + name)[0], result("rc " + name)[0]
            return fold(kept, arrived, len(places[name]))
        elif kind == "ry":
            leaving, count = result("sum " + name)[0], len(places[name])
            inputs = jnp.split(leaving, count, axis=0) if name in APART else [leaving]
        elif kind == "answer":
            stay, count = result("sum " + name)[1], len(places[name])
            if name not in APART:
                total = stay + result("ry " + name)[0].astype(jnp.float32)
                return jnp.split(total.astype(jnp.bfloat16), count, axis=0)
            pieces = list(zip(jnp.split(stay, count, axis=0), result("ry " + name)))
            return [None] + [
                (one + two.astype(jnp.float32)).astype(jnp.bfloat16) for one, two in pieces[1:]
            ]
        elif kind == "last":
            stay = jnp.split(result("sum " + name)[1], len(places[name]), axis=0)[0]
            return [stay, result("ry " + name)[0]]
        elif kind == "load":
            inputs = packed[:1]
        elif kind == "rz":
            inputs = [a for a, at in zip(result("answer " + name), places[name]) if at]
        earlier = [result(step)[-1] for step in ORDER.get(kind + " " + name, ())]
        if earlier:
            inputs = [after(inputs[0], *earlier)] + list(inputs[1:])
        if kind == "load":
            return load(inputs[0])
        if kind == "expert":
            return expert(len(places[name]), inputs, result("load all"))
        if kind == "y" and name in DIRECT:
            return [partner(array, at * SHARDS + 2) for array, at in zip(inputs, places[name])]
        if kind in ("y", "ry"):
            return [partner(array, 2) for array in inputs]
        if kind in ("c", "rc"):
            if kind + " " + name not in SPLIT:
                return [partner(array, 1) for array in inputs]
            halves = [jnp.split(array, 2, axis=0) for array in inputs]
            if kind == "c":
                own = result(("pack " if name == "own" else "z ") + name)
                halves = [(one, two[1]) for one, two in zip(own, halves)]
            halves = [[partner(half, 1) for half in pair] for pair in halves]
            return [jnp.concatenate(pair, axis=0) for pair in halves]
        where = [at for at in places[name] if at]
        return [partner(array, at * SHARDS) for array, at in zip(inputs, where)]

    returned = {}
    for group in GROUPS:
        pieces = list(result("answer " + group))
        if group != "own":
            pieces[-len(result("rz " + group)) :] = result("rz " + group)
        returned.update(zip(places[group], pieces))
    returned = result("last " + APART[0]) + [returned[at] for at in range(1, planes)]

    return pl.pallas_call(
        functools.partial(mix_kernel, planes),
        out_shape=jax.ShapeDtypeStruct((tok_rows, features), jnp.bfloat16),
        in_specs=[vmem] * (planes + 2),
        out_specs=vmem,
        compiler_params=params,
    )(plan, *returned)


def solution(mesh):
    in_specs = (
        P(("groups", "expert"), None),
        P(("groups", "expert"), None),
        P(("groups", "expert"), None),
        P(("groups", "expert"), None),
        P("expert", None, None),
        P("expert", None, None),
        P("expert", None, None),
    )
    out_specs = P(("groups", "expert"), None)
    return jax.shard_map(shards, mesh=mesh, in_specs=in_specs, out_specs=out_specs, check_vma=False)
```
